32 devices in a mesh: dp: 8 (over y, x, core), tensor: 4 (over z).
Axes of the slice: x: 2, y: 2, z: 4, core: 2. Of those that a mesh axis runs over, the one named last changes fastest.
Arguments:
- tokens: bfloat16 [16384, 1536], P('dp'), may hold values from -6 to 6
- norm_gain: float32 [1536], replicated, may hold values from 0.5 to 1.5
- gate_weight: bfloat16 [1536, 3072], P(None, 'tensor'), may hold values from -0.15625 to 0.15625
- value_weight: bfloat16 [1536, 3072], P(None, 'tensor'), may hold values from -0.15625 to 0.15625
- state_weight: bfloat16 [1536, 256], replicated, may hold values from -0.15625 to 0.15625
- step_weight: bfloat16 [1536, 48], P(None, 'tensor'), may hold values from -0.15625 to 0.15625
- value_kernel: float32 [4, 3072], P(None, 'tensor'), may hold values from -3 to 3
- value_bias: float32 [3072], P('tensor'), may hold values from -2 to 2
- state_kernel: float32 [4, 256], replicated, may hold values from -3 to 3
- state_bias: float32 [256], replicated, may hold values from -2 to 2
- step_bias: float32 [48], P('tensor'), may hold values from -5 to -1
- decay_log: float32 [48], P('tensor'), may hold values from 0 to 2.7
- skip_scale: float32 [48], P('tensor'), may hold values from 0.5 to 1.5
- gated_gain: float32 [3072], P('tensor'), may hold values from 0.5 to 1.5
- out_weight: bfloat16 [3072, 1536], P('tensor'), may hold values from -0.109375 to 0.109375
- segment_ids: int32 [8, 2048], P('dp'), may hold values from 0 to 3, never falling along the last dimension, each value on 1 to 1024 neighbouring positions
- out_cotangent: bfloat16 [16384, 1536], P('dp'), may hold values from -6 to 6
Outputs:
- block_out: bfloat16 [16384, 1536], P('dp')
- tokens_grad: float32 [16384, 1536], P(('dp', 'tensor'))
- norm_gain_grad: float32 [1536], replicated
- gate_weight_grad: float32 [1536, 3072], P(None, 'tensor')
- value_weight_grad: float32 [1536, 3072], P(None, 'tensor')
- state_weight_grad: float32 [1536, 256], replicated
- step_weight_grad: float32 [1536, 48], P(None, 'tensor')
- value_kernel_grad: float32 [4, 3072], P(None, 'tensor')
- value_bias_grad: float32 [3072], P('tensor')
- state_kernel_grad: float32 [4, 256], replicated
- state_bias_grad: float32 [256], replicated
- step_bias_grad: float32 [48], P('tensor')
- decay_log_grad: float32 [48], P('tensor')
- skip_scale_grad: float32 [48], P('tensor')
- gated_gain_grad: float32 [3072], P('tensor')
- out_weight_grad: float32 [3072, 1536], P('tensor')
The draws below stay inside these ranges and needn't reach their ends.
Inputs may be any that keep to these rules, and one draw needn't show every extreme that they name: `segment_ids`: segment numbers never fall along a sequence; each sequence holds 4 documents, each of 1 to 1024 tokens, one of exactly 1024.
All inputs are finite; a program needn't handle non-finite values.
Results may differ from the reference program's by a relative error of at most 0.0088.
Values sent between devices are 32-bit elements; how exact they have to be, the bound alone decides.
No kernel may reach another device: no remote copies, remote signals or barrier semaphores. Data moves between devices by JAX's collectives and lax.ppermute only.
A program may use at most 256 MiB of HBM per device.

```python
import math
import jax
import jax.numpy as jnp
import numpy as np
from jax import lax

D = 1536
HEADS = 48
STATE = 128
CONV = 4
GROUP = 256
SEQ_LEN = 2048
INNER = 3072
SEQS = 8
TOKENS = 16384


def level_of(rng, dims, shards, smallest, high):
    level, own = 1.0, jax.random.fold_in(rng, 6)
    for dim, parts in shards:
        heights = jnp.exp(jax.random.uniform(jax.random.fold_in(own, dim), (parts,), jnp.float32, smallest / len(shards), high / len(shards)))
        level = level * jnp.repeat(heights, dims[dim] // parts).reshape([-1 if axis == dim else 1 for axis in range(len(dims))])
    return level


def split_up(number_of, total, limit, slope):
    loads = [(1 << 20) // math.isqrt(rank ** slope) + 1 for rank in range(2, number_of + 1)]
    surplus, given = total - limit - (number_of - 1), [1] * (number_of - 1)
    while surplus > 0:
        free = [i for i in range(number_of - 1) if given[i] < limit]
        mass, budget = sum([loads[i] for i in free]), surplus
        for i in free:
            more = min(limit - given[i], max(1, budget * loads[i] // mass), surplus)
            given[i] = given[i] + more
            surplus = surplus - more
    return np.array([limit] + given)


def uneven(key, count, total, reach, slope):
    if count == 2:
        one = jax.random.randint(key, (), max(1, total - reach), min(reach, total - 1) + 1)
        return jnp.stack([one, total - one])
    tallies = jnp.asarray(split_up(count, total, reach, slope), jnp.int32)
    couples = (count - 1) // 2
    donor, receiver = tallies[1:1 + 2 * couples:2], tallies[2:2 + 2 * couples:2]
    slack = jnp.minimum(donor - 1, reach - receiver)
    passed = jax.random.randint(jax.random.fold_in(key, 1), (couples,), 0, 1 << 20) % (slack + 1)
    tallies = tallies.at[1:1 + 2 * couples:2].set(donor - passed).at[2:2 + 2 * couples:2].set(receiver + passed)
    return tallies[jax.random.permutation(jax.random.fold_in(key, 2), count)]


def centred(own_key, dims, scale, bound, split=(), held_as=jnp.bfloat16):
    drawn = jax.random.normal(own_key, dims, jnp.float32) * scale
    if len(split) > 0:
        drawn = level_of(own_key, dims, split, -0.22, 0.18) * drawn
    return jnp.clip(drawn, min=-bound, max=bound).astype(held_as)


def setup_inputs(seed: int = 0) -> dict:
    streams_of = jax.random.split(jax.random.key(seed), 18)
    return {
        "tokens": centred(streams_of[0], (TOKENS, D), 1.0, 6.0, ((0, 8),)),
        "norm_gain": jnp.clip(1.0 + 0.1 * jax.random.normal(streams_of[1], (D,), jnp.float32), 0.5, 1.5),
        "gate_weight": centred(streams_of[2], (D, INNER), D ** -0.5, 0.15625, ((1, 4),)),
        "value_weight": centred(streams_of[3], (D, INNER), D ** -0.5, 0.15625, ((1, 4),)),
        "state_weight": centred(streams_of[4], (D, 2 * STATE), D ** -0.5, 0.15625),
        "step_weight": centred(streams_of[5], (D, HEADS), D ** -0.5, 0.15625, ((1, 4),)),
        "value_kernel": centred(streams_of[6], (CONV, INNER), 0.5, 3.0, ((1, 4),), jnp.float32),
        "value_bias": centred(streams_of[7], (INNER,), 0.3, 2.0, ((0, 4),), jnp.float32),
        "state_kernel": centred(streams_of[8], (CONV, 2 * STATE), 0.5, 3.0, (), jnp.float32),
        "state_bias": centred(streams_of[9], (2 * STATE,), 0.3, 2.0, (), jnp.float32),
        "step_bias": jnp.clip(-5.0 + 4.0 * jax.random.uniform(streams_of[10], (HEADS,), jnp.float32) ** level_of(streams_of[10], (HEADS,), ((0, 4),), -0.2, 0.2), -5.0, -1.0),
        "decay_log": jnp.clip(2.7 * jax.random.uniform(streams_of[11], (HEADS,), jnp.float32) ** level_of(streams_of[11], (HEADS,), ((0, 4),), -0.2, 0.2), 0.0, 2.7),
        "skip_scale": jnp.clip(0.5 + 1.0 * jax.random.uniform(streams_of[12], (HEADS,), jnp.float32) ** level_of(streams_of[12], (HEADS,), ((0, 4),), -0.2, 0.2), 0.5, 1.5),
        "gated_gain": jnp.clip(1.0 + 0.1 * jax.random.normal(streams_of[13], (INNER,), jnp.float32), 0.5, 1.5),
        "out_weight": centred(streams_of[14], (INNER, D), INNER ** -0.5, 0.109375, ((0, 4),)),
        "segment_ids": jax.vmap(lambda own: jnp.searchsorted(jnp.cumsum(uneven(own, 4, SEQ_LEN, SEQ_LEN // 2, 0)), jnp.arange(SEQ_LEN), side="right"))(jax.random.split(streams_of[15], SEQS)).reshape((SEQS, SEQ_LEN)).astype(jnp.int32),
        "out_cotangent": centred(streams_of[16], (TOKENS, D), 1.0, 6.0, ((0, 8),)),
    }


EPS = 1e-05
precise = lax.Precision.HIGHEST

@jax.custom_vjp
def low(v):
    return lax.optimization_barrier(v.astype(jnp.bfloat16)).astype(jnp.float32)

@jax.custom_vjp
def low_back(v):
    return v

def low_keep(v):
    return (low(v), None)

def low_pass(kept, grad):
    return (grad,)

def back_keep(v):
    return (v, None)

def back_low(kept, grad):
    return (low(grad),)
low.defvjp(low_keep, low_pass)
low_back.defvjp(back_keep, back_low)

def conv_silu(raw_input, kernel, offset_bias, segments):
    width = kernel.shape[0]
    length = raw_input.shape[0]
    padded = jnp.concatenate([jnp.zeros((width - 1, raw_input.shape[1]), raw_input.dtype), raw_input], axis=0)
    padded_ids = jnp.concatenate([jnp.full((width - 1,), -1, jnp.int32), segments.astype(jnp.int32)], axis=0)
    total = jnp.zeros_like(raw_input) + offset_bias
    for place in range(width):
        matches = (padded_ids[place:place + length] == segments).astype(raw_input.dtype)
        total = total + padded[place:place + length] * kernel[place] * matches[:, None]
    return jax.nn.silu(total)

def scan_block(state, pieces):
    values, b_part, c_part, log_decay, steps, block_ids, previous = pieces
    size = values.shape[0]
    local = jnp.cumsum(log_decay, axis=0).T
    later = lax.broadcasted_iota(jnp.int32, (size, size), 0)
    earlier = lax.broadcasted_iota(jnp.int32, (size, size), 1)
    allowed = jnp.logical_and(later >= earlier, block_ids[:, None] == block_ids[None, :])
    mask = allowed.astype(values.dtype)
    spread = local[:, :, None] - local[:, None, :]
    decay = jnp.exp(jnp.where(allowed[None], spread, 0.0)) * mask[None]
    scores = jnp.dot(c_part, b_part.T, precision=precise)
    weights = scores[None] * decay * steps.T[:, None, :]
    inner = jnp.einsum('hts,shp->thp', weights, values, precision=precise)
    carried = (block_ids == previous).astype(values.dtype)
    outer = jnp.einsum('tn,hpn->thp', c_part, state, precision=precise)
    outer = outer * (jnp.exp(local).T * carried[:, None])[:, :, None]
    tail_same = (block_ids == block_ids[-1]).astype(values.dtype)
    tail = jnp.exp(local[:, -1:] - local).T * steps * tail_same[:, None]
    keep_state = (block_ids[-1] == previous).astype(values.dtype)
    fresh = jnp.einsum('shp,sn->hpn', values * tail[:, :, None], b_part, precision=precise)
    new_state = state * (jnp.exp(local[:, -1]) * keep_state)[:, None, None] + fresh
    return (new_state, inner + outer)

def mixer(gate, value_raw, state_mixed, step_raw, value_kernel, value_bias, step_bias, decay_log, skip_scale, segments):
    length = value_raw.shape[0]
    heads = step_bias.shape[0]
    head_size = value_raw.shape[1] // heads
    states = state_mixed.shape[1] // 2
    values = conv_silu(value_raw, value_kernel, value_bias, segments)
    steps = jax.nn.softplus(step_raw + step_bias)
    log_decay = -steps * jnp.exp(decay_log)
    blocks = length // GROUP
    previous = jnp.concatenate([jnp.full((1,), -1, jnp.int32), segments[GROUP - 1:length - 1:GROUP].astype(jnp.int32)], axis=0)
    pieces = (values.reshape(blocks, GROUP, heads, head_size), state_mixed[:, :states].reshape(blocks, GROUP, states), state_mixed[:, states:].reshape(blocks, GROUP, states), log_decay.reshape(blocks, GROUP, heads), steps.reshape(blocks, GROUP, heads), segments.astype(jnp.int32).reshape(blocks, GROUP), previous)
    start = jnp.zeros((heads, head_size, states), values.dtype)
    _, outputs = lax.scan(jax.checkpoint(scan_block), start, pieces)
    mixed = outputs.reshape(length, heads, head_size) + skip_scale[None, :, None] * values.reshape(length, heads, head_size)
    return mixed.reshape(length, heads * head_size) * jax.nn.silu(gate)

def forward(tokens, norm_gain, gate_weight, value_weight, state_weight, step_weight, value_kernel, value_bias, state_kernel, state_bias, step_bias, decay_log, skip_scale, gated_gain, out_weight, segment_ids):
    scale = lax.rsqrt(lax.optimization_barrier(jnp.mean(tokens * tokens, axis=-1, keepdims=True)) + EPS)
    normed = low(tokens * scale * norm_gain)
    gate = low_back(jnp.dot(normed, gate_weight, precision=precise))
    value_raw = low_back(jnp.dot(normed, value_weight, precision=precise))
    state_raw = jnp.dot(normed, state_weight, precision=precise)
    step_raw = low_back(jnp.dot(normed, step_weight, precision=precise))
    sequences = segment_ids.shape[0]

    def one_sequence(pieces):
        gate_seq, value_seq, state_seq, step_seq, doc_ids = pieces
        state_mixed = conv_silu(state_seq, state_kernel, state_bias, doc_ids)
        return mixer(gate_seq, value_seq, state_mixed, step_seq, value_kernel, value_bias, step_bias, decay_log, skip_scale, doc_ids)
    gated = lax.map(one_sequence, (gate.reshape(sequences, SEQ_LEN, INNER), value_raw.reshape(sequences, SEQ_LEN, INNER), state_raw.reshape(sequences, SEQ_LEN, 2 * STATE), step_raw.reshape(sequences, SEQ_LEN, HEADS), segment_ids))
    gated = gated.reshape(sequences * SEQ_LEN, INNER)
    strength = lax.rsqrt(lax.optimization_barrier(jnp.mean(gated * gated, axis=-1, keepdims=True)) + EPS)
    mixed_out = low(gated * strength * gated_gain)
    return tokens + jnp.dot(mixed_out, out_weight, precision=precise)

def reference(tokens, norm_gain, gate_weight, value_weight, state_weight, step_weight, value_kernel, value_bias, state_kernel, state_bias, step_bias, decay_log, skip_scale, gated_gain, out_weight, segment_ids, out_cotangent):
    floats = [argument.astype(jnp.float32) for argument in (tokens, norm_gain, gate_weight, value_weight, state_weight, step_weight, value_kernel, value_bias, state_kernel, state_bias, step_bias, decay_log, skip_scale, gated_gain, out_weight)]

    def wrapped(*params):
        return forward(*params, segment_ids)
    result, pullback = jax.vjp(wrapped, *floats)
    gradients = pullback(out_cotangent.astype(jnp.float32))
    return (result.astype(jnp.bfloat16), gradients[0], gradients[1], gradients[2], gradients[3], gradients[4], gradients[5], gradients[6], gradients[7], gradients[8], gradients[9], gradients[10], gradients[11], gradients[12], gradients[13], gradients[14])
```

```python
import functools

import jax
import jax.numpy as jnp
import numpy as np
from jax import lax
from jax.experimental import pallas as pl
from jax.experimental.pallas import tpu as pltpu
from jax.sharding import PartitionSpec as P

D = 1536
INNER = 3072
EPS = 1e-05
BLOCK = 128
LANES = 128
FAR = -1e30
F32 = jnp.float32
BF16 = jnp.bfloat16
CHUNK = 256
STEP = 128
ROWS = 32
VMEM_LIMIT = 63 * 2**20
SMALL_COST = pl.CostEstimate(flops=1, bytes_accessed=1, transcendentals=0)
PIECES = (1, 1, 1, 1)
SHARE_CHUNK = 3


def matmul(left, right, dims=(1, 0)):
    return lax.dot_general(
        left, right, (((dims[0],), (dims[1],)), ((), ())), preferred_element_type=F32
    )


def exact(left, right):
    return lax.dot_general(
        left,
        right,
        (((1,), (0,)), ((), ())),
        precision=lax.Precision.HIGHEST,
        preferred_element_type=F32,
    )


def sigmoid(v):
    return 0.5 * jnp.tanh(0.5 * v) + 0.5


def softplus(v):
    return jnp.maximum(v, 0.0) + jnp.log1p(jnp.exp(-jnp.abs(v)))


def fold(x):
    return x.reshape(x.shape[0] // 8, 8, x.shape[1]).sum(axis=0)


def triangle(lower):
    row = lax.broadcasted_iota(jnp.int32, (BLOCK, BLOCK), 0)
    col = lax.broadcasted_iota(jnp.int32, (BLOCK, BLOCK), 1)
    return jnp.where(row >= col if lower else row <= col, 1.0, 0.0).astype(F32)


def group_sum(x, spread):
    high = x.astype(BF16)
    low = (x - high.astype(F32)).astype(BF16)
    return matmul(high, spread) + matmul(low, spread)


def upright(rows):
    fill = jnp.zeros((BLOCK - rows.shape[0], BLOCK), F32)
    return jnp.concatenate([rows, fill], axis=0).T


def segment_columns(seg_ref, block, blocks, ahead):
    part = lambda k: seg_ref[:, pl.ds(pl.multiple_of(k * BLOCK, BLOCK), BLOCK)].astype(F32)
    ids = part(block)
    before = jnp.where(block > 0, part(jnp.maximum(block - 1, 0)), -1.0)
    lane = lax.broadcasted_iota(jnp.int32, (1, BLOCK), 1)
    rows = [ids]
    if ahead:
        behind = jnp.where(block < blocks - 1, part(jnp.minimum(block + 1, blocks - 1)), -1.0)
    for far in range(1, 4):
        if ahead:
            moved = jnp.where(
                lane >= BLOCK - far,
                pltpu.roll(behind, BLOCK - far, 1),
                pltpu.roll(ids, BLOCK - far, 1),
            )
        else:
            moved = jnp.where(lane < far, pltpu.roll(before, far, 1), pltpu.roll(ids, far, 1))
        rows.append(jnp.where(moved == ids, 1.0, 0.0))
    rows.append(jnp.where(ids == before[:, BLOCK - 1 :], 1.0, 0.0))
    rows.append(jnp.where(ids == ids[:, BLOCK - 1 :], 1.0, 0.0))
    rows.append(jnp.zeros((2, BLOCK), F32))
    return upright(jnp.concatenate(rows, axis=0)), ids


def decay_terms(step_raw, step_bias, rate, cols, seg_row):
    steps = softplus(step_raw + step_bias)
    rates = -steps * rate
    local = exact(triangle(True), rates)
    last = local[BLOCK - 1 :]
    into = jnp.exp(jnp.where(cols[:, 4:5] > 0.5, local, FAR))
    out = jnp.exp(jnp.where(cols[:, 5:6] > 0.5, last - local, FAR))
    row = lax.broadcasted_iota(jnp.int32, (BLOCK, BLOCK), 0)
    col = lax.broadcasted_iota(jnp.int32, (BLOCK, BLOCK), 1)
    allowed = jnp.logical_and(row >= col, cols[:, 0:1] == seg_row)
    bias = jnp.where(allowed, 0.0, FAR)
    return steps, rates, local, local.T, into, out, bias


def pairwise(x, pair, half):
    return jnp.where(half, x[:, 2 * pair : 2 * pair + 1], x[:, 2 * pair + 1 : 2 * pair + 2])


def split_pair(x, half):
    zero = jnp.zeros_like(x)
    return jnp.concatenate([jnp.where(half, x, zero), jnp.where(half, zero, x)], axis=0)


def decay_of(local, local_t, bias, head):
    return jnp.exp(local[:, head : head + 1] - local_t[head : head + 1, :] + bias)


def sum_over_places(place, own, others):
    parts = len(others) + 1
    total = None
    for k in range(parts):
        value = own
        for turn in range(1, parts):
            value = jnp.where((place - k + parts) % parts == turn, others[turn - 1], value)
        total = value if total is None else total + value
    return total


GAIN_ROW, KERNEL_ROW, BIAS_ROW, GATED_ROW, SKIP_ROW = 0, 2, 6, 7, 8
STATE_KERNEL_ROW, STATE_BIAS_ROW, STEP_ROW, DECAY_ROW = 9, 13, 14, 15


def run_pack(*arrays):
    channels = arrays[1].shape[1]

    def kernel(*refs):
        (norm_gain, kernel, bias, gated, skip, state_kernel, state_bias, step_bias, decay, step_w) = refs[
            :10
        ]
        table, wide = refs[10:]
        table[...] = jnp.zeros_like(table)
        table[GAIN_ROW : GAIN_ROW + 1, :] = norm_gain[:channels].reshape(1, channels)
        table[GAIN_ROW + 1 : GAIN_ROW + 2, :] = norm_gain[channels:].reshape(1, channels)
        table[KERNEL_ROW : KERNEL_ROW + 4, :] = kernel[...]
        table[STATE_KERNEL_ROW : STATE_KERNEL_ROW + 4, : state_kernel.shape[1]] = state_kernel[...]
        rows = ((BIAS_ROW, bias), (GATED_ROW, gated), (SKIP_ROW, skip), (STATE_BIAS_ROW, state_bias))
        for row, ref in rows + ((STEP_ROW, step_bias), (DECAY_ROW, decay)):
            size = ref.shape[0]
            table[row : row + 1, :size] = ref[...].reshape(1, size)
        wide[...] = jnp.zeros_like(wide)
        wide[:, : step_w.shape[1]] = step_w[...]

    return pl.pallas_call(
        kernel,
        out_shape=[
            jax.ShapeDtypeStruct((16, channels), F32),
            jax.ShapeDtypeStruct((arrays[-1].shape[0], LANES), BF16),
        ],
        cost_estimate=SMALL_COST,
        name="pack",
    )(*arrays)


def forward_kernel(first_piece, unused, block_base, *refs):
    tokens, cot, seg, par, gate_w, value_w, state_w, step_w, out_w = refs[:9]
    refs = refs[9:]
    if not first_piece:
        state_in, tail_in, state_tail_in = refs[:3]
        refs = refs[3:]
    refs = refs[unused:]
    (
        gate_out,
        vraw_out,
        pv_out,
        y_out,
        sraw_out,
        spv_out,
        step_out,
        saved_out,
        partial_out,
        stats_out,
        normed_out,
        state,
        tail_out,
        state_tail_out,
        vbuf,
        sbuf,
        scaled,
    ) = refs
    size = tokens.shape[0]
    channels = gate_w.shape[1]
    states = 2 * LANES

    @pl.when(pl.program_id(0) == 0)
    def _():
        if first_piece:
            state[...] = jnp.zeros_like(state)
            vbuf[:8] = jnp.zeros((8, channels), F32)
            sbuf[:8] = jnp.zeros((8, states), F32)
        else:
            state[...] = state_in[...]
            vbuf[:8] = tail_in[...]
            sbuf[:8] = state_tail_in[...]

    norm_gain = jnp.concatenate([par[GAIN_ROW : GAIN_ROW + 1], par[GAIN_ROW + 1 : GAIN_ROW + 2]], axis=1)
    scales = []
    for row in range(0, size, ROWS):
        wide = tokens[row : row + ROWS].astype(F32)
        scale = lax.rsqrt(jnp.mean(wide * wide, axis=-1, keepdims=True) + EPS)
        normed_out[row : row + ROWS] = (wide * scale * norm_gain).astype(BF16)
        scales.append(scale)
    normed = normed_out[...]
    vbuf[8:] = matmul(normed, value_w[...])
    sbuf[8:] = matmul(normed, state_w[...])
    step_out[...] = matmul(normed, step_w[...])
    gate_out[...] = matmul(normed, gate_w[...])

    def conv(buf, row, lanes, cols, kernel_row, bias_row):
        raw = buf[row + 8 : row + 8 + BLOCK, lanes]
        total = par[bias_row : bias_row + 1, lanes] + raw * par[kernel_row + 3 : kernel_row + 4, lanes]
        for back in range(1, 4):
            tap = par[kernel_row + 3 - back : kernel_row + 4 - back, lanes]
            moved = buf[row + 8 - back : row + 8 - back + BLOCK, lanes]
            total = total + moved * tap * cols[:, back : back + 1]
        return raw, total

    half = lax.broadcasted_iota(jnp.int32, (BLOCK, LANES), 1) < LANES // 2
    half_row = half[0:1]
    lane = lax.broadcasted_iota(jnp.int32, (BLOCK, LANES), 1)
    step_bias = par[STEP_ROW : STEP_ROW + 1, :LANES]
    rate = jnp.exp(par[DECAY_ROW : DECAY_ROW + 1, :LANES])
    skips = par[SKIP_ROW : SKIP_ROW + 1, :LANES]
    squares = []
    for sub in range(size // BLOCK):
        rows = slice(sub * BLOCK, (sub + 1) * BLOCK)
        row = sub * BLOCK
        block = block_base + pl.program_id(0) * (size // BLOCK) + sub
        cols, seg_row = segment_columns(seg, block, None, False)
        mixed_state = []
        for part in range(2):
            lanes = slice(part * LANES, (part + 1) * LANES)
            raw, spv = conv(sbuf, row, lanes, cols, STATE_KERNEL_ROW, STATE_BIAS_ROW)
            sraw_out[rows, lanes] = raw.astype(BF16)
            spv_out[rows, lanes] = spv
            mixed_state.append(spv * sigmoid(spv))
        b_low = mixed_state[0].astype(BF16)
        b_turned = mixed_state[0].T.astype(BF16)
        c_low = mixed_state[1].astype(BF16)
        steps, _, local, local_t, into, out, bias = decay_terms(
            step_out[rows], step_bias, rate, cols, seg_row
        )
        keep = into[BLOCK - 1 :]
        scores = matmul(c_low, b_low, (1, 1))
        square = jnp.zeros((BLOCK, LANES), F32)
        for pair in range(channels // LANES):
            lanes = slice(pair * LANES, (pair + 1) * LANES)
            raw, pv = conv(vbuf, row, lanes, cols, KERNEL_ROW, BIAS_ROW)
            vraw_out[rows, lanes] = raw.astype(BF16)
            pv_out[rows, lanes] = pv
            values = pv * sigmoid(pv)
            old = state[:, lanes]
            old_low = old.astype(BF16)
            saved_out[sub, :, lanes] = old_low
            u = values * pairwise(steps, pair, half)
            weights = [
                (scores * decay_of(local, local_t, bias, 2 * pair + k)).astype(BF16)
                for k in range(2)
            ]
            inner = matmul(jnp.concatenate(weights, axis=1), split_pair(u.astype(BF16), half))
            y_ssm = inner + matmul(c_low, old_low) * pairwise(into, pair, half)
            y_out[rows, lanes] = y_ssm
            leaving = (u * pairwise(out, pair, half)).astype(BF16)
            state[:, lanes] = old * pairwise(keep, pair, half_row) + matmul(b_turned, leaving)
            gate = gate_out[rows, lanes]
            gated = (y_ssm + pairwise(skips, pair, half_row) * values) * (gate * sigmoid(gate))
            square = square + gated * gated
            scaled[rows, lanes] = (gated * par[GATED_ROW : GATED_ROW + 1, lanes]).astype(BF16)
        squares.append(jnp.sum(square, axis=-1, keepdims=True))
    vbuf[:8] = vbuf[size:]
    sbuf[:8] = sbuf[size:]
    tail_out[...] = vbuf[:8]
    state_tail_out[...] = sbuf[:8]
    partial_out[...] = matmul(scaled[...], out_w[...])
    products = [
        jnp.sum(cot[row : row + ROWS].astype(F32) * partial_out[row : row + ROWS], axis=-1, keepdims=True)
        for row in range(0, size, ROWS)
    ]
    per = BLOCK // ROWS
    for sub in range(size // BLOCK):
        product = jnp.concatenate(products[sub * per : (sub + 1) * per], axis=0)
        scale = jnp.concatenate(scales[sub * per : (sub + 1) * per], axis=0)
        table = jnp.where(
            lane == 0, squares[sub], jnp.where(lane == 1, product, jnp.where(lane == 2, scale, 0.0))
        )
        stats_out[:, sub * BLOCK : (sub + 1) * BLOCK] = table.T[:8]


def backward_kernel(first_piece, unused, block_base, blocks, *refs):
    (
        place_ref,
        og_ref,
        gate_ref,
        vraw_ref,
        pv_ref,
        y_ref,
        sraw_ref,
        spv_ref,
        step_ref,
        own_stats,
        stats_1,
        stats_2,
        stats_3,
        saved_ref,
        seg,
        par,
    ) = refs[:16]
    refs = refs[16:]
    if not first_piece:
        carried_in = refs[:6]
        refs = refs[6:]
    refs = refs[unused:]
    (
        low_out,
        mixed_out,
        state_out,
        tail_out,
        state_tail_out,
        wide_acc,
        narrow_acc,
        heads_acc,
    ) = refs
    channels = gate_ref.shape[1]
    place = place_ref[0]

    @pl.when(pl.program_id(0) == 0)
    def _():
        outs = (state_out, tail_out, state_tail_out, wide_acc, narrow_acc, heads_acc)
        for k, ref in enumerate(outs):
            ref[...] = jnp.zeros_like(ref) if first_piece else carried_in[k][...]

    block = block_base + pl.num_programs(0) - 1 - pl.program_id(0)
    cols, seg_row = segment_columns(seg, block, blocks, True)
    stats = sum_over_places(place, own_stats[...], [stats_1[...], stats_2[...], stats_3[...]])
    stats = upright(stats)
    strength = lax.rsqrt(stats[:, 0:1] / INNER + EPS)
    pull = strength * strength * strength * stats[:, 1:2] / INNER

    half = lax.broadcasted_iota(jnp.int32, (BLOCK, LANES), 1) < LANES // 2
    half_row = half[0:1]
    spv = [spv_ref[:, :LANES], spv_ref[:, LANES:]]
    spv_sig = [sigmoid(v) for v in spv]
    b_part = spv[0] * spv_sig[0]
    c_part = spv[1] * spv_sig[1]
    b_low = b_part.astype(BF16)
    c_low = c_part.astype(BF16)
    c_turned = c_part.T.astype(BF16)
    step_raw = step_ref[...]
    step_bias = par[STEP_ROW : STEP_ROW + 1, :LANES]
    rate = jnp.exp(par[DECAY_ROW : DECAY_ROW + 1, :LANES])
    skips = par[SKIP_ROW : SKIP_ROW + 1, :LANES]
    steps, rates, local, local_t, into, out, bias = decay_terms(
        step_raw, step_bias, rate, cols, seg_row
    )
    keep = into[BLOCK - 1 :]
    scores = matmul(c_low, b_low, (1, 1))

    def conv_back(pre_grad, raw, lanes, after, kernel_row, acc):
        ext = jnp.concatenate([pre_grad, after[:, lanes]], axis=0)
        after[:, lanes] = pre_grad[:8]
        total = pre_grad * par[kernel_row + 3 : kernel_row + 4, lanes]
        acc[24:32, lanes] += fold(raw * pre_grad)
        acc[32:40, lanes] += fold(pre_grad)
        for ahead in range(1, 4):
            moved = pltpu.roll(ext, BLOCK + 8 - ahead, 0)[:BLOCK]
            term = moved * cols[:, ahead : ahead + 1]
            total = total + term * par[kernel_row + 3 - ahead : kernel_row + 4 - ahead, lanes]
            acc[8 * (3 - ahead) : 8 * (4 - ahead), lanes] += fold(raw * term)
        return total

    score_grad = jnp.zeros((BLOCK, BLOCK), F32)
    b_grad = jnp.zeros((BLOCK, LANES), F32)
    c_grad = jnp.zeros((BLOCK, LANES), F32)
    spread_dl = jnp.zeros((BLOCK, LANES), F32)
    spread_ds = jnp.zeros((BLOCK, LANES), F32)
    spread_end = jnp.zeros((8, LANES), F32)
    for pair in range(channels // LANES):
        lanes = slice(pair * LANES, (pair + 1) * LANES)
        spread = (
            lax.broadcasted_iota(jnp.int32, (LANES, LANES), 0) // (LANES // 2) + 2 * pair
            == lax.broadcasted_iota(jnp.int32, (LANES, LANES), 1)
        ).astype(BF16)
        gain = par[GATED_ROW : GATED_ROW + 1, lanes]
        skip = pairwise(skips, pair, half_row)
        gate = gate_ref[:, lanes]
        gate_sig = sigmoid(gate)
        gate_silu = gate * gate_sig
        pv = pv_ref[:, lanes]
        pv_sig = sigmoid(pv)
        values = pv * pv_sig
        og = og_ref[:, lanes]
        y_ssm = y_ref[:, lanes]
        y = y_ssm + skip * values
        gated = y * gate_silu
        strong = gated * strength
        mixed_out[:, lanes] = (strong * gain).astype(BF16)
        gated_grad = gain * strength * og - gated * pull
        low_out[:, lanes] = (
            gated_grad * y * (gate_sig * (1.0 + gate * (1.0 - gate_sig)))
        ).astype(BF16)
        grad = gated_grad * gate_silu
        wide_acc[40:48, lanes] += fold(og * strong)
        wide_acc[48:56, lanes] += fold(grad * values)

        state_grad = state_out[:, lanes]
        state_grad_low = state_grad.astype(BF16)
        old_low = saved_ref[0, :, lanes]
        pair_steps = pairwise(steps, pair, half)
        pair_out = pairwise(out, pair, half)
        u = values * pair_steps
        u_low = u.astype(BF16)
        g_low = grad.astype(BF16)
        g_split = split_pair(g_low, half)
        decays = [decay_of(local, local_t, bias, 2 * pair + k) for k in range(2)]
        weights = jnp.concatenate([(scores * d).astype(BF16) for d in decays], axis=0)
        weight_grad = matmul(g_split, u_low, (1, 1))
        score_grad = score_grad + weight_grad[:BLOCK] * decays[0] + weight_grad[BLOCK:] * decays[1]
        u_grad_out = matmul(b_low, state_grad_low) * pair_out
        u_grad = matmul(weights, g_split, (0, 0)) + u_grad_out
        u_near = u_low.astype(F32)
        spread_dl = spread_dl + group_sum(g_low.astype(F32) * y_ssm - u_near * u_grad, spread)
        spread_ds = spread_ds + group_sum(values * u_grad, spread)
        keep_row = pairwise(keep, pair, half_row)
        spread_end = spread_end + group_sum(
            fold(u_near * u_grad_out) + fold(state_grad * old_low.astype(F32)) * keep_row, spread
        )
        entering = (grad * pairwise(into, pair, half)).astype(BF16)
        leaving = (u * pair_out).astype(BF16)
        c_grad = c_grad + matmul(entering, old_low, (1, 1))
        b_grad = b_grad + matmul(leaving, state_grad_low, (1, 1))
        state_out[:, lanes] = state_grad * keep_row + matmul(c_turned, entering)
        pre_grad = (pair_steps * u_grad + skip * grad) * (pv_sig * (1.0 + pv * (1.0 - pv_sig)))
        raw_grad = conv_back(
            pre_grad, vraw_ref[:, lanes].astype(F32), lanes, tail_out, KERNEL_ROW, wide_acc
        )
        low_out[:, channels + pair * LANES : channels + (pair + 1) * LANES] = raw_grad.astype(BF16)
    score_low = score_grad.astype(BF16)
    c_grad = c_grad + matmul(score_low, b_low)
    b_grad = b_grad + matmul(score_low, c_low, (0, 0))
    rate_grad = exact(triangle(False), spread_dl) + jnp.sum(spread_end, axis=0, keepdims=True)
    step_grad = (spread_ds - rate * rate_grad) * sigmoid(step_raw + step_bias)
    heads_acc[0:8] += fold(step_grad)
    heads_acc[8:16] += fold(rates * rate_grad)
    for part, grad in enumerate((b_grad, c_grad)):
        lanes = slice(part * LANES, (part + 1) * LANES)
        pre_grad = grad * (spv_sig[part] * (1.0 + spv[part] * (1.0 - spv_sig[part])))
        raw_grad = conv_back(
            pre_grad, sraw_ref[:, lanes].astype(F32), lanes, state_tail_out, STATE_KERNEL_ROW, narrow_acc
        )
        at = 2 * channels + part * LANES
        low_out[:, at : at + LANES] = raw_grad.astype(BF16)
    heads_here = channels // (LANES // 2)
    low_out[:, 2 * channels + 2 * LANES :] = pltpu.roll(step_grad, place * heads_here, 1).astype(BF16)


def out_grad_kernel(unused, cot, out_w, *refs):
    og, token = refs[unused : unused + 2]
    og[...] = matmul(cot[...], out_w[...], (1, 1))
    token[...] = jnp.zeros((8, LANES), F32)


def run_out_grad(chain, cot, out_w, passes):
    length, channels = cot.shape[0], out_w.shape[0]
    deps = chain.deps()
    results = pl.pallas_call(
        functools.partial(out_grad_kernel, len(deps) + len(passes)),
        grid=(length // CHUNK,),
        in_specs=[pl.BlockSpec((CHUNK, D), lambda i: (i, 0)), whole(out_w.shape)]
        + [ANYWHERE for _ in deps + passes],
        out_specs=[pl.BlockSpec((CHUNK, channels), lambda i: (i, 0)), whole((8, LANES))]
        + [ANYWHERE for _ in passes],
        out_shape=[
            jax.ShapeDtypeStruct((length, channels), F32),
            jax.ShapeDtypeStruct((8, LANES), F32),
        ]
        + [jax.ShapeDtypeStruct(p.shape, p.dtype) for p in passes],
        input_output_aliases={2 + len(deps) + k: 2 + k for k in range(len(passes))},
        compiler_params=pltpu.CompilerParams(vmem_limit_bytes=VMEM_LIMIT),
        cost_estimate=SMALL_COST,
        name="out_grad",
    )(cot, out_w, *deps, *passes)
    chain.last = results[1]
    return results[0], results[2:]


def run_matmul(chain, body, ins, outs, count, scratch=(), name=None):
    deps = chain.deps()
    arrays = [a for a, _, _ in ins]

    def kernel(*refs):
        body(*refs[: len(arrays)], *refs[len(arrays) + len(deps) :])
        refs[len(arrays) + len(deps) + len(outs)][...] = jnp.zeros((8, LANES), F32)

    results = pl.pallas_call(
        kernel,
        grid=(count,),
        in_specs=[whole(a.shape) if m is None else pl.BlockSpec(b, m) for a, b, m in ins]
        + [ANYWHERE for _ in deps],
        out_specs=[pl.BlockSpec(b, m) for _, b, m in outs] + [whole((8, LANES))],
        out_shape=[jax.ShapeDtypeStruct(s, F32) for s, _, _ in outs]
        + [jax.ShapeDtypeStruct((8, LANES), F32)],
        scratch_shapes=list(scratch),
        compiler_params=pltpu.CompilerParams(vmem_limit_bytes=VMEM_LIMIT),
        cost_estimate=SMALL_COST,
        name=name,
    )(*arrays, *deps)
    chain.last = results[-1]
    return results[:-1]


def gain_row(value, count):
    out = []
    for k in range(count // BLOCK):
        column = jnp.sum(value[k * BLOCK : (k + 1) * BLOCK], axis=-1, keepdims=True)
        out.append(jnp.broadcast_to(column, (BLOCK, BLOCK)).T[:8])
    return jnp.concatenate(out, axis=1)


def run_rest_grad(chain, normed, low, small_rows, weights):
    width = small_rows.shape[1]
    count = D // CHUNK
    states = weights[0].shape[1]

    def body(left, right, extra, state_w, step_w, out, gain, token):
        @pl.when(pl.program_id(0) < count)
        def _():
            value = matmul(left[...], right[...], (0, 0))
            out[...] = value
            both = jnp.concatenate([state_w[...], step_w[...]], axis=1).astype(F32)
            gain[...] = gain_row(value * both, CHUNK)

        @pl.when(pl.program_id(0) == count)
        def _():
            out[...] = extra[...]

    length, total = low.shape
    held = lambda i: jnp.minimum(i, count - 1)
    tile = lambda a: (a, (CHUNK, a.shape[1]), lambda i: (held(i), 0))
    return run_matmul(
        chain,
        body,
        [
            (normed, (length, CHUNK), lambda i: (0, held(i))),
            (low, (length, width), lambda i: (0, total // width - 1)),
            (small_rows, None, None),
            *[tile(w) for w in weights],
        ],
        [
            ((D + CHUNK, width), (CHUNK, width), lambda i: (i, 0)),
            ((8, D), (8, CHUNK), lambda i: (0, held(i))),
        ],
        count + 1,
        name="rest_grad",
    )


def run_weight_grads(chain, core, normed, low, cot, mixed, weights, gains, unit):
    length = normed.shape[0]
    channels = mixed.shape[1]
    tile = D // 4
    deps = chain.deps()

    def which(i, p):
        return jnp.where(i < 2, 1 - p[0], p[0]) * 2 + i % 2

    def kernel(place, left, right, cots, mix, gate_w, value_w, gain_in, *refs):
        outs, gain, token = refs[len(deps) : len(deps) + 4], refs[-2], refs[-1]
        i = pl.program_id(0)

        @pl.when(i == 0)
        def _():
            gain[...] = gain_in[...]
            token[...] = jnp.zeros((8, LANES), F32)

        gate = matmul(left[...], right[:, :channels], (0, 0))
        value = matmul(left[...], right[:, channels:], (0, 0))
        out = matmul(cots[...], mix[...], (0, 0))
        at = pl.ds(pl.multiple_of(which(i, place) * tile, LANES), tile)
        products = gate * gate_w[...].astype(F32) + value * value_w[...].astype(F32)
        gain[:, at] = gain[:, at] + gain_row(products, tile)
        for k in range(4):

            @pl.when(i == k)
            def _(k=k):
                for n in range(tile // unit):
                    rows = slice(n * unit, (n + 1) * unit)
                    for m, part in enumerate((gate, value, out)):
                        first = (3 * n + m) * unit
                        outs[k][first : first + unit, :] = part[rows]

    lanes = lambda i, p: (0, which(i, p))
    weight_spec = pl.BlockSpec((tile, channels), lambda i, p: (which(i, p), 0))
    results = pl.pallas_call(
        kernel,
        grid_spec=pltpu.PrefetchScalarGridSpec(
            num_scalar_prefetch=1,
            grid=(4,),
            in_specs=[
                pl.BlockSpec((length, tile), lanes),
                pl.BlockSpec((length, 2 * channels), lambda i, p: (0, 0)),
                pl.BlockSpec((length, tile), lanes),
                whole(mixed.shape),
                weight_spec,
                weight_spec,
                whole(gains.shape),
            ]
            + [ANYWHERE for _ in deps],
            out_specs=[whole((3 * tile, channels))] * 4 + [whole(gains.shape), whole((8, LANES))],
        ),
        out_shape=[jax.ShapeDtypeStruct((3 * tile, channels), F32)] * 4
        + [jax.ShapeDtypeStruct(gains.shape, F32), jax.ShapeDtypeStruct((8, LANES), F32)],
        compiler_params=pltpu.CompilerParams(vmem_limit_bytes=VMEM_LIMIT),
        cost_estimate=SMALL_COST,
        name="weight_grads",
    )(core, normed, low, cot, mixed, *weights, gains, *deps)
    chain.last = results[-1]
    return results[:4], results[4]


def run_assemble(chain, core, own, got, unit):
    rows, channels = own[0].shape
    tile = rows // 3
    deps = chain.deps()

    def kernel(place, own_a, own_b, got_a, got_b, *refs):
        gate, value, out, token = refs[len(deps) :]
        i = pl.program_id(0)
        token[...] = jnp.zeros((8, LANES), F32)
        for n, (mine, other) in enumerate(((own_a, got_a), (own_b, got_b))):

            @pl.when(i % 2 == n)
            def _(mine=mine, other=other):
                use_own = i // 2 == place[0]
                pieces = []
                for k in range(rows // unit):
                    at = slice(k * unit, (k + 1) * unit)
                    pieces.append(jnp.where(use_own, mine[at, :], other[at, :]))
                gate[...] = jnp.concatenate(pieces[0::3], axis=0)
                value[...] = jnp.concatenate(pieces[1::3], axis=0)
                out[...] = jnp.concatenate(pieces[2::3], axis=0).T

    row = pl.BlockSpec((tile, channels), lambda i, p: (i, 0))
    gate, value, out, chain.last = pl.pallas_call(
        kernel,
        grid_spec=pltpu.PrefetchScalarGridSpec(
            num_scalar_prefetch=1,
            grid=(4,),
            in_specs=[whole(own[0].shape)] * 4 + [ANYWHERE for _ in deps],
            out_specs=[
                row,
                row,
                pl.BlockSpec((channels, tile), lambda i, p: (0, i)),
                whole((8, LANES)),
            ],
        ),
        out_shape=[
            jax.ShapeDtypeStruct((D, channels), F32),
            jax.ShapeDtypeStruct((D, channels), F32),
            jax.ShapeDtypeStruct((channels, D), F32),
            jax.ShapeDtypeStruct((8, LANES), F32),
        ],
        compiler_params=pltpu.CompilerParams(vmem_limit_bytes=VMEM_LIMIT),
        cost_estimate=SMALL_COST,
        name="assemble",
    )(core, *own, *got, *deps)
    return gate, value, out


def run_total(chain, low, weights):
    length, width = low.shape

    def body(left, gate_w, value_w, state_w, step_w, out, token, joined):
        @pl.when(pl.program_id(0) == 0)
        def _():
            at = 0
            for ref in (gate_w, value_w, state_w, step_w):
                joined[:, at : at + ref.shape[1]] = ref[...]
                at += ref.shape[1]

        out[...] = matmul(left[...], joined[...], (1, 1))

    (out,) = run_matmul(
        chain,
        body,
        [(low, (CHUNK, width), lambda i: (i, 0))] + [(w, None, None) for w in weights],
        [((length, D), (CHUNK, D), lambda i: (i, 0))],
        length // CHUNK,
        scratch=[pltpu.VMEM((D, width), BF16)],
        name="normed_grad",
    )
    return out


def whole(shape):
    return pl.BlockSpec(shape, lambda i, *_: (0,) * len(shape))


ANYWHERE = pl.BlockSpec(memory_space=pl.ANY)


def run_forward(start, count, tokens, cot, seg, small, carried, kept, deps):
    channels = small["gate_w"].shape[1]
    states = 2 * LANES
    size = CHUNK
    length = count * size
    first = start // size
    per = size // BLOCK
    full = tokens.shape[0]

    def row_in(width):
        return pl.BlockSpec((size, width), lambda i: (first + i, 0))

    def row_out(width):
        return pl.BlockSpec((size, width), lambda i: (i, 0))

    constant = [small[n] for n in ("par", "gate_w", "value_w", "state_w", "step_w", "out_w")]
    carry_shapes = [(LANES, channels), (8, channels), (8, states)]
    widths = (
        (channels, F32),
        (channels, BF16),
        (channels, F32),
        (channels, F32),
        (states, BF16),
        (states, F32),
        (LANES, F32),
    )
    inputs = [tokens, cot, seg, *constant, *carried, *deps, *kept]
    outs = pl.pallas_call(
        functools.partial(forward_kernel, not carried, len(deps) + len(kept), start // BLOCK),
        grid=(count,),
        in_specs=[row_in(D), row_in(D), whole(seg.shape)]
        + [whole(c.shape) for c in constant]
        + [whole(c.shape) for c in carried]
        + [ANYWHERE for _ in deps + kept],
        out_specs=[row_out(w) for w, _ in widths]
        + [pl.BlockSpec((per, LANES, channels), lambda i: (i, 0, 0))]
        + [row_out(D)]
        + [pl.BlockSpec((8, size), lambda i: (0, first + i))]
        + [row_in(D)]
        + [whole(c) for c in carry_shapes],
        out_shape=[jax.ShapeDtypeStruct((length, w), k) for w, k in widths]
        + [jax.ShapeDtypeStruct((length // BLOCK, LANES, channels), BF16)]
        + [jax.ShapeDtypeStruct((length, D), F32)]
        + [jax.ShapeDtypeStruct((8, full), F32)]
        + [jax.ShapeDtypeStruct((full, D), BF16)]
        + [jax.ShapeDtypeStruct(c, F32) for c in carry_shapes],
        scratch_shapes=[
            pltpu.VMEM((size + 8, channels), F32),
            pltpu.VMEM((size + 8, states), F32),
            pltpu.VMEM((size, channels), BF16),
        ],
        input_output_aliases={len(inputs) - len(kept) + k: 9 + k for k in range(len(kept))},
        compiler_params=pltpu.CompilerParams(vmem_limit_bytes=VMEM_LIMIT),
        cost_estimate=SMALL_COST,
        name="forward_piece",
    )(*inputs)
    outs = list(outs)
    names = ("gate", "vraw", "pv", "y", "sraw", "spv", "step", "saved", "partial")
    return dict(zip(names, outs[:9])), outs[9:11], outs[11:]


def run_backward(start, piece, og, stats, place, seg, small, carried, low, mixed, deps):
    channels = small["gate_w"].shape[1]
    length = piece["gate"].shape[0]
    full = og.shape[0]
    count = length // BLOCK
    first = start // BLOCK
    flip = lambda i: count - 1 - i

    def row(width):
        return pl.BlockSpec((BLOCK, width), lambda i, *_: (flip(i), 0))

    def shared(width):
        return pl.BlockSpec((BLOCK, width), lambda i, *_: (first + flip(i), 0))

    names = ("gate", "vraw", "pv", "y", "sraw", "spv", "step")
    ins = [piece[n] for n in names]
    low_width = 2 * channels + 3 * LANES
    kept = [] if low is None else [low, mixed]
    carry_shapes = [
        (LANES, channels),
        (8, channels),
        (8, 2 * LANES),
        (56, channels),
        (40, 2 * LANES),
        (16, LANES),
    ]
    inputs = [og, *ins, *stats, piece["saved"], seg, small["par"], *carried, *deps, *kept]
    outs = pl.pallas_call(
        functools.partial(
            backward_kernel, not carried, len(deps) + len(kept), first, full // BLOCK
        ),
        grid_spec=pltpu.PrefetchScalarGridSpec(
            num_scalar_prefetch=1,
            grid=(count,),
            in_specs=[shared(channels)]
            + [row(a.shape[1]) for a in ins]
            + [pl.BlockSpec((8, BLOCK), lambda i, *_: (0, first + flip(i))) for _ in stats]
            + [pl.BlockSpec((1, LANES, channels), lambda i, *_: (flip(i), 0, 0))]
            + [whole(seg.shape), whole(small["par"].shape)]
            + [whole(c.shape) for c in carried]
            + [ANYWHERE for _ in deps + kept],
            out_specs=[shared(low_width), shared(channels)] + [whole(c) for c in carry_shapes],
        ),
        out_shape=[
            jax.ShapeDtypeStruct((full, low_width), BF16),
            jax.ShapeDtypeStruct((full, channels), BF16),
        ]
        + [jax.ShapeDtypeStruct(c, F32) for c in carry_shapes],
        compiler_params=pltpu.CompilerParams(vmem_limit_bytes=VMEM_LIMIT),
        cost_estimate=SMALL_COST,
        input_output_aliases={1 + len(inputs) - 2 + k: k for k in range(len(kept))},
        name="backward_piece",
    )(place, *inputs)
    return outs[0], outs[1], list(outs[2:])


class Chain:
    def __init__(self):
        self.last = None
        self.more = []

    def deps(self):
        found = ([] if self.last is None else [self.last]) + self.more
        self.more = []
        return found


def rowwise(
    chain, place, body, ins, outs, rows, passes=(), step=0, whole_place=False, name=None
):
    step = step or STEP
    steps = rows // step

    def spec(width, first, most=steps):
        if callable(first):
            return pl.BlockSpec(
                (step, width),
                lambda i, p: (
                    jnp.maximum(first(p if whole_place else p[0]) + jnp.minimum(i, most - 1), 0),
                    0,
                ),
            )
        return pl.BlockSpec((step, width), lambda i, p: (first + jnp.minimum(i, most - 1), 0))

    def lying(height, first):
        if callable(first):
            return pl.BlockSpec((height, STEP), lambda i, p: (0, first(p[0]) + i))
        return pl.BlockSpec((height, STEP), lambda i, p: (0, first + i))

    def spec_of(array, first, across=False, most=steps):
        if first is None:
            return fixed(array.shape)
        return lying(array.shape[0], first) if across else spec(array.shape[1], first, most)

    def fixed(shape):
        return pl.BlockSpec(shape, lambda i, p: (0,) * len(shape))

    anywhere = pl.BlockSpec(memory_space=pl.ANY)
    arrays = [entry[0] for entry in ins]
    in_specs = [spec_of(*entry) for entry in ins]
    kept = [(k, o[4]) for k, o in enumerate(outs) if o[4] is not None]
    deps = chain.deps()
    inputs = [*arrays, *[a for _, a in kept], *passes, *deps]
    aliases = {1 + len(arrays) + n: k for n, (k, _) in enumerate(kept)}
    for n in range(len(passes)):
        aliases[1 + len(arrays) + len(kept) + n] = len(outs) + n

    def kernel(place_ref, *refs):
        results = refs[len(inputs) :]
        values = body(place_ref if whole_place else place_ref[0], *refs[: len(arrays)])
        for ref, value in zip(results[: len(outs)], values):
            ref[...] = value
        results[-1][...] = jnp.zeros((8, LANES), F32)

    results = pl.pallas_call(
        kernel,
        grid_spec=pltpu.PrefetchScalarGridSpec(
            num_scalar_prefetch=1,
            grid=(steps,),
            in_specs=in_specs + [anywhere] * (len(inputs) - len(arrays)),
            out_specs=[spec(o[1], o[3], *o[5:]) for o in outs]
            + [anywhere] * len(passes)
            + [fixed((8, LANES))],
        ),
        out_shape=[jax.ShapeDtypeStruct((o[0], o[1]), o[2]) for o in outs]
        + [jax.ShapeDtypeStruct(p.shape, p.dtype) for p in passes]
        + [jax.ShapeDtypeStruct((8, LANES), F32)],
        input_output_aliases=aliases,
        compiler_params=pltpu.CompilerParams(vmem_limit_bytes=VMEM_LIMIT),
        cost_estimate=SMALL_COST,
        name=name,
    )(place, *inputs)
    chain.last = results[-1]
    return list(results[:-1])


def after(chain, *arrays):
    def kernel(*refs):
        refs[-1][...] = jnp.zeros((8, LANES), F32)

    anywhere = pl.BlockSpec(memory_space=pl.ANY)
    deps = chain.deps()
    results = pl.pallas_call(
        kernel,
        in_specs=[anywhere] * (len(arrays) + len(deps)),
        out_specs=[anywhere] * len(arrays) + [pl.BlockSpec(memory_space=pltpu.VMEM)],
        out_shape=[jax.ShapeDtypeStruct(a.shape, a.dtype) for a in arrays]
        + [jax.ShapeDtypeStruct((8, LANES), F32)],
        input_output_aliases={k: k for k in range(len(arrays))},
        cost_estimate=SMALL_COST,
        name="in_order",
    )(*arrays, *deps)
    chain.last = results[-1]
    return list(results[:-1])


INWARD = ((0, 1), (3, 2))
ACROSS = ((1, 2), (2, 1))
OUTWARD = ((1, 0), (2, 3))


def on_device(
    tokens,
    norm_gain,
    gate_weight,
    value_weight,
    state_weight,
    step_weight,
    value_kernel,
    value_bias,
    state_kernel,
    state_bias,
    step_bias,
    decay_log,
    skip_scale,
    gated_gain,
    out_weight,
    segment_ids,
    out_cotangent,
):
    parts = lax.axis_size("tensor")
    place = lax.axis_index("tensor")
    middle = jnp.logical_and(place > 0, place < parts - 1)
    length = tokens.shape[0]
    channels = gate_weight.shape[1]
    head_count = step_bias.shape[0]
    rows = length // parts
    states = 2 * LANES
    par, step_wide = run_pack(
        norm_gain,
        value_kernel,
        value_bias,
        gated_gain,
        skip_scale,
        state_kernel,
        state_bias,
        step_bias,
        decay_log,
        step_weight,
    )
    small = {
        "gate_w": gate_weight,
        "value_w": value_weight,
        "state_w": state_weight,
        "step_w": step_wide,
        "out_w": out_weight,
        "par": par,
    }
    chain = Chain()
    where = place.astype(jnp.int32)[None]
    send = lambda x, pairs: lax.ppermute(x, "tensor", pairs)
    run = functools.partial(rowwise, chain, where)
    steps = lambda n: n // STEP

    spans = [p * length // sum(PIECES) for p in PIECES]
    firsts = [sum(spans[:k]) for k in range(len(spans))]
    pieces = []
    carried = []
    kept = []
    late = {}
    part = 64
    count = len(spans)
    outer, inner, outer_sent, pair_sum = {}, {}, {}, {}

    def forward():
        nonlocal carried, kept
        k = len(pieces)
        outs, kept, carried = run_forward(
            firsts[k],
            spans[k] // CHUNK,
            tokens,
            out_cotangent,
            segment_ids,
            small,
            carried,
            kept,
            chain.deps(),
        )
        pieces.append(outs)
        chain.last = carried[2]

    part = 64

    def send_outer(n, message, both=True):
        outer_sent[n] = message
        outer[n] = send(message, INWARD + OUTWARD if both else INWARD)

    is_middle = lambda p: jnp.logical_and(p > 0, p < parts - 1)
    per = steps(rows)
    at_ends = lambda low_end, high_end: lambda p: jnp.where(p < 2, low_end, high_end) * per

    def event(n, following=None, middle_segment=None):
        chunk = n < count
        extra = [(late["share"], None), (late["share_got"], None)] if n == SHARE_CHUNK else []
        step = part if extra else STEP
        blocks = spans[0] // step
        size = spans[0] + (part if extra else 0)
        if chunk:
            mine = (pieces[n]["partial"], 0, False, blocks)
        else:
            mine = (late["total"], middle_segment, False, blocks)
        ins = [mine, (outer[n], 0, False, blocks)]
        outs = [(size, D, F32, 0, None)]
        if n > 0:
            array, first = following
            if callable(first) and extra:
                first = functools.partial(lambda p, f: f(p) * (STEP // part), f=first)
            if n <= count:
                ins += [(pair_sum[n - 1], 0, False, blocks), (inner[n], 0, False, blocks)]
                ins += [(array, first, False, blocks)]
            else:
                ins += [(array, first, False, blocks), (inner[n], 0, False, blocks)]
            outs.append((spans[0], D, F32, 0, None, blocks))

        def body(p, a, b, *others):
            value = a[...] + b[...]
            if extra:
                x, y = others[-2:]
                value = jnp.where(pl.program_id(0) == blocks, x[...] + y[...], value)
            results = [value]
            if n > 0:
                message = others[0][...] + others[1][...]
                if n <= count:
                    message = jnp.where(is_middle(p), message, others[2][...])
                results.append(message)
            return results

        results = run(body, ins + extra, outs, size, step=step, name="event")
        pair_sum[n] = results[0]
        inner[n + 1] = send(results[0], ACROSS)
        if n > 0:
            send_outer(n + 1, results[1])
        else:
            send_outer(1, following[0], False)

    def finish_chunk(k):
        def body(p, own, got, token, *stats):
            inside = jnp.logical_and(p > 0, p < parts - 1)
            total = jnp.where(inside, own[...], got[...])
            table = upright(sum_over_places(p, stats[0][...], [x[...] for x in stats[1:]]))
            strength = lax.rsqrt(table[:, 0:1] / INNER + EPS)
            return [(token[...].astype(F32) + total * strength).astype(BF16)]

        first = steps(firsts[k])
        (late["block_out"],) = run(
            body,
            [(outer_sent[k + 2], 0), (outer[k + 2], 0), (tokens, first)]
            + [(x, first, True) for x in late["stats"]],
            [(length, D, BF16, first, late.get("block_out"))],
            spans[k],
            name="finish_chunk",
        )

    def finish_grad(n):
        def body(p, mine, side_got, middle_got, token, scale, cot, gain):
            token = token[...].astype(F32)
            scale = upright(scale[...])[:, 2:3]
            weighted = (mine[...] + side_got[...] + middle_got[...]) * gain[...]
            pull = jnp.sum(weighted * token, axis=-1, keepdims=True) / D
            return [cot[...].astype(F32) + scale * weighted - token * scale * scale * scale * pull]

        mine = lambda p: p * per
        (late["tokens_grad"],) = run(
            body,
            [
                (late["total"], mine),
                (outer[n], 0),
                (inner[n], 0),
                (tokens, mine),
                (late["own_stats"], mine, True),
                (out_cotangent, mine),
                (norm_gain[None], None),
            ],
            [(rows, D, F32, 0, None)],
            rows,
            name="finish_grad",
        )

    low = mixed = None
    back = []

    def backward(k):
        nonlocal low, mixed, back
        low, mixed, back = run_backward(
            firsts[k],
            pieces[k],
            late["og"],
            late["stats"],
            where,
            segment_ids,
            small,
            back,
            low,
            mixed,
            chain.deps(),
        )
        chain.last = back[2]

    def exchange_stats():
        own = late["own_stats"] = kept[0]
        late["stats"] = [own] + [
            send(own, [(k, (k + turn) % parts) for k in range(parts)]) for turn in range(1, parts)
        ]
        late["og"], _ = run_out_grad(chain, out_cotangent, out_weight, [])
        chain.more = late["stats"][1:]

    forward()
    send_outer(0, pieces[0]["partial"], False)
    forward()
    forward()
    forward()
    exchange_stats()
    event(0, (pieces[1]["partial"], 0))
    backward(3)
    backward(2)
    backward(1)
    backward(0)
    event(1, (pieces[2]["partial"], 0))

    normed = kept[1]
    wide_acc, narrow_acc, heads_acc = back[3:]
    step_place = lax.dynamic_update_slice(
        jnp.zeros((D, LANES), BF16), step_weight, (0, place * head_count)
    )
    back_weights = [gate_weight, value_weight, state_weight, step_place]
    width = 3 * LANES
    fit = lambda x: jnp.pad(x.reshape(-1), (0, -x.size % width)).reshape(-1, width)
    narrow = narrow_acc.reshape(5, 8, states).sum(axis=1)
    wide_sums = wide_acc.reshape(7, 8, channels).sum(axis=1)
    head_sums = heads_acc.reshape(2, 8, LANES).sum(axis=1)[:, :head_count]
    skip_grad = wide_sums[6].reshape(head_count, channels // head_count).sum(axis=1)
    mine = jnp.concatenate([fit(wide_sums[:6]), fit(jnp.concatenate([head_sums, skip_grad[None]]))])
    mine_rows = mine.shape[0]
    slots = jnp.where(
        lax.broadcasted_iota(jnp.int32, (parts, 1, 1), 0) == place, mine[None], 0.0
    ).reshape(-1, width)
    narrow_rows = fit(narrow)
    filler = jnp.zeros((CHUNK - narrow_rows.shape[0] - slots.shape[0], width), F32)
    shared, gains = run_rest_grad(
        chain, normed, low, jnp.concatenate([narrow_rows, slots, filler]), back_weights[2:]
    )

    ways = lax.axis_size("dp")
    own_dp = lax.axis_index("dp")
    bits = []
    while 2 ** len(bits) < ways:
        bits.append(2 ** len(bits))
    shared_rows = shared.shape[0]
    swap = lambda x, bit: lax.ppermute(x, "dp", [(k, k ^ bit) for k in range(ways)])
    side = lambda n: (own_dp // bits[n]) % 2
    halving = {"keep": shared, "rows": shared_rows, "got": None}

    def halve(n):
        keep, size = halving["keep"], halving["rows"]
        if n > 0:
            add = lambda p, a, b: [a[...] + b[...]]
            size = size // 2
            (keep,) = rowwise(
                chain,
                side(n - 1).astype(jnp.int32)[None],
                add,
                [(keep, lambda p: p), (halving["got"], 0)],
                [(size, width, F32, 0, None)],
                size,
                step=size,
                name="halve",
            )
            halving["rows"] = size
        if n < len(bits):
            away = lax.dynamic_slice_in_dim(keep, (1 - side(n)) * (size // 2), size // 2, 0)
            halving["got"] = swap(away, bits[n])
        halving["keep"] = keep

    core = side(0).astype(jnp.int32)[None]
    core_bit, axes = bits[0], list(range(1, len(bits)))
    turned = axes[len(axes) // 2 :] + axes[: len(axes) // 2]
    orders = (axes, turned)
    sums = {}

    def reduce_step(step):
        sides = jnp.stack([side(orders[k][step]).astype(jnp.int32) for k in range(2)])
        ins, outs = [], []
        size = sums["keep"][0].shape[0] // 2
        unit = size if size < 512 else size // 2
        for k in range(2):
            for stay in (1, 0):
                at = functools.partial(
                    lambda p, k, stay: (p[k] if stay else 1 - p[k]) * (size // unit), k=k, stay=stay
                )
                ins += [(sums["keep"][k], at), (sums["got"][k], at)]
                outs.append((size, channels, F32, 0, None))
        results = rowwise(
            chain,
            sides,
            lambda p, *refs: [refs[2 * n][...] + refs[2 * n + 1][...] for n in range(4)],
            ins,
            outs,
            size,
            step=unit,
            whole_place=True,
            name="reduce_step",
        )
        sums["keep"] = [results[0], results[2]]
        sums["size"] = size
        sums["got"] = [swap(results[2 * k + 1], bits[orders[k][step]]) for k in range(2)]

    unit = D // 4 // 2 ** len(axes)

    def reduce_start():
        tiles, sums["gains"] = run_weight_grads(
            chain, core, normed, low, out_cotangent, mixed, back_weights[:2], gains, unit
        )
        sums["keep"] = tiles[2:]
        sums["got"] = [swap(x, core_bit) for x in tiles[:2]]

    def gather_first():
        sums["full"] = rowwise(
            chain,
            where,
            lambda p, a, b, c, d: [a[...] + b[...], c[...] + d[...]],
            [(x, 0) for k in range(2) for x in (sums["keep"][k], sums["got"][k])],
            [(sums["size"], channels, F32, 0, None)] * 2,
            sums["size"],
            step=sums["size"],
            name="gather_first",
        )
        step = len(axes) - 1
        sums["got"] = [swap(sums["full"][k], bits[orders[k][step]]) for k in range(2)]

    def gather_step(step):
        size = sums["size"]
        sides = jnp.stack([side(orders[k][step]).astype(jnp.int32) for k in range(2)])

        def body(p, *refs):
            upper = pl.program_id(0)
            picked = []
            for k in range(2):
                own, got = refs[2 * k][...], refs[2 * k + 1][...]
                picked.append(jnp.where(upper == p[k], own, got))
            return picked

        sums["full"] = rowwise(
            chain,
            sides,
            body,
            [(x, 0, False, 1) for k in range(2) for x in (sums["full"][k], sums["got"][k])],
            [(2 * size, channels, F32, 0, None)] * 2,
            2 * size,
            step=size,
            whole_place=True,
            name="gather_step",
        )
        sums["size"] = 2 * size
        if step > 0:
            sums["got"] = [swap(sums["full"][k], bits[orders[k][step - 1]]) for k in range(2)]

    def gather_core():
        sums["got"] = [swap(x, core_bit) for x in sums["full"]]

    halve(0)
    reduce_start()
    gain_rows = fit(sums["gains"][0] / norm_gain)
    gain_rows = jnp.pad(gain_rows, ((0, 8 - gain_rows.shape[0]), (0, 0)))
    halve(1)
    event(2, (pieces[3]["partial"], 0))

    reduce_step(0)
    halve(2)
    late["total"] = run_total(chain, low, back_weights)
    for n in range(3, len(bits) + 1):
        halve(n)
    share = jnp.concatenate([halving["keep"].reshape(-1), gain_rows.reshape(-1)])
    share_size = share.shape[0]
    late["share"] = jnp.pad(share, (0, part * D - share_size)).reshape(part, D)
    late["share_got"] = send(late["share"], INWARD)
    finish_chunk(0)
    event(3, (late["total"], at_ends(3, 0)))

    for step in range(1, len(axes)):
        reduce_step(step)
    gather_first()
    finish_chunk(1)
    for step in range(len(axes) - 1, 0, -1):
        gather_step(step)
    event(4, (late["total"], at_ends(2, 1)), at_ends(3, 0))

    share = pair_sum[3][spans[3] :] + inner[4][spans[3] :]
    share_got = send(share, OUTWARD)
    gather_step(0)
    gather_core()
    finish_chunk(2)
    event(5, (late["total"], lambda p: jnp.where(p < 2, 1 - p, 5 - p) * per), at_ends(2, 1))

    share, share_got = after(chain, share, share_got)
    share = jnp.where(middle, share, share_got)
    share = share.reshape(-1)[:share_size].reshape(-1, width)
    share = lax.all_gather(share, "dp")
    finish_chunk(3)
    gate_weight_grad, value_weight_grad, out_weight_grad = run_assemble(
        chain, core, sums["full"], sums["got"], unit
    )
    places = np.array(
        [sum((k >> n & 1) << (len(bits) - 1 - n) for n in range(len(bits))) for k in range(ways)]
    )
    order = np.argsort(places)
    gain_sums = share[:, -8:].sum(axis=0)
    share = jnp.concatenate([share[k, :-8] for k in order] + [gain_sums])
    shared = share
    norm_gain_grad = shared[-8:].reshape(-1)[:D]
    rest, shared = shared[:D], shared[D:]
    state_weight_grad = rest[:, :states]
    step_weight_grad = lax.dynamic_slice(rest, (0, states + place * head_count), (D, head_count))
    at = narrow_rows.shape[0]
    narrow = shared[:at].reshape(-1)[: 5 * states].reshape(5, states)
    mine = lax.dynamic_slice_in_dim(shared, at + place * mine_rows, mine_rows, 0).reshape(-1)
    wide_sums = mine[: 6 * channels].reshape(6, channels)
    head_sums = mine[6 * channels :][: 3 * head_count].reshape(3, head_count)
    chain.more = [state_weight_grad, step_weight_grad, norm_gain_grad, narrow, wide_sums, head_sums]
    finish_grad(6)
    return (
        late["block_out"],
        late["tokens_grad"],
        norm_gain_grad,
        gate_weight_grad,
        value_weight_grad,
        state_weight_grad,
        step_weight_grad,
        wide_sums[:4],
        wide_sums[4],
        narrow[:4],
        narrow[4],
        head_sums[0],
        head_sums[1],
        head_sums[2],
        wide_sums[5],
        out_weight_grad,
    )


def solution(mesh):
    placed = (
        P("dp", None),
        P(),
        P(None, "tensor"),
        P(None, "tensor"),
        P(),
        P(None, "tensor"),
        P(None, "tensor"),
        P("tensor"),
        P(),
        P(),
        P("tensor"),
        P("tensor"),
        P("tensor"),
        P("tensor"),
        P("tensor", None),
        P("dp", None),
        P("dp", None),
    )
    return jax.shard_map(
        on_device,
        mesh=mesh,
        in_specs=placed,
        out_specs=(
            P("dp", None),
            P(("dp", "tensor"), None),
            P(),
            P(None, "tensor"),
            P(None, "tensor"),
            P(),
            P(None, "tensor"),
            P(None, "tensor"),
            P("tensor"),
            P(),
            P(),
            P("tensor"),
            P("tensor"),
            P("tensor"),
            P("tensor"),
            P("tensor", None),
        ),
        check_vma=False,
    )
```

```python
import functools

import jax
import jax.numpy as jnp
import numpy as np
from jax import lax
from jax.experimental import pallas as pl
from jax.experimental.pallas import tpu as pltpu
from jax.sharding import PartitionSpec as P

D = 1536
INNER = 3072
EPS = 1e-05
BLOCK = 128
LANES = 128
FAR = -1e30
F32 = jnp.float32
BF16 = jnp.bfloat16
CHUNK = 256
STEP = 128
ROWS = 32
VMEM_LIMIT = 63 * 2**20
SMALL_COST = pl.CostEstimate(flops=1, bytes_accessed=1, transcendentals=0)
PIECES = (1, 1, 1, 1)
SHARE_CHUNK = 3


def matmul(left, right, dims=(1, 0)):
    return lax.dot_general(
        left, right, (((dims[0],), (dims[1],)), ((), ())), preferred_element_type=F32
    )


def exact(left, right):
    return lax.dot_general(
        left,
        right,
        (((1,), (0,)), ((), ())),
        precision=lax.Precision.HIGHEST,
        preferred_element_type=F32,
    )


def sigmoid(v):
    return 0.5 * jnp.tanh(0.5 * v) + 0.5


def softplus(v):
    return jnp.maximum(v, 0.0) + jnp.log1p(jnp.exp(-jnp.abs(v)))


def fold(x):
    return x.reshape(x.shape[0] // 8, 8, x.shape[1]).sum(axis=0)


def triangle(lower):
    row = lax.broadcasted_iota(jnp.int32, (BLOCK, BLOCK), 0)
    col = lax.broadcasted_iota(jnp.int32, (BLOCK, BLOCK), 1)
    return jnp.where(row >= col if lower else row <= col, 1.0, 0.0).astype(F32)


def group_sum(x, spread):
    high = x.astype(BF16)
    low = (x - high.astype(F32)).astype(BF16)
    return matmul(high, spread) + matmul(low, spread)


def upright(rows):
    fill = jnp.zeros((BLOCK - rows.shape[0], BLOCK), F32)
    return jnp.concatenate([rows, fill], axis=0).T


def segment_columns(seg_ref, block, blocks, ahead):
    part = lambda k: seg_ref[:, pl.ds(pl.multiple_of(k * BLOCK, BLOCK), BLOCK)].astype(F32)
    ids = part(block)
    before = jnp.where(block > 0, part(jnp.maximum(block - 1, 0)), -1.0)
    lane = lax.broadcasted_iota(jnp.int32, (1, BLOCK), 1)
    rows = [ids]
    if ahead:
        behind = jnp.where(block < blocks - 1, part(jnp.minimum(block + 1, blocks - 1)), -1.0)
    for far in range(1, 4):
        if ahead:
            moved = jnp.where(
                lane >= BLOCK - far,
                pltpu.roll(behind, BLOCK - far, 1),
                pltpu.roll(ids, BLOCK - far, 1),
            )
        else:
            moved = jnp.where(lane < far, pltpu.roll(before, far, 1), pltpu.roll(ids, far, 1))
        rows.append(jnp.where(moved == ids, 1.0, 0.0))
    rows.append(jnp.where(ids == before[:, BLOCK - 1 :], 1.0, 0.0))
    rows.append(jnp.where(ids == ids[:, BLOCK - 1 :], 1.0, 0.0))
    rows.append(jnp.zeros((2, BLOCK), F32))
    return upright(jnp.concatenate(rows, axis=0)), ids


def decay_terms(step_raw, step_bias, rate, cols, seg_row):
    steps = softplus(step_raw + step_bias)
    rates = -steps * rate
    local = exact(triangle(True), rates)
    last = local[BLOCK - 1 :]
    into = jnp.exp(jnp.where(cols[:, 4:5] > 0.5, local, FAR))
    out = jnp.exp(jnp.where(cols[:, 5:6] > 0.5, last - local, FAR))
    row = lax.broadcasted_iota(jnp.int32, (BLOCK, BLOCK), 0)
    col = lax.broadcasted_iota(jnp.int32, (BLOCK, BLOCK), 1)
    allowed = jnp.logical_and(row >= col, cols[:, 0:1] == seg_row)
    bias = jnp.where(allowed, 0.0, FAR)
    return steps, rates, local, local.T, into, out, bias


def pairwise(x, pair, half):
    return jnp.where(half, x[:, 2 * pair : 2 * pair + 1], x[:, 2 * pair + 1 : 2 * pair + 2])


def split_pair(x, half):
    zero = jnp.zeros_like(x)
    return jnp.concatenate([jnp.where(half, x, zero), jnp.where(half, zero, x)], axis=0)


def decay_of(local, local_t, bias, head):
    return jnp.exp(local[:, head : head + 1] - local_t[head : head + 1, :] + bias)


def sum_over_places(place, own, others):
    parts = len(others) + 1
    total = None
    for k in range(parts):
        value = own
        for turn in range(1, parts):
            value = jnp.where((place - k + parts) % parts == turn, others[turn - 1], value)
        total = value if total is None else total + value
    return total


GAIN_ROW, KERNEL_ROW, BIAS_ROW, GATED_ROW, SKIP_ROW = 0, 2, 6, 7, 8
STATE_KERNEL_ROW, STATE_BIAS_ROW, STEP_ROW, DECAY_ROW = 9, 13, 14, 15


def run_pack(place, *arrays):
    channels = arrays[1].shape[1]

    def kernel(place_ref, *refs):
        (norm_gain, kernel, bias, gated, skip, state_kernel, state_bias, step_bias, decay, step_w) = refs[
            :10
        ]
        table, wide, placed = refs[10:]
        table[...] = jnp.zeros_like(table)
        table[GAIN_ROW : GAIN_ROW + 1, :] = norm_gain[:channels].reshape(1, channels)
        table[GAIN_ROW + 1 : GAIN_ROW + 2, :] = norm_gain[channels:].reshape(1, channels)
        table[KERNEL_ROW : KERNEL_ROW + 4, :] = kernel[...]
        table[STATE_KERNEL_ROW : STATE_KERNEL_ROW + 4, : state_kernel.shape[1]] = state_kernel[...]
        rows = ((BIAS_ROW, bias), (GATED_ROW, gated), (SKIP_ROW, skip), (STATE_BIAS_ROW, state_bias))
        for row, ref in rows + ((STEP_ROW, step_bias), (DECAY_ROW, decay)):
            size = ref.shape[0]
            table[row : row + 1, :size] = ref[...].reshape(1, size)
        rows = step_w[...].astype(F32)
        fill = jnp.zeros((LANES - rows.shape[0], rows.shape[1]), F32)
        columns = jnp.concatenate([rows, fill], axis=0).T
        wide[...] = columns.astype(BF16)
        placed[...] = pltpu.roll(columns, place_ref[0] * rows.shape[0], 1).astype(BF16)

    return pl.pallas_call(
        kernel,
        out_shape=[
            jax.ShapeDtypeStruct((16, channels), F32),
            jax.ShapeDtypeStruct((arrays[-1].shape[1], LANES), BF16),
            jax.ShapeDtypeStruct((arrays[-1].shape[1], LANES), BF16),
        ],
        in_specs=[pl.BlockSpec(memory_space=pltpu.SMEM)]
        + [pl.BlockSpec(memory_space=pltpu.VMEM) for _ in arrays],
        cost_estimate=SMALL_COST,
        name="pack",
    )(place, *arrays)


def forward_kernel(first_piece, unused, block_base, *refs):
    tokens, cot, seg, par, gate_w, value_w, state_w, step_w, out_w = refs[:9]
    refs = refs[9:]
    if not first_piece:
        state_in, tail_in, state_tail_in = refs[:3]
        refs = refs[3:]
    refs = refs[unused:]
    (
        gate_out,
        vraw_out,
        pv_out,
        y_out,
        sraw_out,
        spv_out,
        step_out,
        saved_out,
        partial_out,
        stats_out,
        normed_out,
        state,
        tail_out,
        state_tail_out,
        vbuf,
        sbuf,
        scaled,
    ) = refs
    size = tokens.shape[0]
    channels = gate_w.shape[1]
    states = 2 * LANES

    @pl.when(pl.program_id(0) == 0)
    def _():
        if first_piece:
            state[...] = jnp.zeros_like(state)
            vbuf[:8] = jnp.zeros((8, channels), F32)
            sbuf[:8] = jnp.zeros((8, states), F32)
        else:
            state[...] = state_in[...]
            vbuf[:8] = tail_in[...]
            sbuf[:8] = state_tail_in[...]

    norm_gain = jnp.concatenate([par[GAIN_ROW : GAIN_ROW + 1], par[GAIN_ROW + 1 : GAIN_ROW + 2]], axis=1)
    scales = []
    for row in range(0, size, ROWS):
        wide = tokens[row : row + ROWS].astype(F32)
        scale = lax.rsqrt(jnp.mean(wide * wide, axis=-1, keepdims=True) + EPS)
        normed_out[row : row + ROWS] = (wide * scale * norm_gain).astype(BF16)
        scales.append(scale)
    normed = normed_out[...]
    vbuf[8:] = matmul(normed, value_w[...])
    sbuf[8:] = matmul(normed, state_w[...])
    step_out[...] = matmul(normed, step_w[...])
    gate_out[...] = matmul(normed, gate_w[...])

    def conv(buf, row, lanes, cols, kernel_row, bias_row):
        raw = buf[row + 8 : row + 8 + BLOCK, lanes]
        total = par[bias_row : bias_row + 1, lanes] + raw * par[kernel_row + 3 : kernel_row + 4, lanes]
        for back in range(1, 4):
            tap = par[kernel_row + 3 - back : kernel_row + 4 - back, lanes]
            moved = buf[row + 8 - back : row + 8 - back + BLOCK, lanes]
            total = total + moved * tap * cols[:, back : back + 1]
        return raw, total

    half = lax.broadcasted_iota(jnp.int32, (BLOCK, LANES), 1) < LANES // 2
    half_row = half[0:1]
    lane = lax.broadcasted_iota(jnp.int32, (BLOCK, LANES), 1)
    step_bias = par[STEP_ROW : STEP_ROW + 1, :LANES]
    rate = jnp.exp(par[DECAY_ROW : DECAY_ROW + 1, :LANES])
    skips = par[SKIP_ROW : SKIP_ROW + 1, :LANES]
    squares = []
    for sub in range(size // BLOCK):
        rows = slice(sub * BLOCK, (sub + 1) * BLOCK)
        row = sub * BLOCK
        block = block_base + pl.program_id(0) * (size // BLOCK) + sub
        cols, seg_row = segment_columns(seg, block, None, False)
        mixed_state = []
        for part in range(2):
            lanes = slice(part * LANES, (part + 1) * LANES)
            raw, spv = conv(sbuf, row, lanes, cols, STATE_KERNEL_ROW, STATE_BIAS_ROW)
            sraw_out[rows, lanes] = raw.astype(BF16)
            spv_out[rows, lanes] = spv
            mixed_state.append(spv * sigmoid(spv))
        b_low = mixed_state[0].astype(BF16)
        b_turned = mixed_state[0].T.astype(BF16)
        c_low = mixed_state[1].astype(BF16)
        steps, _, local, local_t, into, out, bias = decay_terms(
            step_out[rows], step_bias, rate, cols, seg_row
        )
        keep = into[BLOCK - 1 :]
        scores = matmul(c_low, b_low, (1, 1))
        square = jnp.zeros((BLOCK, LANES), F32)
        for pair in range(channels // LANES):
            lanes = slice(pair * LANES, (pair + 1) * LANES)
            raw, pv = conv(vbuf, row, lanes, cols, KERNEL_ROW, BIAS_ROW)
            vraw_out[rows, lanes] = raw.astype(BF16)
            pv_out[rows, lanes] = pv
            values = pv * sigmoid(pv)
            old = state[:, lanes]
            old_low = old.astype(BF16)
            saved_out[sub, :, lanes] = old_low
            u = values * pairwise(steps, pair, half)
            weights = [
                (scores * decay_of(local, local_t, bias, 2 * pair + k)).astype(BF16)
                for k in range(2)
            ]
            inner = matmul(jnp.concatenate(weights, axis=1), split_pair(u.astype(BF16), half))
            y_ssm = inner + matmul(c_low, old_low) * pairwise(into, pair, half)
            y_out[rows, lanes] = y_ssm
            leaving = (u * pairwise(out, pair, half)).astype(BF16)
            state[:, lanes] = old * pairwise(keep, pair, half_row) + matmul(b_turned, leaving)
            gate = gate_out[rows, lanes]
            gated = (y_ssm + pairwise(skips, pair, half_row) * values) * (gate * sigmoid(gate))
            square = square + gated * gated
            scaled[rows, lanes] = (gated * par[GATED_ROW : GATED_ROW + 1, lanes]).astype(BF16)
        squares.append(jnp.sum(square, axis=-1, keepdims=True))
    vbuf[:8] = vbuf[size:]
    sbuf[:8] = sbuf[size:]
    tail_out[...] = vbuf[:8]
    state_tail_out[...] = sbuf[:8]
    partial_out[...] = matmul(scaled[...], out_w[...])
    products = [
        jnp.sum(cot[row : row + ROWS].astype(F32) * partial_out[row : row + ROWS], axis=-1, keepdims=True)
        for row in range(0, size, ROWS)
    ]
    per = BLOCK // ROWS
    for sub in range(size // BLOCK):
        product = jnp.concatenate(products[sub * per : (sub + 1) * per], axis=0)
        scale = jnp.concatenate(scales[sub * per : (sub + 1) * per], axis=0)
        table = jnp.where(
            lane == 0, squares[sub], jnp.where(lane == 1, product, jnp.where(lane == 2, scale, 0.0))
        )
        stats_out[:, sub * BLOCK : (sub + 1) * BLOCK] = table.T[:8]


def backward_kernel(first_piece, unused, block_base, blocks, *refs):
    (
        place_ref,
        og_ref,
        gate_ref,
        vraw_ref,
        pv_ref,
        y_ref,
        sraw_ref,
        spv_ref,
        step_ref,
        own_stats,
        stats_1,
        stats_2,
        stats_3,
        saved_ref,
        seg,
        par,
    ) = refs[:16]
    refs = refs[16:]
    if not first_piece:
        carried_in = refs[:6]
        refs = refs[6:]
    refs = refs[unused:]
    (
        low_out,
        mixed_out,
        state_out,
        tail_out,
        state_tail_out,
        wide_acc,
        narrow_acc,
        heads_acc,
    ) = refs
    channels = gate_ref.shape[1]
    place = place_ref[0]

    @pl.when(pl.program_id(0) == 0)
    def _():
        outs = (state_out, tail_out, state_tail_out, wide_acc, narrow_acc, heads_acc)
        for k, ref in enumerate(outs):
            ref[...] = jnp.zeros_like(ref) if first_piece else carried_in[k][...]

    block = block_base + pl.num_programs(0) - 1 - pl.program_id(0)
    cols, seg_row = segment_columns(seg, block, blocks, True)
    stats = sum_over_places(place, own_stats[...], [stats_1[...], stats_2[...], stats_3[...]])
    stats = upright(stats)
    strength = lax.rsqrt(stats[:, 0:1] / INNER + EPS)
    pull = strength * strength * strength * stats[:, 1:2] / INNER

    half = lax.broadcasted_iota(jnp.int32, (BLOCK, LANES), 1) < LANES // 2
    half_row = half[0:1]
    spv = [spv_ref[:, :LANES], spv_ref[:, LANES:]]
    spv_sig = [sigmoid(v) for v in spv]
    b_part = spv[0] * spv_sig[0]
    c_part = spv[1] * spv_sig[1]
    b_low = b_part.astype(BF16)
    c_low = c_part.astype(BF16)
    c_turned = c_part.T.astype(BF16)
    step_raw = step_ref[...]
    step_bias = par[STEP_ROW : STEP_ROW + 1, :LANES]
    rate = jnp.exp(par[DECAY_ROW : DECAY_ROW + 1, :LANES])
    skips = par[SKIP_ROW : SKIP_ROW + 1, :LANES]
    steps, rates, local, local_t, into, out, bias = decay_terms(
        step_raw, step_bias, rate, cols, seg_row
    )
    keep = into[BLOCK - 1 :]
    scores = matmul(c_low, b_low, (1, 1))

    def conv_back(pre_grad, raw, lanes, after, kernel_row, acc):
        ext = jnp.concatenate([pre_grad, after[:, lanes]], axis=0)
        after[:, lanes] = pre_grad[:8]
        total = pre_grad * par[kernel_row + 3 : kernel_row + 4, lanes]
        acc[24:32, lanes] += fold(raw * pre_grad)
        acc[32:40, lanes] += fold(pre_grad)
        for ahead in range(1, 4):
            moved = pltpu.roll(ext, BLOCK + 8 - ahead, 0)[:BLOCK]
            term = moved * cols[:, ahead : ahead + 1]
            total = total + term * par[kernel_row + 3 - ahead : kernel_row + 4 - ahead, lanes]
            acc[8 * (3 - ahead) : 8 * (4 - ahead), lanes] += fold(raw * term)
        return total

    score_grad = jnp.zeros((BLOCK, BLOCK), F32)
    b_grad = jnp.zeros((BLOCK, LANES), F32)
    c_grad = jnp.zeros((BLOCK, LANES), F32)
    spread_dl = jnp.zeros((BLOCK, LANES), F32)
    spread_ds = jnp.zeros((BLOCK, LANES), F32)
    spread_end = jnp.zeros((8, LANES), F32)
    for pair in range(channels // LANES):
        lanes = slice(pair * LANES, (pair + 1) * LANES)
        spread = (
            lax.broadcasted_iota(jnp.int32, (LANES, LANES), 0) // (LANES // 2) + 2 * pair
            == lax.broadcasted_iota(jnp.int32, (LANES, LANES), 1)
        ).astype(BF16)
        gain = par[GATED_ROW : GATED_ROW + 1, lanes]
        skip = pairwise(skips, pair, half_row)
        gate = gate_ref[:, lanes]
        gate_sig = sigmoid(gate)
        gate_silu = gate * gate_sig
        pv = pv_ref[:, lanes]
        pv_sig = sigmoid(pv)
        values = pv * pv_sig
        og = og_ref[:, lanes]
        y_ssm = y_ref[:, lanes]
        y = y_ssm + skip * values
        gated = y * gate_silu
        strong = gated * strength
        mixed_out[:, lanes] = (strong * gain).astype(BF16)
        gated_grad = gain * strength * og - gated * pull
        low_out[:, lanes] = (
            gated_grad * y * (gate_sig * (1.0 + gate * (1.0 - gate_sig)))
        ).astype(BF16)
        grad = gated_grad * gate_silu
        wide_acc[40:48, lanes] += fold(og * strong)
        wide_acc[48:56, lanes] += fold(grad * values)

        state_grad = state_out[:, lanes]
        state_grad_low = state_grad.astype(BF16)
        old_low = saved_ref[0, :, lanes]
        pair_steps = pairwise(steps, pair, half)
        pair_out = pairwise(out, pair, half)
        u = values * pair_steps
        u_low = u.astype(BF16)
        g_low = grad.astype(BF16)
        g_split = split_pair(g_low, half)
        decays = [decay_of(local, local_t, bias, 2 * pair + k) for k in range(2)]
        weights = jnp.concatenate([(scores * d).astype(BF16) for d in decays], axis=0)
        weight_grad = matmul(g_split, u_low, (1, 1))
        score_grad = score_grad + weight_grad[:BLOCK] * decays[0] + weight_grad[BLOCK:] * decays[1]
        u_grad_out = matmul(b_low, state_grad_low) * pair_out
        u_grad = matmul(weights, g_split, (0, 0)) + u_grad_out
        u_near = u_low.astype(F32)
        spread_dl = spread_dl + group_sum(g_low.astype(F32) * y_ssm - u_near * u_grad, spread)
        spread_ds = spread_ds + group_sum(values * u_grad, spread)
        keep_row = pairwise(keep, pair, half_row)
        spread_end = spread_end + group_sum(
            fold(u_near * u_grad_out) + fold(state_grad * old_low.astype(F32)) * keep_row, spread
        )
        entering = (grad * pairwise(into, pair, half)).astype(BF16)
        leaving = (u * pair_out).astype(BF16)
        c_grad = c_grad + matmul(entering, old_low, (1, 1))
        b_grad = b_grad + matmul(leaving, state_grad_low, (1, 1))
        state_out[:, lanes] = state_grad * keep_row + matmul(c_turned, entering)
        pre_grad = (pair_steps * u_grad + skip * grad) * (pv_sig * (1.0 + pv * (1.0 - pv_sig)))
        raw_grad = conv_back(
            pre_grad, vraw_ref[:, lanes].astype(F32), lanes, tail_out, KERNEL_ROW, wide_acc
        )
        low_out[:, channels + pair * LANES : channels + (pair + 1) * LANES] = raw_grad.astype(BF16)
    score_low = score_grad.astype(BF16)
    c_grad = c_grad + matmul(score_low, b_low)
    b_grad = b_grad + matmul(score_low, c_low, (0, 0))
    rate_grad = exact(triangle(False), spread_dl) + jnp.sum(spread_end, axis=0, keepdims=True)
    step_grad = (spread_ds - rate * rate_grad) * sigmoid(step_raw + step_bias)
    heads_acc[0:8] += fold(step_grad)
    heads_acc[8:16] += fold(rates * rate_grad)
    for part, grad in enumerate((b_grad, c_grad)):
        lanes = slice(part * LANES, (part + 1) * LANES)
        pre_grad = grad * (spv_sig[part] * (1.0 + spv[part] * (1.0 - spv_sig[part])))
        raw_grad = conv_back(
            pre_grad, sraw_ref[:, lanes].astype(F32), lanes, state_tail_out, STATE_KERNEL_ROW, narrow_acc
        )
        at = 2 * channels + part * LANES
        low_out[:, at : at + LANES] = raw_grad.astype(BF16)
    heads_here = channels // (LANES // 2)
    low_out[:, 2 * channels + 2 * LANES :] = pltpu.roll(step_grad, place * heads_here, 1).astype(BF16)


def out_grad_kernel(unused, cot, out_w, *refs):
    og, token = refs[unused : unused + 2]
    og[...] = matmul(cot[...], out_w[...], (1, 1))
    token[...] = jnp.zeros((8, LANES), F32)


def run_out_grad(chain, cot, out_w, passes):
    length, channels = cot.shape[0], out_w.shape[0]
    deps = chain.deps()
    results = pl.pallas_call(
        functools.partial(out_grad_kernel, len(deps) + len(passes)),
        grid=(length // CHUNK,),
        in_specs=[pl.BlockSpec((CHUNK, D), lambda i: (i, 0)), whole(out_w.shape)]
        + [ANYWHERE for _ in deps + passes],
        out_specs=[pl.BlockSpec((CHUNK, channels), lambda i: (i, 0)), whole((8, LANES))]
        + [ANYWHERE for _ in passes],
        out_shape=[
            jax.ShapeDtypeStruct((length, channels), F32),
            jax.ShapeDtypeStruct((8, LANES), F32),
        ]
        + [jax.ShapeDtypeStruct(p.shape, p.dtype) for p in passes],
        input_output_aliases={2 + len(deps) + k: 2 + k for k in range(len(passes))},
        compiler_params=pltpu.CompilerParams(vmem_limit_bytes=VMEM_LIMIT),
        cost_estimate=SMALL_COST,
        name="out_grad",
    )(cot, out_w, *deps, *passes)
    chain.last = results[1]
    return results[0], results[2:]


def run_matmul(chain, body, ins, outs, count, scratch=(), name=None):
    deps = chain.deps()
    arrays = [a for a, _, _ in ins]

    def kernel(*refs):
        body(*refs[: len(arrays)], *refs[len(arrays) + len(deps) :])
        refs[len(arrays) + len(deps) + len(outs)][...] = jnp.zeros((8, LANES), F32)

    results = pl.pallas_call(
        kernel,
        grid=(count,),
        in_specs=[whole(a.shape) if m is None else pl.BlockSpec(b, m) for a, b, m in ins]
        + [ANYWHERE for _ in deps],
        out_specs=[pl.BlockSpec(b, m) for _, b, m in outs] + [whole((8, LANES))],
        out_shape=[jax.ShapeDtypeStruct(s, F32) for s, _, _ in outs]
        + [jax.ShapeDtypeStruct((8, LANES), F32)],
        scratch_shapes=list(scratch),
        compiler_params=pltpu.CompilerParams(vmem_limit_bytes=VMEM_LIMIT),
        cost_estimate=SMALL_COST,
        name=name,
    )(*arrays, *deps)
    chain.last = results[-1]
    return results[:-1]


def gain_row(value, count):
    out = []
    for k in range(count // BLOCK):
        column = jnp.sum(value[k * BLOCK : (k + 1) * BLOCK], axis=-1, keepdims=True)
        out.append(jnp.broadcast_to(column, (BLOCK, BLOCK)).T[:8])
    return jnp.concatenate(out, axis=1)


def run_rest_grad(chain, normed, low, small_rows, weights):
    width = small_rows.shape[1]
    count = D // CHUNK
    states = weights[0].shape[1]

    def body(left, right, extra, state_w, step_w, out, gain, token):
        @pl.when(pl.program_id(0) < count)
        def _():
            value = matmul(left[...], right[...], (0, 0))
            out[...] = value
            both = jnp.concatenate([state_w[...], step_w[...]], axis=1).astype(F32)
            gain[...] = gain_row(value * both, CHUNK)

        @pl.when(pl.program_id(0) == count)
        def _():
            out[...] = extra[...]

    length, total = low.shape
    held = lambda i: jnp.minimum(i, count - 1)
    tile = lambda a: (a, (CHUNK, a.shape[1]), lambda i: (held(i), 0))
    return run_matmul(
        chain,
        body,
        [
            (normed, (length, CHUNK), lambda i: (0, held(i))),
            (low, (length, width), lambda i: (0, total // width - 1)),
            (small_rows, None, None),
            *[tile(w) for w in weights],
        ],
        [
            ((D + CHUNK, width), (CHUNK, width), lambda i: (i, 0)),
            ((8, D), (8, CHUNK), lambda i: (0, held(i))),
        ],
        count + 1,
        name="rest_grad",
    )


def run_weight_grads(chain, core, normed, low, cot, mixed, weights, gains, unit):
    length = normed.shape[0]
    channels = mixed.shape[1]
    tile = D // 4
    deps = chain.deps()

    def which(i, p):
        return jnp.where(i < 2, 1 - p[0], p[0]) * 2 + i % 2

    def kernel(place, left, right, cots, mix, gate_w, value_w, gain_in, *refs):
        outs, gain, token = refs[len(deps) : len(deps) + 4], refs[-2], refs[-1]
        i = pl.program_id(0)

        @pl.when(i == 0)
        def _():
            gain[...] = gain_in[...]
            token[...] = jnp.zeros((8, LANES), F32)

        gate = matmul(left[...], right[:, :channels], (0, 0))
        value = matmul(left[...], right[:, channels:], (0, 0))
        out = matmul(cots[...], mix[...], (0, 0))
        at = pl.ds(pl.multiple_of(which(i, place) * tile, LANES), tile)
        products = gate * gate_w[...].astype(F32) + value * value_w[...].astype(F32)
        gain[:, at] = gain[:, at] + gain_row(products, tile)
        for k in range(4):

            @pl.when(i == k)
            def _(k=k):
                for n in range(tile // unit):
                    rows = slice(n * unit, (n + 1) * unit)
                    for m, part in enumerate((gate, value, out)):
                        first = (3 * n + m) * unit
                        outs[k][first : first + unit, :] = part[rows]

    lanes = lambda i, p: (0, which(i, p))
    weight_spec = pl.BlockSpec((tile, channels), lambda i, p: (which(i, p), 0))
    results = pl.pallas_call(
        kernel,
        grid_spec=pltpu.PrefetchScalarGridSpec(
            num_scalar_prefetch=1,
            grid=(4,),
            in_specs=[
                pl.BlockSpec((length, tile), lanes),
                pl.BlockSpec((length, 2 * channels), lambda i, p: (0, 0)),
                pl.BlockSpec((length, tile), lanes),
                whole(mixed.shape),
                weight_spec,
                weight_spec,
                whole(gains.shape),
            ]
            + [ANYWHERE for _ in deps],
            out_specs=[whole((3 * tile, channels))] * 4 + [whole(gains.shape), whole((8, LANES))],
        ),
        out_shape=[jax.ShapeDtypeStruct((3 * tile, channels), F32)] * 4
        + [jax.ShapeDtypeStruct(gains.shape, F32), jax.ShapeDtypeStruct((8, LANES), F32)],
        compiler_params=pltpu.CompilerParams(vmem_limit_bytes=VMEM_LIMIT),
        cost_estimate=SMALL_COST,
        name="weight_grads",
    )(core, normed, low, cot, mixed, *weights, gains, *deps)
    chain.last = results[-1]
    return results[:4], results[4]


def run_assemble(chain, core, own, got, unit):
    rows, channels = own[0].shape
    tile = rows // 3
    deps = chain.deps()

    def kernel(place, own_a, own_b, got_a, got_b, *refs):
        gate, value, out, token = refs[len(deps) :]
        i = pl.program_id(0)
        token[...] = jnp.zeros((8, LANES), F32)
        for n, (mine, other) in enumerate(((own_a, got_a), (own_b, got_b))):

            @pl.when(i % 2 == n)
            def _(mine=mine, other=other):
                use_own = i // 2 == place[0]
                pieces = []
                for k in range(rows // unit):
                    at = slice(k * unit, (k + 1) * unit)
                    pieces.append(jnp.where(use_own, mine[at, :], other[at, :]))
                gate[...] = jnp.concatenate(pieces[0::3], axis=0)
                value[...] = jnp.concatenate(pieces[1::3], axis=0)
                out[...] = jnp.concatenate(pieces[2::3], axis=0).T

    row = pl.BlockSpec((tile, channels), lambda i, p: (i, 0))
    gate, value, out, chain.last = pl.pallas_call(
        kernel,
        grid_spec=pltpu.PrefetchScalarGridSpec(
            num_scalar_prefetch=1,
            grid=(4,),
            in_specs=[whole(own[0].shape)] * 4 + [ANYWHERE for _ in deps],
            out_specs=[
                row,
                row,
                pl.BlockSpec((channels, tile), lambda i, p: (0, i)),
                whole((8, LANES)),
            ],
        ),
        out_shape=[
            jax.ShapeDtypeStruct((D, channels), F32),
            jax.ShapeDtypeStruct((D, channels), F32),
            jax.ShapeDtypeStruct((channels, D), F32),
            jax.ShapeDtypeStruct((8, LANES), F32),
        ],
        compiler_params=pltpu.CompilerParams(vmem_limit_bytes=VMEM_LIMIT),
        cost_estimate=SMALL_COST,
        name="assemble",
    )(core, *own, *got, *deps)
    return gate, value, out


def run_total(chain, low, weights):
    length, width = low.shape

    def body(left, gate_w, value_w, state_w, step_w, out, token, joined):
        @pl.when(pl.program_id(0) == 0)
        def _():
            at = 0
            for ref in (gate_w, value_w, state_w, step_w):
                joined[:, at : at + ref.shape[1]] = ref[...]
                at += ref.shape[1]

        out[...] = matmul(left[...], joined[...], (1, 1))

    (out,) = run_matmul(
        chain,
        body,
        [(low, (CHUNK, width), lambda i: (i, 0))] + [(w, None, None) for w in weights],
        [((length, D), (CHUNK, D), lambda i: (i, 0))],
        length // CHUNK,
        scratch=[pltpu.VMEM((D, width), BF16)],
        name="normed_grad",
    )
    return out


def whole(shape):
    return pl.BlockSpec(shape, lambda i, *_: (0,) * len(shape))


ANYWHERE = pl.BlockSpec(memory_space=pl.ANY)


def run_forward(start, count, tokens, cot, seg, small, carried, kept, deps):
    channels = small["gate_w"].shape[1]
    states = 2 * LANES
    size = CHUNK
    length = count * size
    first = start // size
    per = size // BLOCK
    full = tokens.shape[0]

    def row_in(width):
        return pl.BlockSpec((size, width), lambda i: (first + i, 0))

    def row_out(width):
        return pl.BlockSpec((size, width), lambda i: (i, 0))

    constant = [small[n] for n in ("par", "gate_w", "value_w", "state_w", "step_w", "out_w")]
    carry_shapes = [(LANES, channels), (8, channels), (8, states)]
    widths = (
        (channels, F32),
        (channels, BF16),
        (channels, F32),
        (channels, F32),
        (states, BF16),
        (states, F32),
        (LANES, F32),
    )
    inputs = [tokens, cot, seg, *constant, *carried, *deps, *kept]
    outs = pl.pallas_call(
        functools.partial(forward_kernel, not carried, len(deps) + len(kept), start // BLOCK),
        grid=(count,),
        in_specs=[row_in(D), row_in(D), whole(seg.shape)]
        + [whole(c.shape) for c in constant]
        + [whole(c.shape) for c in carried]
        + [ANYWHERE for _ in deps + kept],
        out_specs=[row_out(w) for w, _ in widths]
        + [pl.BlockSpec((per, LANES, channels), lambda i: (i, 0, 0))]
        + [row_out(D)]
        + [pl.BlockSpec((8, size), lambda i: (0, first + i))]
        + [row_in(D)]
        + [whole(c) for c in carry_shapes],
        out_shape=[jax.ShapeDtypeStruct((length, w), k) for w, k in widths]
        + [jax.ShapeDtypeStruct((length // BLOCK, LANES, channels), BF16)]
        + [jax.ShapeDtypeStruct((length, D), F32)]
        + [jax.ShapeDtypeStruct((8, full), F32)]
        + [jax.ShapeDtypeStruct((full, D), BF16)]
        + [jax.ShapeDtypeStruct(c, F32) for c in carry_shapes],
        scratch_shapes=[
            pltpu.VMEM((size + 8, channels), F32),
            pltpu.VMEM((size + 8, states), F32),
            pltpu.VMEM((size, channels), BF16),
        ],
        input_output_aliases={len(inputs) - len(kept) + k: 9 + k for k in range(len(kept))},
        compiler_params=pltpu.CompilerParams(vmem_limit_bytes=VMEM_LIMIT),
        cost_estimate=SMALL_COST,
        name="forward_piece",
    )(*inputs)
    outs = list(outs)
    names = ("gate", "vraw", "pv", "y", "sraw", "spv", "step", "saved", "partial")
    return dict(zip(names, outs[:9])), outs[9:11], outs[11:]


def run_backward(start, piece, og, stats, place, seg, small, carried, low, mixed, deps):
    channels = small["gate_w"].shape[1]
    length = piece["gate"].shape[0]
    full = og.shape[0]
    count = length // BLOCK
    first = start // BLOCK
    flip = lambda i: count - 1 - i

    def row(width):
        return pl.BlockSpec((BLOCK, width), lambda i, *_: (flip(i), 0))

    def shared(width):
        return pl.BlockSpec((BLOCK, width), lambda i, *_: (first + flip(i), 0))

    names = ("gate", "vraw", "pv", "y", "sraw", "spv", "step")
    ins = [piece[n] for n in names]
    low_width = 2 * channels + 3 * LANES
    kept = [] if low is None else [low, mixed]
    carry_shapes = [
        (LANES, channels),
        (8, channels),
        (8, 2 * LANES),
        (56, channels),
        (40, 2 * LANES),
        (16, LANES),
    ]
    inputs = [og, *ins, *stats, piece["saved"], seg, small["par"], *carried, *deps, *kept]
    outs = pl.pallas_call(
        functools.partial(
            backward_kernel, not carried, len(deps) + len(kept), first, full // BLOCK
        ),
        grid_spec=pltpu.PrefetchScalarGridSpec(
            num_scalar_prefetch=1,
            grid=(count,),
            in_specs=[shared(channels)]
            + [row(a.shape[1]) for a in ins]
            + [pl.BlockSpec((8, BLOCK), lambda i, *_: (0, first + flip(i))) for _ in stats]
            + [pl.BlockSpec((1, LANES, channels), lambda i, *_: (flip(i), 0, 0))]
            + [whole(seg.shape), whole(small["par"].shape)]
            + [whole(c.shape) for c in carried]
            + [ANYWHERE for _ in deps + kept],
            out_specs=[shared(low_width), shared(channels)] + [whole(c) for c in carry_shapes],
        ),
        out_shape=[
            jax.ShapeDtypeStruct((full, low_width), BF16),
            jax.ShapeDtypeStruct((full, channels), BF16),
        ]
        + [jax.ShapeDtypeStruct(c, F32) for c in carry_shapes],
        compiler_params=pltpu.CompilerParams(vmem_limit_bytes=VMEM_LIMIT),
        cost_estimate=SMALL_COST,
        input_output_aliases={1 + len(inputs) - 2 + k: k for k in range(len(kept))},
        name="backward_piece",
    )(place, *inputs)
    return outs[0], outs[1], list(outs[2:])


class Chain:
    def __init__(self):
        self.last = None
        self.more = []

    def deps(self):
        found = ([] if self.last is None else [self.last]) + self.more
        self.more = []
        return found


def rowwise(
    chain, place, body, ins, outs, rows, passes=(), step=0, whole_place=False, name=None
):
    step = step or STEP
    steps = rows // step

    def spec(width, first, most=steps, where=None):
        if where is not None:
            base = first if callable(first) else lambda p: first
            return pl.BlockSpec(
                (step, width),
                lambda i, p: (
                    jnp.where(where(p[0]), base(p[0]) + jnp.minimum(i, most - 1), 0),
                    0,
                ),
            )
        if callable(first):
            return pl.BlockSpec(
                (step, width),
                lambda i, p: (
                    jnp.maximum(first(p if whole_place else p[0]) + jnp.minimum(i, most - 1), 0),
                    0,
                ),
            )
        return pl.BlockSpec((step, width), lambda i, p: (first + jnp.minimum(i, most - 1), 0))

    def lying(height, first):
        if callable(first):
            return pl.BlockSpec((height, STEP), lambda i, p: (0, first(p[0]) + i))
        return pl.BlockSpec((height, STEP), lambda i, p: (0, first + i))

    def spec_of(array, first, across=False, most=steps, where=None):
        if first is None:
            return fixed(array.shape)
        return lying(array.shape[0], first) if across else spec(array.shape[1], first, most, where)

    def fixed(shape):
        return pl.BlockSpec(shape, lambda i, p: (0,) * len(shape))

    anywhere = pl.BlockSpec(memory_space=pl.ANY)
    arrays = [entry[0] for entry in ins]
    in_specs = [spec_of(*entry) for entry in ins]
    kept = [(k, o[4]) for k, o in enumerate(outs) if o[4] is not None]
    deps = chain.deps()
    inputs = [*arrays, *[a for _, a in kept], *passes, *deps]
    aliases = {1 + len(arrays) + n: k for n, (k, _) in enumerate(kept)}
    for n in range(len(passes)):
        aliases[1 + len(arrays) + len(kept) + n] = len(outs) + n

    def kernel(place_ref, *refs):
        results = refs[len(inputs) :]
        values = body(place_ref if whole_place else place_ref[0], *refs[: len(arrays)])
        for ref, value in zip(results[: len(outs)], values):
            ref[...] = value
        results[-1][...] = jnp.zeros((8, LANES), F32)

    results = pl.pallas_call(
        kernel,
        grid_spec=pltpu.PrefetchScalarGridSpec(
            num_scalar_prefetch=1,
            grid=(steps,),
            in_specs=in_specs + [anywhere] * (len(inputs) - len(arrays)),
            out_specs=[spec(o[1], o[3], *o[5:]) for o in outs]
            + [anywhere] * len(passes)
            + [fixed((8, LANES))],
        ),
        out_shape=[jax.ShapeDtypeStruct((o[0], o[1]), o[2]) for o in outs]
        + [jax.ShapeDtypeStruct(p.shape, p.dtype) for p in passes]
        + [jax.ShapeDtypeStruct((8, LANES), F32)],
        input_output_aliases=aliases,
        compiler_params=pltpu.CompilerParams(vmem_limit_bytes=VMEM_LIMIT),
        cost_estimate=SMALL_COST,
        name=name,
    )(place, *inputs)
    chain.last = results[-1]
    return list(results[:-1])


def after(chain, *arrays):
    def kernel(*refs):
        refs[-1][...] = jnp.zeros((8, LANES), F32)

    anywhere = pl.BlockSpec(memory_space=pl.ANY)
    deps = chain.deps()
    results = pl.pallas_call(
        kernel,
        in_specs=[anywhere] * (len(arrays) + len(deps)),
        out_specs=[anywhere] * len(arrays) + [pl.BlockSpec(memory_space=pltpu.VMEM)],
        out_shape=[jax.ShapeDtypeStruct(a.shape, a.dtype) for a in arrays]
        + [jax.ShapeDtypeStruct((8, LANES), F32)],
        input_output_aliases={k: k for k in range(len(arrays))},
        cost_estimate=SMALL_COST,
        name="in_order",
    )(*arrays, *deps)
    chain.last = results[-1]
    return list(results[:-1])


INWARD = ((0, 1), (3, 2))
ACROSS = ((1, 2), (2, 1))
OUTWARD = ((1, 0), (2, 3))


def on_device(
    tokens,
    norm_gain,
    gate_weight,
    value_weight,
    state_weight,
    step_weight,
    value_kernel,
    value_bias,
    state_kernel,
    state_bias,
    step_bias,
    decay_log,
    skip_scale,
    gated_gain,
    out_weight,
    segment_ids,
    out_cotangent,
):
    parts = lax.axis_size("tensor")
    place = lax.axis_index("tensor")
    middle = jnp.logical_and(place > 0, place < parts - 1)
    length = tokens.shape[0]
    channels = gate_weight.shape[1]
    head_count = step_bias.shape[0]
    rows = length // parts
    states = 2 * LANES
    where = place.astype(jnp.int32)[None]
    par, step_wide, step_place = run_pack(
        where,
        norm_gain,
        value_kernel,
        value_bias,
        gated_gain,
        skip_scale,
        state_kernel,
        state_bias,
        step_bias,
        decay_log,
        step_weight.T,
    )
    small = {
        "gate_w": gate_weight,
        "value_w": value_weight,
        "state_w": state_weight,
        "step_w": step_wide,
        "out_w": out_weight,
        "par": par,
    }
    chain = Chain()
    send = lambda x, pairs: lax.ppermute(x, "tensor", pairs)
    run = functools.partial(rowwise, chain, where)
    steps = lambda n: n // STEP

    spans = [p * length // sum(PIECES) for p in PIECES]
    firsts = [sum(spans[:k]) for k in range(len(spans))]
    pieces = []
    carried = []
    kept = []
    late = {}
    part = 64
    count = len(spans)
    outer, inner, outer_sent, pair_sum = {}, {}, {}, {}

    def forward():
        nonlocal carried, kept
        k = len(pieces)
        outs, kept, carried = run_forward(
            firsts[k],
            spans[k] // CHUNK,
            tokens,
            out_cotangent,
            segment_ids,
            small,
            carried,
            kept,
            chain.deps(),
        )
        pieces.append(outs)
        chain.last = carried[2]

    part = 64

    def send_outer(n, message, both=True):
        outer_sent[n] = message
        outer[n] = send(message, INWARD + OUTWARD if both else INWARD)

    is_middle = lambda p: jnp.logical_and(p > 0, p < parts - 1)
    per = steps(rows)
    at_ends = lambda low_end, high_end: lambda p: jnp.where(p < 2, low_end, high_end) * per

    def event(n, following=None, middle_segment=None):
        chunk = n < count
        extra = [(late["share"], None), (late["share_got"], None)] if n == SHARE_CHUNK else []
        step = part if extra else STEP
        blocks = spans[0] // step
        size = spans[0] + (part if extra else 0)
        is_end = lambda p: jnp.logical_not(is_middle(p))
        if chunk:
            mine = (pieces[n]["partial"], 0, False, blocks, is_middle)
        else:
            mine = (late["total"], middle_segment, False, blocks, is_middle)
        ins = [mine, (outer[n], 0, False, blocks, is_middle)]
        outs = [(size, D, F32, 0, None, blocks + (1 if extra else 0), is_middle)]
        if n > 0:
            array, first = following
            if callable(first) and extra:
                first = functools.partial(lambda p, f: f(p) * (STEP // part), f=first)
            from_middle = (inner[n], 0, False, blocks, is_middle)
            if n <= count:
                ins += [(pair_sum[n - 1], 0, False, blocks, is_middle), from_middle]
                ins += [(array, first, False, blocks, is_end)]
            else:
                ins += [(array, first, False, blocks), from_middle]
            outs.append((spans[0], D, F32, 0, None, blocks))

        def body(p, a, b, *others):
            value = a[...] + b[...]
            if extra:
                x, y = others[-2:]
                value = jnp.where(pl.program_id(0) == blocks, x[...] + y[...], value)
            results = [value]
            if n > 0:
                message = others[0][...] + others[1][...]
                if n <= count:
                    message = jnp.where(is_middle(p), message, others[2][...])
                results.append(message)
            return results

        results = run(body, ins + extra, outs, size, step=step, name="event")
        pair_sum[n] = results[0]
        inner[n + 1] = send(results[0], ACROSS)
        if n > 0:
            send_outer(n + 1, results[1])
        else:
            send_outer(1, following[0], False)

    def finish_chunk(k):
        def body(p, own, got, token, *stats):
            inside = jnp.logical_and(p > 0, p < parts - 1)
            total = jnp.where(inside, own[...], got[...])
            table = upright(sum_over_places(p, stats[0][...], [x[...] for x in stats[1:]]))
            strength = lax.rsqrt(table[:, 0:1] / INNER + EPS)
            return [(token[...].astype(F32) + total * strength).astype(BF16)]

        first = steps(firsts[k])
        (late["block_out"],) = run(
            body,
            [(outer_sent[k + 2], 0), (outer[k + 2], 0), (tokens, first)]
            + [(x, first, True) for x in late["stats"]],
            [(length, D, BF16, first, late.get("block_out"))],
            spans[k],
            name="finish_chunk",
        )

    def finish_grad(n):
        def body(p, mine, side_got, middle_got, token, scale, cot, gain):
            token = token[...].astype(F32)
            scale = upright(scale[...])[:, 2:3]
            weighted = (mine[...] + side_got[...] + middle_got[...]) * gain[...]
            pull = jnp.sum(weighted * token, axis=-1, keepdims=True) / D
            return [cot[...].astype(F32) + scale * weighted - token * scale * scale * scale * pull]

        mine = lambda p: p * per
        (late["tokens_grad"],) = run(
            body,
            [
                (late["total"], mine),
                (outer[n], 0),
                (inner[n], 0),
                (tokens, mine),
                (late["own_stats"], mine, True),
                (out_cotangent, mine),
                (norm_gain[None], None),
            ],
            [(rows, D, F32, 0, None)],
            rows,
            name="finish_grad",
        )

    low = mixed = None
    back = []

    def backward(k):
        nonlocal low, mixed, back
        low, mixed, back = run_backward(
            firsts[k],
            pieces[k],
            late["og"],
            late["stats"],
            where,
            segment_ids,
            small,
            back,
            low,
            mixed,
            chain.deps(),
        )
        chain.last = back[2]

    def exchange_stats():
        own = late["own_stats"] = kept[0]
        late["stats"] = [own] + [
            send(own, [(k, (k + turn) % parts) for k in range(parts)]) for turn in range(1, parts)
        ]
        chain.more = late["stats"][1:]

    forward()
    send_outer(0, pieces[0]["partial"], False)
    forward()
    forward()
    late["og"], _ = run_out_grad(chain, out_cotangent, out_weight, [])
    forward()
    exchange_stats()
    event(0, (pieces[1]["partial"], 0))
    backward(3)
    backward(2)
    backward(1)
    backward(0)
    event(1, (pieces[2]["partial"], 0))

    normed = kept[1]
    wide_acc, narrow_acc, heads_acc = back[3:]
    back_weights = [gate_weight, value_weight, state_weight, step_place]
    width = 3 * LANES
    fit = lambda x: jnp.pad(x.reshape(-1), (0, -x.size % width)).reshape(-1, width)
    narrow = narrow_acc.reshape(5, 8, states).sum(axis=1)
    wide_sums = wide_acc.reshape(7, 8, channels).sum(axis=1)
    head_sums = heads_acc.reshape(2, 8, LANES).sum(axis=1)[:, :head_count]
    skip_grad = wide_sums[6].reshape(head_count, channels // head_count).sum(axis=1)
    mine = jnp.concatenate([fit(wide_sums[:6]), fit(jnp.concatenate([head_sums, skip_grad[None]]))])
    mine_rows = mine.shape[0]
    slots = jnp.where(
        lax.broadcasted_iota(jnp.int32, (parts, 1, 1), 0) == place, mine[None], 0.0
    ).reshape(-1, width)
    narrow_rows = fit(narrow)
    filler = jnp.zeros((CHUNK - narrow_rows.shape[0] - slots.shape[0], width), F32)
    shared, gains = run_rest_grad(
        chain, normed, low, jnp.concatenate([narrow_rows, slots, filler]), back_weights[2:]
    )

    ways = lax.axis_size("dp")
    own_dp = lax.axis_index("dp")
    bits = []
    while 2 ** len(bits) < ways:
        bits.append(2 ** len(bits))
    shared_rows = shared.shape[0]
    swap = lambda x, bit: lax.ppermute(x, "dp", [(k, k ^ bit) for k in range(ways)])
    side = lambda n: (own_dp // bits[n]) % 2
    halving = {"keep": shared, "rows": shared_rows, "got": None}

    def halve(n):
        keep, size = halving["keep"], halving["rows"]
        if n > 0:
            add = lambda p, a, b: [a[...] + b[...]]
            size = size // 2
            (keep,) = rowwise(
                chain,
                side(n - 1).astype(jnp.int32)[None],
                add,
                [(keep, lambda p: p), (halving["got"], 0)],
                [(size, width, F32, 0, None)],
                size,
                step=size,
                name="halve",
            )
            halving["rows"] = size
        if n < len(bits):
            away = lax.dynamic_slice_in_dim(keep, (1 - side(n)) * (size // 2), size // 2, 0)
            halving["got"] = swap(away, bits[n])
        halving["keep"] = keep

    core = side(0).astype(jnp.int32)[None]
    core_bit, axes = bits[0], list(range(1, len(bits)))
    turned = axes[len(axes) // 2 :] + axes[: len(axes) // 2]
    orders = (axes, turned)
    sums = {}

    def reduce_step(step):
        sides = jnp.stack([side(orders[k][step]).astype(jnp.int32) for k in range(2)])
        ins, outs = [], []
        size = sums["keep"][0].shape[0] // 2
        unit = size if size < 512 else size // 2
        for k in range(2):
            for stay in (1, 0):
                at = functools.partial(
                    lambda p, k, stay: (p[k] if stay else 1 - p[k]) * (size // unit), k=k, stay=stay
                )
                ins += [(sums["keep"][k], at), (sums["got"][k], at)]
                outs.append((size, channels, F32, 0, None))
        results = rowwise(
            chain,
            sides,
            lambda p, *refs: [refs[2 * n][...] + refs[2 * n + 1][...] for n in range(4)],
            ins,
            outs,
            size,
            step=unit,
            whole_place=True,
            name="reduce_step",
        )
        sums["keep"] = [results[0], results[2]]
        sums["size"] = size
        sums["got"] = [swap(results[2 * k + 1], bits[orders[k][step]]) for k in range(2)]

    unit = D // 4 // 2 ** len(axes)

    def reduce_start():
        tiles, sums["gains"] = run_weight_grads(
            chain, core, normed, low, out_cotangent, mixed, back_weights[:2], gains, unit
        )
        sums["keep"] = tiles[2:]
        sums["got"] = [swap(x, core_bit) for x in tiles[:2]]

    def gather_first():
        sums["full"] = rowwise(
            chain,
            where,
            lambda p, a, b, c, d: [a[...] + b[...], c[...] + d[...]],
            [(x, 0) for k in range(2) for x in (sums["keep"][k], sums["got"][k])],
            [(sums["size"], channels, F32, 0, None)] * 2,
            sums["size"],
            step=sums["size"],
            name="gather_first",
        )
        step = len(axes) - 1
        sums["got"] = [swap(sums["full"][k], bits[orders[k][step]]) for k in range(2)]

    def gather_step(step):
        size = sums["size"]
        sides = jnp.stack([side(orders[k][step]).astype(jnp.int32) for k in range(2)])

        def body(p, *refs):
            upper = pl.program_id(0)
            picked = []
            for k in range(2):
                own, got = refs[2 * k][...], refs[2 * k + 1][...]
                picked.append(jnp.where(upper == p[k], own, got))
            return picked

        sums["full"] = rowwise(
            chain,
            sides,
            body,
            [(x, 0, False, 1) for k in range(2) for x in (sums["full"][k], sums["got"][k])],
            [(2 * size, channels, F32, 0, None)] * 2,
            2 * size,
            step=size,
            whole_place=True,
            name="gather_step",
        )
        sums["size"] = 2 * size
        if step > 0:
            sums["got"] = [swap(sums["full"][k], bits[orders[k][step - 1]]) for k in range(2)]

    def gather_core():
        sums["got"] = [swap(x, core_bit) for x in sums["full"]]

    halve(0)
    reduce_start()
    gain_rows = fit(sums["gains"][0] / norm_gain)
    gain_rows = jnp.pad(gain_rows, ((0, 8 - gain_rows.shape[0]), (0, 0)))
    halve(1)
    event(2, (pieces[3]["partial"], 0))

    reduce_step(0)
    halve(2)
    late["total"] = run_total(chain, low, back_weights)
    for n in range(3, len(bits) + 1):
        halve(n)
    share = jnp.concatenate([halving["keep"].reshape(-1), gain_rows.reshape(-1)])
    share_size = share.shape[0]
    late["share"] = jnp.pad(share, (0, part * D - share_size)).reshape(part, D)
    late["share_got"] = send(late["share"], INWARD)
    finish_chunk(0)
    event(3, (late["total"], at_ends(3, 0)))

    for step in range(1, len(axes)):
        reduce_step(step)
    gather_first()
    finish_chunk(1)
    for step in range(len(axes) - 1, 0, -1):
        gather_step(step)
    event(4, (late["total"], at_ends(2, 1)), at_ends(3, 0))

    share = pair_sum[3][spans[3] :] + inner[4][spans[3] :]
    share_got = send(share, OUTWARD)
    gather_step(0)
    gather_core()
    finish_chunk(2)
    event(5, (late["total"], lambda p: jnp.where(p < 2, 1 - p, 5 - p) * per), at_ends(2, 1))

    share, share_got = after(chain, share, share_got)
    share = jnp.where(middle, share, share_got)
    share = share.reshape(-1)[:share_size].reshape(-1, width)
    share = lax.all_gather(share, "dp")
    finish_chunk(3)
    gate_weight_grad, value_weight_grad, out_weight_grad = run_assemble(
        chain, core, sums["full"], sums["got"], unit
    )
    places = np.array(
        [sum((k >> n & 1) << (len(bits) - 1 - n) for n in range(len(bits))) for k in range(ways)]
    )
    order = np.argsort(places)
    gain_sums = share[:, -8:].sum(axis=0)
    share = jnp.concatenate([share[k, :-8] for k in order] + [gain_sums])
    shared = share
    norm_gain_grad = shared[-8:].reshape(-1)[:D]
    rest, shared = shared[:D], shared[D:]
    state_weight_grad = rest[:, :states]
    step_weight_grad = lax.dynamic_slice(rest, (0, states + place * head_count), (D, head_count))
    at = narrow_rows.shape[0]
    narrow = shared[:at].reshape(-1)[: 5 * states].reshape(5, states)
    mine = lax.dynamic_slice_in_dim(shared, at + place * mine_rows, mine_rows, 0).reshape(-1)
    wide_sums = mine[: 6 * channels].reshape(6, channels)
    head_sums = mine[6 * channels :][: 3 * head_count].reshape(3, head_count)
    chain.more = [state_weight_grad, step_weight_grad, norm_gain_grad, narrow, wide_sums, head_sums]
    finish_grad(6)
    return (
        late["block_out"],
        late["tokens_grad"],
        norm_gain_grad,
        gate_weight_grad,
        value_weight_grad,
        state_weight_grad,
        step_weight_grad,
        wide_sums[:4],
        wide_sums[4],
        narrow[:4],
        narrow[4],
        head_sums[0],
        head_sums[1],
        head_sums[2],
        wide_sums[5],
        out_weight_grad,
    )


def solution(mesh):
    placed = (
        P("dp", None),
        P(),
        P(None, "tensor"),
        P(None, "tensor"),
        P(),
        P(None, "tensor"),
        P(None, "tensor"),
        P("tensor"),
        P(),
        P(),
        P("tensor"),
        P("tensor"),
        P("tensor"),
        P("tensor"),
        P("tensor", None),
        P("dp", None),
        P("dp", None),
    )
    return jax.shard_map(
        on_device,
        mesh=mesh,
        in_specs=placed,
        out_specs=(
            P("dp", None),
            P(("dp", "tensor"), None),
            P(),
            P(None, "tensor"),
            P(None, "tensor"),
            P(),
            P(None, "tensor"),
            P(None, "tensor"),
            P("tensor"),
            P(),
            P(),
            P("tensor"),
            P("tensor"),
            P("tensor"),
            P("tensor"),
            P("tensor", None),
        ),
        check_vma=False,
    )
```

```python
import functools

import jax
import jax.numpy as jnp
import numpy as np
from jax import lax
from jax.experimental import pallas as pl
from jax.experimental.pallas import tpu as pltpu
from jax.sharding import PartitionSpec as P

D = 1536
INNER = 3072
EPS = 1e-05
BLOCK = 128
LANES = 128
FAR = -1e30
F32 = jnp.float32
BF16 = jnp.bfloat16
CHUNK = 256
STEP = 128
ROWS = 32
VMEM_LIMIT = 63 * 2**20
SMALL_COST = pl.CostEstimate(flops=1, bytes_accessed=1, transcendentals=0)
PIECES = (1, 1, 1, 1)


def matmul(left, right, dims=(1, 0)):
    return lax.dot_general(
        left, right, (((dims[0],), (dims[1],)), ((), ())), preferred_element_type=F32
    )


def exact(left, right):
    return lax.dot_general(
        left,
        right,
        (((1,), (0,)), ((), ())),
        precision=lax.Precision.HIGHEST,
        preferred_element_type=F32,
    )


def sigmoid(v):
    return 0.5 * jnp.tanh(0.5 * v) + 0.5


def softplus(v):
    return jnp.maximum(v, 0.0) + jnp.log1p(jnp.exp(-jnp.abs(v)))


def fold(x):
    return x.reshape(x.shape[0] // 8, 8, x.shape[1]).sum(axis=0)


def triangle(lower):
    row = lax.broadcasted_iota(jnp.int32, (BLOCK, BLOCK), 0)
    col = lax.broadcasted_iota(jnp.int32, (BLOCK, BLOCK), 1)
    return jnp.where(row >= col if lower else row <= col, 1.0, 0.0).astype(F32)


def group_sum(x, spread):
    high = x.astype(BF16)
    low = (x - high.astype(F32)).astype(BF16)
    return matmul(high, spread) + matmul(low, spread)


def upright(rows):
    fill = jnp.zeros((BLOCK - rows.shape[0], BLOCK), F32)
    return jnp.concatenate([rows, fill], axis=0).T


def segment_columns(seg_ref, block, blocks, ahead):
    part = lambda k: seg_ref[:, pl.ds(pl.multiple_of(k * BLOCK, BLOCK), BLOCK)].astype(F32)
    ids = part(block)
    before = jnp.where(block > 0, part(jnp.maximum(block - 1, 0)), -1.0)
    lane = lax.broadcasted_iota(jnp.int32, (1, BLOCK), 1)
    rows = [ids]
    if ahead:
        behind = jnp.where(block < blocks - 1, part(jnp.minimum(block + 1, blocks - 1)), -1.0)
    for far in range(1, 4):
        if ahead:
            moved = jnp.where(
                lane >= BLOCK - far,
                pltpu.roll(behind, BLOCK - far, 1),
                pltpu.roll(ids, BLOCK - far, 1),
            )
        else:
            moved = jnp.where(lane < far, pltpu.roll(before, far, 1), pltpu.roll(ids, far, 1))
        rows.append(jnp.where(moved == ids, 1.0, 0.0))
    rows.append(jnp.where(ids == before[:, BLOCK - 1 :], 1.0, 0.0))
    rows.append(jnp.where(ids == ids[:, BLOCK - 1 :], 1.0, 0.0))
    rows.append(jnp.zeros((2, BLOCK), F32))
    return upright(jnp.concatenate(rows, axis=0)), ids


def decay_terms(step_raw, step_bias, rate, cols, seg_row):
    steps = softplus(step_raw + step_bias)
    rates = -steps * rate
    local = exact(triangle(True), rates)
    last = local[BLOCK - 1 :]
    into = jnp.exp(jnp.where(cols[:, 4:5] > 0.5, local, FAR))
    out = jnp.exp(jnp.where(cols[:, 5:6] > 0.5, last - local, FAR))
    row = lax.broadcasted_iota(jnp.int32, (BLOCK, BLOCK), 0)
    col = lax.broadcasted_iota(jnp.int32, (BLOCK, BLOCK), 1)
    allowed = jnp.logical_and(row >= col, cols[:, 0:1] == seg_row)
    bias = jnp.where(allowed, 0.0, FAR)
    return steps, rates, local, local.T, into, out, bias


def pairwise(x, pair, half):
    return jnp.where(half, x[:, 2 * pair : 2 * pair + 1], x[:, 2 * pair + 1 : 2 * pair + 2])


def split_pair(x, half):
    zero = jnp.zeros_like(x)
    return jnp.concatenate([jnp.where(half, x, zero), jnp.where(half, zero, x)], axis=0)


def decay_of(local, local_t, bias, head):
    return jnp.exp(local[:, head : head + 1] - local_t[head : head + 1, :] + bias)


def sum_over_places(place, own, others):
    parts = len(others) + 1
    total = None
    for k in range(parts):
        value = own
        for turn in range(1, parts):
            value = jnp.where((place - k + parts) % parts == turn, others[turn - 1], value)
        total = value if total is None else total + value
    return total


GAIN_ROW, KERNEL_ROW, BIAS_ROW, GATED_ROW, SKIP_ROW = 0, 2, 6, 7, 8
STATE_KERNEL_ROW, STATE_BIAS_ROW, STEP_ROW, DECAY_ROW = 9, 13, 14, 15


def run_pack(place, *arrays):
    channels = arrays[1].shape[1]

    def kernel(place_ref, *refs):
        (norm_gain, kernel, bias, gated, skip, state_kernel, state_bias, step_bias, decay, step_w) = refs[
            :10
        ]
        table, wide, placed = refs[10:]
        table[...] = jnp.zeros_like(table)
        table[GAIN_ROW : GAIN_ROW + 1, :] = norm_gain[:channels].reshape(1, channels)
        table[GAIN_ROW + 1 : GAIN_ROW + 2, :] = norm_gain[channels:].reshape(1, channels)
        table[KERNEL_ROW : KERNEL_ROW + 4, :] = kernel[...]
        table[STATE_KERNEL_ROW : STATE_KERNEL_ROW + 4, : state_kernel.shape[1]] = state_kernel[...]
        rows = ((BIAS_ROW, bias), (GATED_ROW, gated), (SKIP_ROW, skip), (STATE_BIAS_ROW, state_bias))
        for row, ref in rows + ((STEP_ROW, step_bias), (DECAY_ROW, decay)):
            size = ref.shape[0]
            table[row : row + 1, :size] = ref[...].reshape(1, size)
        rows = step_w[...].astype(F32)
        fill = jnp.zeros((LANES - rows.shape[0], rows.shape[1]), F32)
        columns = jnp.concatenate([rows, fill], axis=0).T
        wide[...] = columns.astype(BF16)
        placed[...] = pltpu.roll(columns, place_ref[0] * rows.shape[0], 1).astype(BF16)

    return pl.pallas_call(
        kernel,
        out_shape=[
            jax.ShapeDtypeStruct((16, channels), F32),
            jax.ShapeDtypeStruct((arrays[-1].shape[1], LANES), BF16),
            jax.ShapeDtypeStruct((arrays[-1].shape[1], LANES), BF16),
        ],
        in_specs=[pl.BlockSpec(memory_space=pltpu.SMEM)]
        + [pl.BlockSpec(memory_space=pltpu.VMEM) for _ in arrays],
        cost_estimate=SMALL_COST,
        name="pack",
    )(place, *arrays)


def forward_kernel(first_piece, unused, block_base, *refs):
    tokens, cot, seg, par, gate_w, value_w, state_w, step_w, out_w = refs[:9]
    refs = refs[9:]
    if not first_piece:
        state_in, tail_in, state_tail_in = refs[:3]
        refs = refs[3:]
    refs = refs[unused:]
    (
        gate_out,
        vraw_out,
        pv_out,
        y_out,
        sraw_out,
        spv_out,
        step_out,
        saved_out,
        partial_out,
        stats_out,
        normed_out,
        state,
        tail_out,
        state_tail_out,
        vbuf,
        sbuf,
        scaled,
    ) = refs
    size = tokens.shape[0]
    channels = gate_w.shape[1]
    states = 2 * LANES

    @pl.when(pl.program_id(0) == 0)
    def _():
        if first_piece:
            state[...] = jnp.zeros_like(state)
            vbuf[:8] = jnp.zeros((8, channels), F32)
            sbuf[:8] = jnp.zeros((8, states), F32)
        else:
            state[...] = state_in[...]
            vbuf[:8] = tail_in[...]
            sbuf[:8] = state_tail_in[...]

    norm_gain = jnp.concatenate([par[GAIN_ROW : GAIN_ROW + 1], par[GAIN_ROW + 1 : GAIN_ROW + 2]], axis=1)
    scales = []
    for row in range(0, size, ROWS):
        wide = tokens[row : row + ROWS].astype(F32)
        scale = lax.rsqrt(jnp.mean(wide * wide, axis=-1, keepdims=True) + EPS)
        normed_out[row : row + ROWS] = (wide * scale * norm_gain).astype(BF16)
        scales.append(scale)
    normed = normed_out[...]
    vbuf[8:] = matmul(normed, value_w[...])
    sbuf[8:] = matmul(normed, state_w[...])
    step_out[...] = matmul(normed, step_w[...])
    gate_out[...] = matmul(normed, gate_w[...])

    def conv(buf, row, lanes, cols, kernel_row, bias_row):
        raw = buf[row + 8 : row + 8 + BLOCK, lanes]
        total = par[bias_row : bias_row + 1, lanes] + raw * par[kernel_row + 3 : kernel_row + 4, lanes]
        for back in range(1, 4):
            tap = par[kernel_row + 3 - back : kernel_row + 4 - back, lanes]
            moved = buf[row + 8 - back : row + 8 - back + BLOCK, lanes]
            total = total + moved * tap * cols[:, back : back + 1]
        return raw, total

    half = lax.broadcasted_iota(jnp.int32, (BLOCK, LANES), 1) < LANES // 2
    half_row = half[0:1]
    lane = lax.broadcasted_iota(jnp.int32, (BLOCK, LANES), 1)
    step_bias = par[STEP_ROW : STEP_ROW + 1, :LANES]
    rate = jnp.exp(par[DECAY_ROW : DECAY_ROW + 1, :LANES])
    skips = par[SKIP_ROW : SKIP_ROW + 1, :LANES]
    squares = []
    for sub in range(size // BLOCK):
        rows = slice(sub * BLOCK, (sub + 1) * BLOCK)
        row = sub * BLOCK
        block = block_base + pl.program_id(0) * (size // BLOCK) + sub
        cols, seg_row = segment_columns(seg, block, None, False)
        mixed_state = []
        for part in range(2):
            lanes = slice(part * LANES, (part + 1) * LANES)
            raw, spv = conv(sbuf, row, lanes, cols, STATE_KERNEL_ROW, STATE_BIAS_ROW)
            sraw_out[rows, lanes] = raw.astype(BF16)
            spv_out[rows, lanes] = spv
            mixed_state.append(spv * sigmoid(spv))
        b_low = mixed_state[0].astype(BF16)
        b_turned = mixed_state[0].T.astype(BF16)
        c_low = mixed_state[1].astype(BF16)
        steps, _, local, local_t, into, out, bias = decay_terms(
            step_out[rows], step_bias, rate, cols, seg_row
        )
        keep = into[BLOCK - 1 :]
        scores = matmul(c_low, b_low, (1, 1))
        square = jnp.zeros((BLOCK, LANES), F32)
        for pair in range(channels // LANES):
            lanes = slice(pair * LANES, (pair + 1) * LANES)
            raw, pv = conv(vbuf, row, lanes, cols, KERNEL_ROW, BIAS_ROW)
            vraw_out[rows, lanes] = raw.astype(BF16)
            pv_out[rows, lanes] = pv
            values = pv * sigmoid(pv)
            old = state[:, lanes]
            old_low = old.astype(BF16)
            saved_out[sub, :, lanes] = old_low
            u = values * pairwise(steps, pair, half)
            weights = [
                (scores * decay_of(local, local_t, bias, 2 * pair + k)).astype(BF16)
                for k in range(2)
            ]
            inner = matmul(jnp.concatenate(weights, axis=1), split_pair(u.astype(BF16), half))
            y_ssm = inner + matmul(c_low, old_low) * pairwise(into, pair, half)
            y_out[rows, lanes] = y_ssm
            leaving = (u * pairwise(out, pair, half)).astype(BF16)
            state[:, lanes] = old * pairwise(keep, pair, half_row) + matmul(b_turned, leaving)
            gate = gate_out[rows, lanes]
            gated = (y_ssm + pairwise(skips, pair, half_row) * values) * (gate * sigmoid(gate))
            square = square + gated * gated
            scaled[rows, lanes] = (gated * par[GATED_ROW : GATED_ROW + 1, lanes]).astype(BF16)
        squares.append(jnp.sum(square, axis=-1, keepdims=True))
    vbuf[:8] = vbuf[size:]
    sbuf[:8] = sbuf[size:]
    tail_out[...] = vbuf[:8]
    state_tail_out[...] = sbuf[:8]
    partial_out[...] = matmul(scaled[...], out_w[...])
    products = [
        jnp.sum(cot[row : row + ROWS].astype(F32) * partial_out[row : row + ROWS], axis=-1, keepdims=True)
        for row in range(0, size, ROWS)
    ]
    per = BLOCK // ROWS
    for sub in range(size // BLOCK):
        product = jnp.concatenate(products[sub * per : (sub + 1) * per], axis=0)
        scale = jnp.concatenate(scales[sub * per : (sub + 1) * per], axis=0)
        table = jnp.where(
            lane == 0, squares[sub], jnp.where(lane == 1, product, jnp.where(lane == 2, scale, 0.0))
        )
        stats_out[:, sub * BLOCK : (sub + 1) * BLOCK] = table.T[:8]


def backward_kernel(first_piece, unused, block_base, blocks, *refs):
    (
        place_ref,
        og_ref,
        gate_ref,
        vraw_ref,
        pv_ref,
        y_ref,
        sraw_ref,
        spv_ref,
        step_ref,
        own_stats,
        stats_1,
        stats_2,
        stats_3,
        saved_ref,
        seg,
        par,
    ) = refs[:16]
    refs = refs[16:]
    if not first_piece:
        carried_in = refs[:6]
        refs = refs[6:]
    refs = refs[unused:]
    (
        low_out,
        mixed_out,
        state_out,
        tail_out,
        state_tail_out,
        wide_acc,
        narrow_acc,
        heads_acc,
    ) = refs
    channels = gate_ref.shape[1]
    place = place_ref[0]

    @pl.when(pl.program_id(0) == 0)
    def _():
        outs = (state_out, tail_out, state_tail_out, wide_acc, narrow_acc, heads_acc)
        for k, ref in enumerate(outs):
            ref[...] = jnp.zeros_like(ref) if first_piece else carried_in[k][...]

    block = block_base + pl.num_programs(0) - 1 - pl.program_id(0)
    cols, seg_row = segment_columns(seg, block, blocks, True)
    stats = sum_over_places(place, own_stats[...], [stats_1[...], stats_2[...], stats_3[...]])
    stats = upright(stats)
    strength = lax.rsqrt(stats[:, 0:1] / INNER + EPS)
    pull = strength * strength * strength * stats[:, 1:2] / INNER

    half = lax.broadcasted_iota(jnp.int32, (BLOCK, LANES), 1) < LANES // 2
    half_row = half[0:1]
    spv = [spv_ref[:, :LANES], spv_ref[:, LANES:]]
    spv_sig = [sigmoid(v) for v in spv]
    b_part = spv[0] * spv_sig[0]
    c_part = spv[1] * spv_sig[1]
    b_low = b_part.astype(BF16)
    c_low = c_part.astype(BF16)
    c_turned = c_part.T.astype(BF16)
    step_raw = step_ref[...]
    step_bias = par[STEP_ROW : STEP_ROW + 1, :LANES]
    rate = jnp.exp(par[DECAY_ROW : DECAY_ROW + 1, :LANES])
    skips = par[SKIP_ROW : SKIP_ROW + 1, :LANES]
    steps, rates, local, local_t, into, out, bias = decay_terms(
        step_raw, step_bias, rate, cols, seg_row
    )
    keep = into[BLOCK - 1 :]
    scores = matmul(c_low, b_low, (1, 1))

    def conv_back(pre_grad, raw, lanes, after, kernel_row, acc):
        ext = jnp.concatenate([pre_grad, after[:, lanes]], axis=0)
        after[:, lanes] = pre_grad[:8]
        total = pre_grad * par[kernel_row + 3 : kernel_row + 4, lanes]
        acc[24:32, lanes] += fold(raw * pre_grad)
        acc[32:40, lanes] += fold(pre_grad)
        for ahead in range(1, 4):
            moved = pltpu.roll(ext, BLOCK + 8 - ahead, 0)[:BLOCK]
            term = moved * cols[:, ahead : ahead + 1]
            total = total + term * par[kernel_row + 3 - ahead : kernel_row + 4 - ahead, lanes]
            acc[8 * (3 - ahead) : 8 * (4 - ahead), lanes] += fold(raw * term)
        return total

    score_grad = jnp.zeros((BLOCK, BLOCK), F32)
    b_grad = jnp.zeros((BLOCK, LANES), F32)
    c_grad = jnp.zeros((BLOCK, LANES), F32)
    spread_dl = jnp.zeros((BLOCK, LANES), F32)
    spread_ds = jnp.zeros((BLOCK, LANES), F32)
    spread_end = jnp.zeros((8, LANES), F32)
    for pair in range(channels // LANES):
        lanes = slice(pair * LANES, (pair + 1) * LANES)
        spread = (
            lax.broadcasted_iota(jnp.int32, (LANES, LANES), 0) // (LANES // 2) + 2 * pair
            == lax.broadcasted_iota(jnp.int32, (LANES, LANES), 1)
        ).astype(BF16)
        gain = par[GATED_ROW : GATED_ROW + 1, lanes]
        skip = pairwise(skips, pair, half_row)
        gate = gate_ref[:, lanes]
        gate_sig = sigmoid(gate)
        gate_silu = gate * gate_sig
        pv = pv_ref[:, lanes]
        pv_sig = sigmoid(pv)
        values = pv * pv_sig
        og = og_ref[:, lanes]
        y_ssm = y_ref[:, lanes]
        y = y_ssm + skip * values
        gated = y * gate_silu
        strong = gated * strength
        mixed_out[:, lanes] = (strong * gain).astype(BF16)
        gated_grad = gain * strength * og - gated * pull
        low_out[:, lanes] = (
            gated_grad * y * (gate_sig * (1.0 + gate * (1.0 - gate_sig)))
        ).astype(BF16)
        grad = gated_grad * gate_silu
        wide_acc[40:48, lanes] += fold(og * strong)
        wide_acc[48:56, lanes] += fold(grad * values)

        state_grad = state_out[:, lanes]
        state_grad_low = state_grad.astype(BF16)
        old_low = saved_ref[0, :, lanes]
        pair_steps = pairwise(steps, pair, half)
        pair_out = pairwise(out, pair, half)
        u = values * pair_steps
        u_low = u.astype(BF16)
        g_low = grad.astype(BF16)
        g_split = split_pair(g_low, half)
        decays = [decay_of(local, local_t, bias, 2 * pair + k) for k in range(2)]
        weights = jnp.concatenate([(scores * d).astype(BF16) for d in decays], axis=0)
        weight_grad = matmul(g_split, u_low, (1, 1))
        score_grad = score_grad + weight_grad[:BLOCK] * decays[0] + weight_grad[BLOCK:] * decays[1]
        u_grad_out = matmul(b_low, state_grad_low) * pair_out
        u_grad = matmul(weights, g_split, (0, 0)) + u_grad_out
        u_near = u_low.astype(F32)
        spread_dl = spread_dl + group_sum(g_low.astype(F32) * y_ssm - u_near * u_grad, spread)
        spread_ds = spread_ds + group_sum(values * u_grad, spread)
        keep_row = pairwise(keep, pair, half_row)
        spread_end = spread_end + group_sum(
            fold(u_near * u_grad_out) + fold(state_grad * old_low.astype(F32)) * keep_row, spread
        )
        entering = (grad * pairwise(into, pair, half)).astype(BF16)
        leaving = (u * pair_out).astype(BF16)
        c_grad = c_grad + matmul(entering, old_low, (1, 1))
        b_grad = b_grad + matmul(leaving, state_grad_low, (1, 1))
        state_out[:, lanes] = state_grad * keep_row + matmul(c_turned, entering)
        pre_grad = (pair_steps * u_grad + skip * grad) * (pv_sig * (1.0 + pv * (1.0 - pv_sig)))
        raw_grad = conv_back(
            pre_grad, vraw_ref[:, lanes].astype(F32), lanes, tail_out, KERNEL_ROW, wide_acc
        )
        low_out[:, channels + pair * LANES : channels + (pair + 1) * LANES] = raw_grad.astype(BF16)
    score_low = score_grad.astype(BF16)
    c_grad = c_grad + matmul(score_low, b_low)
    b_grad = b_grad + matmul(score_low, c_low, (0, 0))
    rate_grad = exact(triangle(False), spread_dl) + jnp.sum(spread_end, axis=0, keepdims=True)
    step_grad = (spread_ds - rate * rate_grad) * sigmoid(step_raw + step_bias)
    heads_acc[0:8] += fold(step_grad)
    heads_acc[8:16] += fold(rates * rate_grad)
    for part, grad in enumerate((b_grad, c_grad)):
        lanes = slice(part * LANES, (part + 1) * LANES)
        pre_grad = grad * (spv_sig[part] * (1.0 + spv[part] * (1.0 - spv_sig[part])))
        raw_grad = conv_back(
            pre_grad, sraw_ref[:, lanes].astype(F32), lanes, state_tail_out, STATE_KERNEL_ROW, narrow_acc
        )
        at = 2 * channels + part * LANES
        low_out[:, at : at + LANES] = raw_grad.astype(BF16)
    heads_here = channels // (LANES // 2)
    low_out[:, 2 * channels + 2 * LANES :] = pltpu.roll(step_grad, place * heads_here, 1).astype(BF16)


def out_grad_kernel(unused, cot, out_w, *refs):
    og, token = refs[unused : unused + 2]
    og[...] = matmul(cot[...], out_w[...], (1, 1))
    token[...] = jnp.zeros((8, LANES), F32)


def run_out_grad(chain, cot, out_w, passes):
    length, channels = cot.shape[0], out_w.shape[0]
    deps = chain.deps()
    results = pl.pallas_call(
        functools.partial(out_grad_kernel, len(deps) + len(passes)),
        grid=(length // CHUNK,),
        in_specs=[pl.BlockSpec((CHUNK, D), lambda i: (i, 0)), whole(out_w.shape)]
        + [ANYWHERE for _ in deps + passes],
        out_specs=[pl.BlockSpec((CHUNK, channels), lambda i: (i, 0)), whole((8, LANES))]
        + [ANYWHERE for _ in passes],
        out_shape=[
            jax.ShapeDtypeStruct((length, channels), F32),
            jax.ShapeDtypeStruct((8, LANES), F32),
        ]
        + [jax.ShapeDtypeStruct(p.shape, p.dtype) for p in passes],
        input_output_aliases={2 + len(deps) + k: 2 + k for k in range(len(passes))},
        compiler_params=pltpu.CompilerParams(vmem_limit_bytes=VMEM_LIMIT),
        cost_estimate=SMALL_COST,
        name="out_grad",
    )(cot, out_w, *deps, *passes)
    chain.last = results[1]
    return results[0], results[2:]


def run_matmul(chain, body, ins, outs, count, scratch=(), name=None):
    deps = chain.deps()
    arrays = [a for a, _, _ in ins]

    def kernel(*refs):
        body(*refs[: len(arrays)], *refs[len(arrays) + len(deps) :])
        refs[len(arrays) + len(deps) + len(outs)][...] = jnp.zeros((8, LANES), F32)

    results = pl.pallas_call(
        kernel,
        grid=(count,),
        in_specs=[whole(a.shape) if m is None else pl.BlockSpec(b, m) for a, b, m in ins]
        + [ANYWHERE for _ in deps],
        out_specs=[pl.BlockSpec(b, m) for _, b, m in outs] + [whole((8, LANES))],
        out_shape=[jax.ShapeDtypeStruct(s, F32) for s, _, _ in outs]
        + [jax.ShapeDtypeStruct((8, LANES), F32)],
        scratch_shapes=list(scratch),
        compiler_params=pltpu.CompilerParams(vmem_limit_bytes=VMEM_LIMIT),
        cost_estimate=SMALL_COST,
        name=name,
    )(*arrays, *deps)
    chain.last = results[-1]
    return results[:-1]


def gain_row(value, count):
    out = []
    for k in range(count // BLOCK):
        column = jnp.sum(value[k * BLOCK : (k + 1) * BLOCK], axis=-1, keepdims=True)
        out.append(jnp.broadcast_to(column, (BLOCK, BLOCK)).T[:8])
    return jnp.concatenate(out, axis=1)


def run_rest_grad(chain, normed, low, small_rows, weights):
    width = small_rows.shape[1]
    count = D // CHUNK
    states = weights[0].shape[1]

    def body(left, right, extra, state_w, step_w, out, gain, token):
        @pl.when(pl.program_id(0) < count)
        def _():
            value = matmul(left[...], right[...], (0, 0))
            out[...] = value
            both = jnp.concatenate([state_w[...], step_w[...]], axis=1).astype(F32)
            gain[...] = gain_row(value * both, CHUNK)

        @pl.when(pl.program_id(0) == count)
        def _():
            out[...] = extra[...]

    length, total = low.shape
    held = lambda i: jnp.minimum(i, count - 1)
    tile = lambda a: (a, (CHUNK, a.shape[1]), lambda i: (held(i), 0))
    return run_matmul(
        chain,
        body,
        [
            (normed, (length, CHUNK), lambda i: (0, held(i))),
            (low, (length, width), lambda i: (0, total // width - 1)),
            (small_rows, None, None),
            *[tile(w) for w in weights],
        ],
        [
            ((D + CHUNK, width), (CHUNK, width), lambda i: (i, 0)),
            ((8, D), (8, CHUNK), lambda i: (0, held(i))),
        ],
        count + 1,
        name="rest_grad",
    )


def run_weight_grads(chain, core, normed, low, cot, mixed, weights, gains, unit):
    length = normed.shape[0]
    channels = mixed.shape[1]
    tile = D // 4
    deps = chain.deps()

    def which(i, p):
        return jnp.where(i < 2, 1 - p[0], p[0]) * 2 + i % 2

    def kernel(place, left, right, cots, mix, gate_w, value_w, gain_in, *refs):
        outs, gain, token = refs[len(deps) : len(deps) + 4], refs[-2], refs[-1]
        i = pl.program_id(0)

        @pl.when(i == 0)
        def _():
            gain[...] = gain_in[...]
            token[...] = jnp.zeros((8, LANES), F32)

        gate = matmul(left[...], right[:, :channels], (0, 0))
        value = matmul(left[...], right[:, channels:], (0, 0))
        out = matmul(cots[...], mix[...], (0, 0))
        at = pl.ds(pl.multiple_of(which(i, place) * tile, LANES), tile)
        products = gate * gate_w[...].astype(F32) + value * value_w[...].astype(F32)
        gain[:, at] = gain[:, at] + gain_row(products, tile)
        for k in range(4):

            @pl.when(i == k)
            def _(k=k):
                for n in range(tile // unit):
                    rows = slice(n * unit, (n + 1) * unit)
                    for m, part in enumerate((gate, value, out)):
                        first = (3 * n + m) * unit
                        outs[k][first : first + unit, :] = part[rows]

    lanes = lambda i, p: (0, which(i, p))
    weight_spec = pl.BlockSpec((tile, channels), lambda i, p: (which(i, p), 0))
    results = pl.pallas_call(
        kernel,
        grid_spec=pltpu.PrefetchScalarGridSpec(
            num_scalar_prefetch=1,
            grid=(4,),
            in_specs=[
                pl.BlockSpec((length, tile), lanes),
                pl.BlockSpec((length, 2 * channels), lambda i, p: (0, 0)),
                pl.BlockSpec((length, tile), lanes),
                whole(mixed.shape),
                weight_spec,
                weight_spec,
                whole(gains.shape),
            ]
            + [ANYWHERE for _ in deps],
            out_specs=[whole((3 * tile, channels))] * 4 + [whole(gains.shape), whole((8, LANES))],
        ),
        out_shape=[jax.ShapeDtypeStruct((3 * tile, channels), F32)] * 4
        + [jax.ShapeDtypeStruct(gains.shape, F32), jax.ShapeDtypeStruct((8, LANES), F32)],
        compiler_params=pltpu.CompilerParams(vmem_limit_bytes=VMEM_LIMIT),
        cost_estimate=SMALL_COST,
        name="weight_grads",
    )(core, normed, low, cot, mixed, *weights, gains, *deps)
    chain.last = results[-1]
    return results[:4], results[4]


def run_assemble(chain, core, own, got, unit):
    rows, channels = own[0].shape
    tile = rows // 3
    deps = chain.deps()

    def kernel(place, own_a, own_b, got_a, got_b, *refs):
        gate, value, out, token = refs[len(deps) :]
        i = pl.program_id(0)
        token[...] = jnp.zeros((8, LANES), F32)
        for n, (mine, other) in enumerate(((own_a, got_a), (own_b, got_b))):

            @pl.when(i % 2 == n)
            def _(mine=mine, other=other):
                use_own = i // 2 == place[0]
                pieces = []
                for k in range(rows // unit):
                    at = slice(k * unit, (k + 1) * unit)
                    pieces.append(jnp.where(use_own, mine[at, :], other[at, :]))
                gate[...] = jnp.concatenate(pieces[0::3], axis=0)
                value[...] = jnp.concatenate(pieces[1::3], axis=0)
                out[...] = jnp.concatenate(pieces[2::3], axis=0).T

    row = pl.BlockSpec((tile, channels), lambda i, p: (i, 0))
    gate, value, out, chain.last = pl.pallas_call(
        kernel,
        grid_spec=pltpu.PrefetchScalarGridSpec(
            num_scalar_prefetch=1,
            grid=(4,),
            in_specs=[whole(own[0].shape)] * 4 + [ANYWHERE for _ in deps],
            out_specs=[
                row,
                row,
                pl.BlockSpec((channels, tile), lambda i, p: (0, i)),
                whole((8, LANES)),
            ],
        ),
        out_shape=[
            jax.ShapeDtypeStruct((D, channels), F32),
            jax.ShapeDtypeStruct((D, channels), F32),
            jax.ShapeDtypeStruct((channels, D), F32),
            jax.ShapeDtypeStruct((8, LANES), F32),
        ],
        compiler_params=pltpu.CompilerParams(vmem_limit_bytes=VMEM_LIMIT),
        cost_estimate=SMALL_COST,
        name="assemble",
    )(core, *own, *got, *deps)
    return gate, value, out


def run_total(chain, low, weights):
    length, width = low.shape

    def body(left, gate_w, value_w, state_w, step_w, out, token, joined):
        @pl.when(pl.program_id(0) == 0)
        def _():
            at = 0
            for ref in (gate_w, value_w, state_w, step_w):
                joined[:, at : at + ref.shape[1]] = ref[...]
                at += ref.shape[1]

        out[...] = matmul(left[...], joined[...], (1, 1))

    (out,) = run_matmul(
        chain,
        body,
        [(low, (CHUNK, width), lambda i: (i, 0))] + [(w, None, None) for w in weights],
        [((length, D), (CHUNK, D), lambda i: (i, 0))],
        length // CHUNK,
        scratch=[pltpu.VMEM((D, width), BF16)],
        name="normed_grad",
    )
    return out


def whole(shape):
    return pl.BlockSpec(shape, lambda i, *_: (0,) * len(shape))


ANYWHERE = pl.BlockSpec(memory_space=pl.ANY)


def run_forward(start, count, tokens, cot, seg, small, carried, kept, deps):
    channels = small["gate_w"].shape[1]
    states = 2 * LANES
    size = CHUNK
    length = count * size
    first = start // size
    per = size // BLOCK
    full = tokens.shape[0]

    def row_in(width):
        return pl.BlockSpec((size, width), lambda i: (first + i, 0))

    def row_out(width):
        return pl.BlockSpec((size, width), lambda i: (i, 0))

    constant = [small[n] for n in ("par", "gate_w", "value_w", "state_w", "step_w", "out_w")]
    carry_shapes = [(LANES, channels), (8, channels), (8, states)]
    widths = (
        (channels, F32),
        (channels, BF16),
        (channels, F32),
        (channels, F32),
        (states, BF16),
        (states, F32),
        (LANES, F32),
    )
    inputs = [tokens, cot, seg, *constant, *carried, *deps, *kept]
    outs = pl.pallas_call(
        functools.partial(forward_kernel, not carried, len(deps) + len(kept), start // BLOCK),
        grid=(count,),
        in_specs=[row_in(D), row_in(D), whole(seg.shape)]
        + [whole(c.shape) for c in constant]
        + [whole(c.shape) for c in carried]
        + [ANYWHERE for _ in deps + kept],
        out_specs=[row_out(w) for w, _ in widths]
        + [pl.BlockSpec((per, LANES, channels), lambda i: (i, 0, 0))]
        + [row_out(D)]
        + [pl.BlockSpec((8, size), lambda i: (0, first + i))]
        + [row_in(D)]
        + [whole(c) for c in carry_shapes],
        out_shape=[jax.ShapeDtypeStruct((length, w), k) for w, k in widths]
        + [jax.ShapeDtypeStruct((length // BLOCK, LANES, channels), BF16)]
        + [jax.ShapeDtypeStruct((length, D), F32)]
        + [jax.ShapeDtypeStruct((8, full), F32)]
        + [jax.ShapeDtypeStruct((full, D), BF16)]
        + [jax.ShapeDtypeStruct(c, F32) for c in carry_shapes],
        scratch_shapes=[
            pltpu.VMEM((size + 8, channels), F32),
            pltpu.VMEM((size + 8, states), F32),
            pltpu.VMEM((size, channels), BF16),
        ],
        input_output_aliases={len(inputs) - len(kept) + k: 9 + k for k in range(len(kept))},
        compiler_params=pltpu.CompilerParams(vmem_limit_bytes=VMEM_LIMIT),
        cost_estimate=SMALL_COST,
        name="forward_piece",
    )(*inputs)
    outs = list(outs)
    names = ("gate", "vraw", "pv", "y", "sraw", "spv", "step", "saved", "partial")
    return dict(zip(names, outs[:9])), outs[9:11], outs[11:]


def run_backward(start, piece, og, stats, place, seg, small, carried, low, mixed, deps):
    channels = small["gate_w"].shape[1]
    length = piece["gate"].shape[0]
    full = og.shape[0]
    count = length // BLOCK
    first = start // BLOCK
    flip = lambda i: count - 1 - i

    def row(width):
        return pl.BlockSpec((BLOCK, width), lambda i, *_: (flip(i), 0))

    def shared(width):
        return pl.BlockSpec((BLOCK, width), lambda i, *_: (first + flip(i), 0))

    names = ("gate", "vraw", "pv", "y", "sraw", "spv", "step")
    ins = [piece[n] for n in names]
    low_width = 2 * channels + 3 * LANES
    kept = [] if low is None else [low, mixed]
    carry_shapes = [
        (LANES, channels),
        (8, channels),
        (8, 2 * LANES),
        (56, channels),
        (40, 2 * LANES),
        (16, LANES),
    ]
    inputs = [og, *ins, *stats, piece["saved"], seg, small["par"], *carried, *deps, *kept]
    outs = pl.pallas_call(
        functools.partial(
            backward_kernel, not carried, len(deps) + len(kept), first, full // BLOCK
        ),
        grid_spec=pltpu.PrefetchScalarGridSpec(
            num_scalar_prefetch=1,
            grid=(count,),
            in_specs=[shared(channels)]
            + [row(a.shape[1]) for a in ins]
            + [pl.BlockSpec((8, BLOCK), lambda i, *_: (0, first + flip(i))) for _ in stats]
            + [pl.BlockSpec((1, LANES, channels), lambda i, *_: (flip(i), 0, 0))]
            + [whole(seg.shape), whole(small["par"].shape)]
            + [whole(c.shape) for c in carried]
            + [ANYWHERE for _ in deps + kept],
            out_specs=[shared(low_width), shared(channels)] + [whole(c) for c in carry_shapes],
        ),
        out_shape=[
            jax.ShapeDtypeStruct((full, low_width), BF16),
            jax.ShapeDtypeStruct((full, channels), BF16),
        ]
        + [jax.ShapeDtypeStruct(c, F32) for c in carry_shapes],
        compiler_params=pltpu.CompilerParams(vmem_limit_bytes=VMEM_LIMIT),
        cost_estimate=SMALL_COST,
        input_output_aliases={1 + len(inputs) - 2 + k: k for k in range(len(kept))},
        name="backward_piece",
    )(place, *inputs)
    return outs[0], outs[1], list(outs[2:])


class Chain:
    def __init__(self):
        self.last = None
        self.more = []

    def deps(self):
        found = ([] if self.last is None else [self.last]) + self.more
        self.more = []
        return found


def rowwise(
    chain, place, body, ins, outs, rows, passes=(), step=0, whole_place=False, name=None
):
    step = step or STEP
    steps = rows // step

    def spec(width, first, most=steps, where=None):
        if where is not None:
            base = first if callable(first) else lambda p: first
            return pl.BlockSpec(
                (step, width),
                lambda i, p: (
                    jnp.where(where(p[0]), base(p[0]) + jnp.minimum(i, most - 1), 0),
                    0,
                ),
            )
        if callable(first):
            return pl.BlockSpec(
                (step, width),
                lambda i, p: (
                    jnp.maximum(first(p if whole_place else p[0]) + jnp.minimum(i, most - 1), 0),
                    0,
                ),
            )
        return pl.BlockSpec((step, width), lambda i, p: (first + jnp.minimum(i, most - 1), 0))

    def lying(height, first):
        if callable(first):
            return pl.BlockSpec((height, STEP), lambda i, p: (0, first(p[0]) + i))
        return pl.BlockSpec((height, STEP), lambda i, p: (0, first + i))

    def spec_of(array, first, across=False, most=steps, where=None):
        if first is None:
            return fixed(array.shape)
        return lying(array.shape[0], first) if across else spec(array.shape[1], first, most, where)

    def fixed(shape):
        return pl.BlockSpec(shape, lambda i, p: (0,) * len(shape))

    anywhere = pl.BlockSpec(memory_space=pl.ANY)
    arrays = [entry[0] for entry in ins]
    in_specs = [spec_of(*entry) for entry in ins]
    kept = [(k, o[4]) for k, o in enumerate(outs) if o[4] is not None]
    deps = chain.deps()
    inputs = [*arrays, *[a for _, a in kept], *passes, *deps]
    aliases = {1 + len(arrays) + n: k for n, (k, _) in enumerate(kept)}
    for n in range(len(passes)):
        aliases[1 + len(arrays) + len(kept) + n] = len(outs) + n

    def kernel(place_ref, *refs):
        results = refs[len(inputs) :]
        values = body(place_ref if whole_place else place_ref[0], *refs[: len(arrays)])
        for ref, value in zip(results[: len(outs)], values):
            ref[...] = value
        results[-1][...] = jnp.zeros((8, LANES), F32)

    results = pl.pallas_call(
        kernel,
        grid_spec=pltpu.PrefetchScalarGridSpec(
            num_scalar_prefetch=1,
            grid=(steps,),
            in_specs=in_specs + [anywhere] * (len(inputs) - len(arrays)),
            out_specs=[spec(o[1], o[3], *o[5:]) for o in outs]
            + [anywhere] * len(passes)
            + [fixed((8, LANES))],
        ),
        out_shape=[jax.ShapeDtypeStruct((o[0], o[1]), o[2]) for o in outs]
        + [jax.ShapeDtypeStruct(p.shape, p.dtype) for p in passes]
        + [jax.ShapeDtypeStruct((8, LANES), F32)],
        input_output_aliases=aliases,
        compiler_params=pltpu.CompilerParams(vmem_limit_bytes=VMEM_LIMIT),
        cost_estimate=SMALL_COST,
        name=name,
    )(place, *inputs)
    chain.last = results[-1]
    return list(results[:-1])


def after(chain, *arrays):
    def kernel(*refs):
        refs[-1][...] = jnp.zeros((8, LANES), F32)

    anywhere = pl.BlockSpec(memory_space=pl.ANY)
    deps = chain.deps()
    results = pl.pallas_call(
        kernel,
        in_specs=[anywhere] * (len(arrays) + len(deps)),
        out_specs=[anywhere] * len(arrays) + [pl.BlockSpec(memory_space=pltpu.VMEM)],
        out_shape=[jax.ShapeDtypeStruct(a.shape, a.dtype) for a in arrays]
        + [jax.ShapeDtypeStruct((8, LANES), F32)],
        input_output_aliases={k: k for k in range(len(arrays))},
        cost_estimate=SMALL_COST,
        name="in_order",
    )(*arrays, *deps)
    chain.last = results[-1]
    return list(results[:-1])


INWARD = ((0, 1), (3, 2))
ACROSS = ((1, 2), (2, 1))
OUTWARD = ((1, 0), (2, 3))


def on_device(
    tokens,
    norm_gain,
    gate_weight,
    value_weight,
    state_weight,
    step_weight,
    value_kernel,
    value_bias,
    state_kernel,
    state_bias,
    step_bias,
    decay_log,
    skip_scale,
    gated_gain,
    out_weight,
    segment_ids,
    out_cotangent,
):
    parts = lax.axis_size("tensor")
    place = lax.axis_index("tensor")
    middle = jnp.logical_and(place > 0, place < parts - 1)
    length = tokens.shape[0]
    channels = gate_weight.shape[1]
    head_count = step_bias.shape[0]
    rows = length // parts
    states = 2 * LANES
    where = place.astype(jnp.int32)[None]
    par, step_wide, step_place = run_pack(
        where,
        norm_gain,
        value_kernel,
        value_bias,
        gated_gain,
        skip_scale,
        state_kernel,
        state_bias,
        step_bias,
        decay_log,
        step_weight.T,
    )
    small = {
        "gate_w": gate_weight,
        "value_w": value_weight,
        "state_w": state_weight,
        "step_w": step_wide,
        "out_w": out_weight,
        "par": par,
    }
    chain = Chain()
    send = lambda x, pairs: lax.ppermute(x, "tensor", pairs)
    run = functools.partial(rowwise, chain, where)
    steps = lambda n: n // STEP

    spans = [p * length // sum(PIECES) for p in PIECES]
    firsts = [sum(spans[:k]) for k in range(len(spans))]
    pieces = []
    carried = []
    kept = []
    late = {}
    count = len(spans)
    outer, inner, outer_sent, pair_sum = {}, {}, {}, {}

    def forward():
        nonlocal carried, kept
        k = len(pieces)
        outs, kept, carried = run_forward(
            firsts[k],
            spans[k] // CHUNK,
            tokens,
            out_cotangent,
            segment_ids,
            small,
            carried,
            kept,
            chain.deps(),
        )
        pieces.append(outs)
        chain.last = carried[2]


    def send_outer(n, message, both=True):
        outer_sent[n] = message
        outer[n] = send(message, INWARD + OUTWARD if both else INWARD)

    is_middle = lambda p: jnp.logical_and(p > 0, p < parts - 1)
    per = steps(rows)
    at_ends = lambda low_end, high_end: lambda p: jnp.where(p < 2, low_end, high_end) * per

    def event(n, following=None, middle_segment=None):
        chunk = n < count
        step = STEP
        blocks = spans[0] // step
        size = spans[0]
        is_end = lambda p: jnp.logical_not(is_middle(p))
        if chunk:
            mine = (pieces[n]["partial"], 0, False, blocks, is_middle)
        else:
            mine = (late["total"], middle_segment, False, blocks, is_middle)
        ins = [mine, (outer[n], 0, False, blocks, is_middle)]
        outs = [(size, D, F32, 0, None, blocks, is_middle)]
        if n > 0:
            array, first = following
            from_middle = (inner[n], 0, False, blocks, is_middle)
            if n <= count:
                ins += [(pair_sum[n - 1], 0, False, blocks, is_middle), from_middle]
                ins += [(array, first, False, blocks, is_end)]
            else:
                ins += [(array, first, False, blocks), from_middle]
            outs.append((spans[0], D, F32, 0, None, blocks))

        def body(p, a, b, *others):
            value = a[...] + b[...]
            results = [value]
            if n > 0:
                message = others[0][...] + others[1][...]
                if n <= count:
                    message = jnp.where(is_middle(p), message, others[2][...])
                results.append(message)
            return results

        results = run(body, ins, outs, size, step=step, name="event")
        pair_sum[n] = results[0]
        inner[n + 1] = send(results[0], ACROSS)
        if n > 0:
            send_outer(n + 1, results[1])
        else:
            send_outer(1, following[0], False)

    def finish_chunk(k):
        def body(p, own, got, token, *stats):
            inside = jnp.logical_and(p > 0, p < parts - 1)
            total = jnp.where(inside, own[...], got[...])
            table = upright(sum_over_places(p, stats[0][...], [x[...] for x in stats[1:]]))
            strength = lax.rsqrt(table[:, 0:1] / INNER + EPS)
            return [(token[...].astype(F32) + total * strength).astype(BF16)]

        first = steps(firsts[k])
        (late["block_out"],) = run(
            body,
            [(outer_sent[k + 2], 0), (outer[k + 2], 0), (tokens, first)]
            + [(x, first, True) for x in late["stats"]],
            [(length, D, BF16, first, late.get("block_out"))],
            spans[k],
            name="finish_chunk",
        )

    def finish_grad(n):
        def body(p, mine, side_got, middle_got, token, scale, cot, gain):
            token = token[...].astype(F32)
            scale = upright(scale[...])[:, 2:3]
            weighted = (mine[...] + side_got[...] + middle_got[...]) * gain[...]
            pull = jnp.sum(weighted * token, axis=-1, keepdims=True) / D
            return [cot[...].astype(F32) + scale * weighted - token * scale * scale * scale * pull]

        mine = lambda p: p * per
        (late["tokens_grad"],) = run(
            body,
            [
                (late["total"], mine),
                (outer[n], 0),
                (inner[n], 0),
                (tokens, mine),
                (late["own_stats"], mine, True),
                (out_cotangent, mine),
                (norm_gain[None], None),
            ],
            [(rows, D, F32, 0, None)],
            rows,
            name="finish_grad",
        )

    low = mixed = None
    back = []

    def backward(k):
        nonlocal low, mixed, back
        low, mixed, back = run_backward(
            firsts[k],
            pieces[k],
            late["og"],
            late["stats"],
            where,
            segment_ids,
            small,
            back,
            low,
            mixed,
            chain.deps(),
        )
        chain.last = back[2]

    def exchange_stats():
        own = late["own_stats"] = kept[0]
        late["stats"] = [own] + [
            send(own, [(k, (k + turn) % parts) for k in range(parts)]) for turn in range(1, parts)
        ]
        chain.more = late["stats"][1:]

    forward()
    send_outer(0, pieces[0]["partial"], False)
    forward()
    forward()
    late["og"], _ = run_out_grad(chain, out_cotangent, out_weight, [])
    forward()
    exchange_stats()
    event(0, (pieces[1]["partial"], 0))
    backward(3)
    backward(2)
    backward(1)
    backward(0)
    event(1, (pieces[2]["partial"], 0))

    normed = kept[1]
    wide_acc, narrow_acc, heads_acc = back[3:]
    back_weights = [gate_weight, value_weight, state_weight, step_place]
    width = 3 * LANES
    fit = lambda x: jnp.pad(x.reshape(-1), (0, -x.size % width)).reshape(-1, width)
    narrow = narrow_acc.reshape(5, 8, states).sum(axis=1)
    wide_sums = wide_acc.reshape(7, 8, channels).sum(axis=1)
    head_sums = heads_acc.reshape(2, 8, LANES).sum(axis=1)[:, :head_count]
    skip_grad = wide_sums[6].reshape(head_count, channels // head_count).sum(axis=1)
    mine = jnp.concatenate([fit(wide_sums[:6]), fit(jnp.concatenate([head_sums, skip_grad[None]]))])
    mine_rows = mine.shape[0]
    slots = jnp.where(
        lax.broadcasted_iota(jnp.int32, (parts, 1, 1), 0) == place, mine[None], 0.0
    ).reshape(-1, width)
    narrow_rows = fit(narrow)
    filler = jnp.zeros((CHUNK - narrow_rows.shape[0] - slots.shape[0], width), F32)
    shared, gains = run_rest_grad(
        chain, normed, low, jnp.concatenate([narrow_rows, slots, filler]), back_weights[2:]
    )

    ways = lax.axis_size("dp")
    own_dp = lax.axis_index("dp")
    bits = []
    while 2 ** len(bits) < ways:
        bits.append(2 ** len(bits))
    shared_rows = shared.shape[0]
    swap = lambda x, bit: lax.ppermute(x, "dp", [(k, k ^ bit) for k in range(ways)])
    side = lambda n: (own_dp // bits[n]) % 2
    halving = {"keep": shared, "rows": shared_rows, "got": None}

    def halve(n):
        keep, size = halving["keep"], halving["rows"]
        if n > 0:
            add = lambda p, a, b: [a[...] + b[...]]
            size = size // 2
            (keep,) = rowwise(
                chain,
                side(n - 1).astype(jnp.int32)[None],
                add,
                [(keep, lambda p: p), (halving["got"], 0)],
                [(size, width, F32, 0, None)],
                size,
                step=size,
                name="halve",
            )
            halving["rows"] = size
        if n < len(bits):
            away = lax.dynamic_slice_in_dim(keep, (1 - side(n)) * (size // 2), size // 2, 0)
            halving["got"] = swap(away, bits[n])
        halving["keep"] = keep

    core = side(0).astype(jnp.int32)[None]
    core_bit, axes = bits[0], list(range(1, len(bits)))
    turned = axes[len(axes) // 2 :] + axes[: len(axes) // 2]
    orders = (axes, turned)
    sums = {}

    def reduce_step(step):
        sides = jnp.stack([side(orders[k][step]).astype(jnp.int32) for k in range(2)])
        ins, outs = [], []
        size = sums["keep"][0].shape[0] // 2
        unit = size if size < 512 else size // 2
        for k in range(2):
            for stay in (1, 0):
                at = functools.partial(
                    lambda p, k, stay: (p[k] if stay else 1 - p[k]) * (size // unit), k=k, stay=stay
                )
                ins += [(sums["keep"][k], at), (sums["got"][k], at)]
                outs.append((size, channels, F32, 0, None))
        results = rowwise(
            chain,
            sides,
            lambda p, *refs: [refs[2 * n][...] + refs[2 * n + 1][...] for n in range(4)],
            ins,
            outs,
            size,
            step=unit,
            whole_place=True,
            name="reduce_step",
        )
        sums["keep"] = [results[0], results[2]]
        sums["size"] = size
        sums["got"] = [swap(results[2 * k + 1], bits[orders[k][step]]) for k in range(2)]

    unit = D // 4 // 2 ** len(axes)

    def reduce_start():
        tiles, sums["gains"] = run_weight_grads(
            chain, core, normed, low, out_cotangent, mixed, back_weights[:2], gains, unit
        )
        sums["keep"] = tiles[2:]
        sums["got"] = [swap(x, core_bit) for x in tiles[:2]]

    def gather_first():
        sums["full"] = rowwise(
            chain,
            where,
            lambda p, a, b, c, d: [a[...] + b[...], c[...] + d[...]],
            [(x, 0) for k in range(2) for x in (sums["keep"][k], sums["got"][k])],
            [(sums["size"], channels, F32, 0, None)] * 2,
            sums["size"],
            step=sums["size"],
            name="gather_first",
        )
        step = len(axes) - 1
        sums["got"] = [swap(sums["full"][k], bits[orders[k][step]]) for k in range(2)]

    def gather_step(step):
        size = sums["size"]
        sides = jnp.stack([side(orders[k][step]).astype(jnp.int32) for k in range(2)])

        def body(p, *refs):
            upper = pl.program_id(0)
            picked = []
            for k in range(2):
                own, got = refs[2 * k][...], refs[2 * k + 1][...]
                picked.append(jnp.where(upper == p[k], own, got))
            return picked

        sums["full"] = rowwise(
            chain,
            sides,
            body,
            [(x, 0, False, 1) for k in range(2) for x in (sums["full"][k], sums["got"][k])],
            [(2 * size, channels, F32, 0, None)] * 2,
            2 * size,
            step=size,
            whole_place=True,
            name="gather_step",
        )
        sums["size"] = 2 * size
        if step > 0:
            sums["got"] = [swap(sums["full"][k], bits[orders[k][step - 1]]) for k in range(2)]

    def gather_core():
        sums["got"] = [swap(x, core_bit) for x in sums["full"]]

    halve(0)
    reduce_start()
    gain_rows = fit(sums["gains"][0] / norm_gain)
    gain_rows = jnp.pad(gain_rows, ((0, 8 - gain_rows.shape[0]), (0, 0)))
    halve(1)
    event(2, (pieces[3]["partial"], 0))

    halve(2)
    reduce_step(0)
    late["total"] = run_total(chain, low, back_weights)
    finish_chunk(0)
    event(3, (late["total"], at_ends(3, 0)))

    for step in range(1, len(axes)):
        reduce_step(step)
    gather_first()
    finish_chunk(1)
    for step in range(len(axes) - 1, 0, -1):
        gather_step(step)
    for n in range(3, len(bits) + 1):
        halve(n)
    share = jnp.concatenate([halving["keep"], gain_rows])
    share = lax.psum(share, "tensor")
    event(4, (late["total"], at_ends(2, 1)), at_ends(3, 0))

    gather_step(0)
    gather_core()
    finish_chunk(2)
    event(5, (late["total"], lambda p: jnp.where(p < 2, 1 - p, 5 - p) * per), at_ends(2, 1))

    (share,) = after(chain, share)
    share = lax.all_gather(share, "dp")
    finish_chunk(3)
    gate_weight_grad, value_weight_grad, out_weight_grad = run_assemble(
        chain, core, sums["full"], sums["got"], unit
    )

    places = np.array(
        [sum((k >> n & 1) << (len(bits) - 1 - n) for n in range(len(bits))) for k in range(ways)]
    )
    order = np.argsort(places)
    gain_sums = share[:, -8:].sum(axis=0)
    share = jnp.concatenate([share[k, :-8] for k in order] + [gain_sums])
    shared = share
    norm_gain_grad = shared[-8:].reshape(-1)[:D]
    rest, shared = shared[:D], shared[D:]
    state_weight_grad = rest[:, :states]
    step_weight_grad = lax.dynamic_slice(rest, (0, states + place * head_count), (D, head_count))
    at = narrow_rows.shape[0]
    narrow = shared[:at].reshape(-1)[: 5 * states].reshape(5, states)
    mine = lax.dynamic_slice_in_dim(shared, at + place * mine_rows, mine_rows, 0).reshape(-1)
    wide_sums = mine[: 6 * channels].reshape(6, channels)
    head_sums = mine[6 * channels :][: 3 * head_count].reshape(3, head_count)
    chain.more = [state_weight_grad, step_weight_grad, norm_gain_grad, narrow, wide_sums, head_sums]
    finish_grad(6)
    return (
        late["block_out"],
        late["tokens_grad"],
        norm_gain_grad,
        gate_weight_grad,
        value_weight_grad,
        state_weight_grad,
        step_weight_grad,
        wide_sums[:4],
        wide_sums[4],
        narrow[:4],
        narrow[4],
        head_sums[0],
        head_sums[1],
        head_sums[2],
        wide_sums[5],
        out_weight_grad,
    )


def solution(mesh):
    placed = (
        P("dp", None),
        P(),
        P(None, "tensor"),
        P(None, "tensor"),
        P(),
        P(None, "tensor"),
        P(None, "tensor"),
        P("tensor"),
        P(),
        P(),
        P("tensor"),
        P("tensor"),
        P("tensor"),
        P("tensor"),
        P("tensor", None),
        P("dp", None),
        P("dp", None),
    )
    return jax.shard_map(
        on_device,
        mesh=mesh,
        in_specs=placed,
        out_specs=(
            P("dp", None),
            P(("dp", "tensor"), None),
            P(),
            P(None, "tensor"),
            P(None, "tensor"),
            P(),
            P(None, "tensor"),
            P(None, "tensor"),
            P("tensor"),
            P(),
            P(),
            P("tensor"),
            P("tensor"),
            P("tensor"),
            P("tensor"),
            P("tensor", None),
        ),
        check_vma=False,
    )
```

```python
import functools

import jax
import jax.numpy as jnp
import numpy as np
from jax import lax
from jax.experimental import pallas as pl
from jax.experimental.pallas import tpu as pltpu
from jax.sharding import PartitionSpec as P

D = 1536
INNER = 3072
EPS = 1e-05
BLOCK = 128
LANES = 128
FAR = -1e30
F32 = jnp.float32
BF16 = jnp.bfloat16
CHUNK = 256
STEP = 128
ROWS = 32
VMEM_LIMIT = 63 * 2**20
SMALL_COST = pl.CostEstimate(flops=1, bytes_accessed=1, transcendentals=0)
PIECES = (1, 3)


def matmul(left, right, dims=(1, 0)):
    return lax.dot_general(
        left, right, (((dims[0],), (dims[1],)), ((), ())), preferred_element_type=F32
    )


def exact(left, right):
    return lax.dot_general(
        left,
        right,
        (((1,), (0,)), ((), ())),
        precision=lax.Precision.HIGHEST,
        preferred_element_type=F32,
    )


def sigmoid(v):
    return 0.5 * jnp.tanh(0.5 * v) + 0.5


def softplus(v):
    return jnp.maximum(v, 0.0) + jnp.log1p(jnp.exp(-jnp.abs(v)))


def fold(x):
    return x.reshape(x.shape[0] // 8, 8, x.shape[1]).sum(axis=0)


def triangle(lower):
    row = lax.broadcasted_iota(jnp.int32, (BLOCK, BLOCK), 0)
    col = lax.broadcasted_iota(jnp.int32, (BLOCK, BLOCK), 1)
    return jnp.where(row >= col if lower else row <= col, 1.0, 0.0).astype(F32)


def group_sum(x, spread):
    high = x.astype(BF16)
    low = (x - high.astype(F32)).astype(BF16)
    return matmul(high, spread) + matmul(low, spread)


def upright(rows):
    fill = jnp.zeros((BLOCK - rows.shape[0], BLOCK), F32)
    return jnp.concatenate([rows, fill], axis=0).T


def segment_columns(seg_ref, block, blocks, ahead):
    part = lambda k: seg_ref[:, pl.ds(pl.multiple_of(k * BLOCK, BLOCK), BLOCK)].astype(F32)
    ids = part(block)
    before = jnp.where(block > 0, part(jnp.maximum(block - 1, 0)), -1.0)
    lane = lax.broadcasted_iota(jnp.int32, (1, BLOCK), 1)
    rows = [ids]
    if ahead:
        behind = jnp.where(block < blocks - 1, part(jnp.minimum(block + 1, blocks - 1)), -1.0)
    for far in range(1, 4):
        if ahead:
            moved = jnp.where(
                lane >= BLOCK - far,
                pltpu.roll(behind, BLOCK - far, 1),
                pltpu.roll(ids, BLOCK - far, 1),
            )
        else:
            moved = jnp.where(lane < far, pltpu.roll(before, far, 1), pltpu.roll(ids, far, 1))
        rows.append(jnp.where(moved == ids, 1.0, 0.0))
    rows.append(jnp.where(ids == before[:, BLOCK - 1 :], 1.0, 0.0))
    rows.append(jnp.where(ids == ids[:, BLOCK - 1 :], 1.0, 0.0))
    rows.append(jnp.zeros((2, BLOCK), F32))
    return upright(jnp.concatenate(rows, axis=0)), ids


def decay_terms(step_raw, step_bias, rate, cols, seg_row):
    steps = softplus(step_raw + step_bias)
    rates = -steps * rate
    local = exact(triangle(True), rates)
    last = local[BLOCK - 1 :]
    into = jnp.exp(jnp.where(cols[:, 4:5] > 0.5, local, FAR))
    out = jnp.exp(jnp.where(cols[:, 5:6] > 0.5, last - local, FAR))
    row = lax.broadcasted_iota(jnp.int32, (BLOCK, BLOCK), 0)
    col = lax.broadcasted_iota(jnp.int32, (BLOCK, BLOCK), 1)
    allowed = jnp.logical_and(row >= col, cols[:, 0:1] == seg_row)
    bias = jnp.where(allowed, 0.0, FAR)
    return steps, rates, local, local.T, into, out, bias


def pairwise(x, pair, half):
    return jnp.where(half, x[:, 2 * pair : 2 * pair + 1], x[:, 2 * pair + 1 : 2 * pair + 2])


def split_pair(x, half):
    zero = jnp.zeros_like(x)
    return jnp.concatenate([jnp.where(half, x, zero), jnp.where(half, zero, x)], axis=0)


def decay_of(local, local_t, bias, head):
    return jnp.exp(local[:, head : head + 1] - local_t[head : head + 1, :] + bias)


def sum_over_places(place, own, others):
    parts = len(others) + 1
    total = None
    for k in range(parts):
        value = own
        for turn in range(1, parts):
            value = jnp.where((place - k + parts) % parts == turn, others[turn - 1], value)
        total = value if total is None else total + value
    return total


GAIN_ROW, KERNEL_ROW, BIAS_ROW, GATED_ROW, SKIP_ROW = 0, 2, 6, 7, 8
STATE_KERNEL_ROW, STATE_BIAS_ROW, STEP_ROW, DECAY_ROW = 9, 13, 14, 15


def run_pack(place, *arrays):
    channels = arrays[1].shape[1]

    def kernel(place_ref, *refs):
        (norm_gain, kernel, bias, gated, skip, state_kernel, state_bias, step_bias, decay, step_w) = refs[
            :10
        ]
        table, wide, placed = refs[10:]
        table[...] = jnp.zeros_like(table)
        table[GAIN_ROW : GAIN_ROW + 1, :] = norm_gain[:channels].reshape(1, channels)
        table[GAIN_ROW + 1 : GAIN_ROW + 2, :] = norm_gain[channels:].reshape(1, channels)
        table[KERNEL_ROW : KERNEL_ROW + 4, :] = kernel[...]
        table[STATE_KERNEL_ROW : STATE_KERNEL_ROW + 4, : state_kernel.shape[1]] = state_kernel[...]
        rows = ((BIAS_ROW, bias), (GATED_ROW, gated), (SKIP_ROW, skip), (STATE_BIAS_ROW, state_bias))
        for row, ref in rows + ((STEP_ROW, step_bias), (DECAY_ROW, decay)):
            size = ref.shape[0]
            table[row : row + 1, :size] = ref[...].reshape(1, size)
        rows = step_w[...].astype(F32)
        fill = jnp.zeros((LANES - rows.shape[0], rows.shape[1]), F32)
        columns = jnp.concatenate([rows, fill], axis=0).T
        wide[...] = columns.astype(BF16)
        placed[...] = pltpu.roll(columns, place_ref[0] * rows.shape[0], 1).astype(BF16)

    return pl.pallas_call(
        kernel,
        out_shape=[
            jax.ShapeDtypeStruct((16, channels), F32),
            jax.ShapeDtypeStruct((arrays[-1].shape[1], LANES), BF16),
            jax.ShapeDtypeStruct((arrays[-1].shape[1], LANES), BF16),
        ],
        in_specs=[pl.BlockSpec(memory_space=pltpu.SMEM)]
        + [pl.BlockSpec(memory_space=pltpu.VMEM) for _ in arrays],
        cost_estimate=SMALL_COST,
        name="pack",
    )(place, *arrays)


def forward_kernel(first_piece, unused, block_base, chunks, *refs):
    tokens, cot, seg, par, gate_w, value_w, state_w, step_w, out_w = refs[:9]
    refs = refs[9:]
    if not first_piece:
        state_in, tail_in, state_tail_in = refs[:3]
        refs = refs[3:]
    refs = refs[unused:]
    (
        gate_out,
        vraw_out,
        pv_out,
        y_out,
        sraw_out,
        spv_out,
        step_out,
        saved_out,
        stats_out,
        normed_out,
        state,
        tail_out,
        state_tail_out,
    ) = refs[:13]
    partial_outs = refs[13 : 13 + chunks]
    vbuf, sbuf, scaled, partial = refs[13 + chunks :]
    size = tokens.shape[0]
    channels = gate_w.shape[1]
    states = 2 * LANES

    @pl.when(pl.program_id(0) == 0)
    def _():
        if first_piece:
            state[...] = jnp.zeros_like(state)
            vbuf[:8] = jnp.zeros((8, channels), F32)
            sbuf[:8] = jnp.zeros((8, states), F32)
        else:
            state[...] = state_in[...]
            vbuf[:8] = tail_in[...]
            sbuf[:8] = state_tail_in[...]

    norm_gain = jnp.concatenate([par[GAIN_ROW : GAIN_ROW + 1], par[GAIN_ROW + 1 : GAIN_ROW + 2]], axis=1)
    scales = []
    for row in range(0, size, ROWS):
        wide = tokens[row : row + ROWS].astype(F32)
        scale = lax.rsqrt(jnp.mean(wide * wide, axis=-1, keepdims=True) + EPS)
        normed_out[row : row + ROWS] = (wide * scale * norm_gain).astype(BF16)
        scales.append(scale)
    normed = normed_out[...]
    vbuf[8:] = matmul(normed, value_w[...])
    sbuf[8:] = matmul(normed, state_w[...])
    step_out[...] = matmul(normed, step_w[...])
    gate_out[...] = matmul(normed, gate_w[...])

    def conv(buf, row, lanes, cols, kernel_row, bias_row):
        raw = buf[row + 8 : row + 8 + BLOCK, lanes]
        total = par[bias_row : bias_row + 1, lanes] + raw * par[kernel_row + 3 : kernel_row + 4, lanes]
        for back in range(1, 4):
            tap = par[kernel_row + 3 - back : kernel_row + 4 - back, lanes]
            moved = buf[row + 8 - back : row + 8 - back + BLOCK, lanes]
            total = total + moved * tap * cols[:, back : back + 1]
        return raw, total

    half = lax.broadcasted_iota(jnp.int32, (BLOCK, LANES), 1) < LANES // 2
    half_row = half[0:1]
    lane = lax.broadcasted_iota(jnp.int32, (BLOCK, LANES), 1)
    step_bias = par[STEP_ROW : STEP_ROW + 1, :LANES]
    rate = jnp.exp(par[DECAY_ROW : DECAY_ROW + 1, :LANES])
    skips = par[SKIP_ROW : SKIP_ROW + 1, :LANES]
    squares = []
    for sub in range(size // BLOCK):
        rows = slice(sub * BLOCK, (sub + 1) * BLOCK)
        row = sub * BLOCK
        block = block_base + pl.program_id(0) * (size // BLOCK) + sub
        cols, seg_row = segment_columns(seg, block, None, False)
        mixed_state = []
        for part in range(2):
            lanes = slice(part * LANES, (part + 1) * LANES)
            raw, spv = conv(sbuf, row, lanes, cols, STATE_KERNEL_ROW, STATE_BIAS_ROW)
            sraw_out[rows, lanes] = raw.astype(BF16)
            spv_out[rows, lanes] = spv
            mixed_state.append(spv * sigmoid(spv))
        b_low = mixed_state[0].astype(BF16)
        b_turned = mixed_state[0].T.astype(BF16)
        c_low = mixed_state[1].astype(BF16)
        steps, _, local, local_t, into, out, bias = decay_terms(
            step_out[rows], step_bias, rate, cols, seg_row
        )
        keep = into[BLOCK - 1 :]
        scores = matmul(c_low, b_low, (1, 1))
        square = jnp.zeros((BLOCK, LANES), F32)
        for pair in range(channels // LANES):
            lanes = slice(pair * LANES, (pair + 1) * LANES)
            raw, pv = conv(vbuf, row, lanes, cols, KERNEL_ROW, BIAS_ROW)
            vraw_out[rows, lanes] = raw.astype(BF16)
            pv_out[rows, lanes] = pv
            values = pv * sigmoid(pv)
            old = state[:, lanes]
            old_low = old.astype(BF16)
            saved_out[sub, :, lanes] = old_low
            u = values * pairwise(steps, pair, half)
            weights = [
                (scores * decay_of(local, local_t, bias, 2 * pair + k)).astype(BF16)
                for k in range(2)
            ]
            inner = matmul(jnp.concatenate(weights, axis=1), split_pair(u.astype(BF16), half))
            y_ssm = inner + matmul(c_low, old_low) * pairwise(into, pair, half)
            y_out[rows, lanes] = y_ssm
            leaving = (u * pairwise(out, pair, half)).astype(BF16)
            state[:, lanes] = old * pairwise(keep, pair, half_row) + matmul(b_turned, leaving)
            gate = gate_out[rows, lanes]
            gated = (y_ssm + pairwise(skips, pair, half_row) * values) * (gate * sigmoid(gate))
            square = square + gated * gated
            scaled[rows, lanes] = (gated * par[GATED_ROW : GATED_ROW + 1, lanes]).astype(BF16)
        squares.append(jnp.sum(square, axis=-1, keepdims=True))
    vbuf[:8] = vbuf[size:]
    sbuf[:8] = sbuf[size:]
    tail_out[...] = vbuf[:8]
    state_tail_out[...] = sbuf[:8]
    partial[...] = matmul(scaled[...], out_w[...])
    steps_each = pl.num_programs(0) // chunks
    for index, partial_out in enumerate(partial_outs):

        @pl.when(pl.program_id(0) // steps_each == index)
        def _(partial_out=partial_out):
            partial_out[...] = partial[...]

    products = [
        jnp.sum(cot[row : row + ROWS].astype(F32) * partial[row : row + ROWS], axis=-1, keepdims=True)
        for row in range(0, size, ROWS)
    ]
    per = BLOCK // ROWS
    for sub in range(size // BLOCK):
        product = jnp.concatenate(products[sub * per : (sub + 1) * per], axis=0)
        scale = jnp.concatenate(scales[sub * per : (sub + 1) * per], axis=0)
        table = jnp.where(
            lane == 0, squares[sub], jnp.where(lane == 1, product, jnp.where(lane == 2, scale, 0.0))
        )
        stats_out[:, sub * BLOCK : (sub + 1) * BLOCK] = table.T[:8]


def backward_kernel(first_piece, unused, block_base, blocks, *refs):
    (
        place_ref,
        og_ref,
        gate_ref,
        vraw_ref,
        pv_ref,
        y_ref,
        sraw_ref,
        spv_ref,
        step_ref,
        own_stats,
        stats_1,
        stats_2,
        stats_3,
        saved_ref,
        seg,
        par,
    ) = refs[:16]
    refs = refs[16:]
    if not first_piece:
        carried_in = refs[:6]
        refs = refs[6:]
    refs = refs[unused:]
    (
        low_out,
        mixed_out,
        state_out,
        tail_out,
        state_tail_out,
        wide_acc,
        narrow_acc,
        heads_acc,
    ) = refs
    channels = gate_ref.shape[1]
    place = place_ref[0]

    @pl.when(pl.program_id(0) == 0)
    def _():
        outs = (state_out, tail_out, state_tail_out, wide_acc, narrow_acc, heads_acc)
        for k, ref in enumerate(outs):
            ref[...] = jnp.zeros_like(ref) if first_piece else carried_in[k][...]

    block = block_base + pl.num_programs(0) - 1 - pl.program_id(0)
    cols, seg_row = segment_columns(seg, block, blocks, True)
    stats = sum_over_places(place, own_stats[...], [stats_1[...], stats_2[...], stats_3[...]])
    stats = upright(stats)
    strength = lax.rsqrt(stats[:, 0:1] / INNER + EPS)
    pull = strength * strength * strength * stats[:, 1:2] / INNER

    half = lax.broadcasted_iota(jnp.int32, (BLOCK, LANES), 1) < LANES // 2
    half_row = half[0:1]
    spv = [spv_ref[:, :LANES], spv_ref[:, LANES:]]
    spv_sig = [sigmoid(v) for v in spv]
    b_part = spv[0] * spv_sig[0]
    c_part = spv[1] * spv_sig[1]
    b_low = b_part.astype(BF16)
    c_low = c_part.astype(BF16)
    c_turned = c_part.T.astype(BF16)
    step_raw = step_ref[...]
    step_bias = par[STEP_ROW : STEP_ROW + 1, :LANES]
    rate = jnp.exp(par[DECAY_ROW : DECAY_ROW + 1, :LANES])
    skips = par[SKIP_ROW : SKIP_ROW + 1, :LANES]
    steps, rates, local, local_t, into, out, bias = decay_terms(
        step_raw, step_bias, rate, cols, seg_row
    )
    keep = into[BLOCK - 1 :]
    scores = matmul(c_low, b_low, (1, 1))

    def conv_back(pre_grad, raw, lanes, after, kernel_row, acc):
        ext = jnp.concatenate([pre_grad, after[:, lanes]], axis=0)
        after[:, lanes] = pre_grad[:8]
        total = pre_grad * par[kernel_row + 3 : kernel_row + 4, lanes]
        acc[24:32, lanes] += fold(raw * pre_grad)
        acc[32:40, lanes] += fold(pre_grad)
        for ahead in range(1, 4):
            moved = pltpu.roll(ext, BLOCK + 8 - ahead, 0)[:BLOCK]
            term = moved * cols[:, ahead : ahead + 1]
            total = total + term * par[kernel_row + 3 - ahead : kernel_row + 4 - ahead, lanes]
            acc[8 * (3 - ahead) : 8 * (4 - ahead), lanes] += fold(raw * term)
        return total

    score_grad = jnp.zeros((BLOCK, BLOCK), F32)
    b_grad = jnp.zeros((BLOCK, LANES), F32)
    c_grad = jnp.zeros((BLOCK, LANES), F32)
    spread_dl = jnp.zeros((BLOCK, LANES), F32)
    spread_ds = jnp.zeros((BLOCK, LANES), F32)
    spread_end = jnp.zeros((8, LANES), F32)
    for pair in range(channels // LANES):
        lanes = slice(pair * LANES, (pair + 1) * LANES)
        spread = (
            lax.broadcasted_iota(jnp.int32, (LANES, LANES), 0) // (LANES // 2) + 2 * pair
            == lax.broadcasted_iota(jnp.int32, (LANES, LANES), 1)
        ).astype(BF16)
        gain = par[GATED_ROW : GATED_ROW + 1, lanes]
        skip = pairwise(skips, pair, half_row)
        gate = gate_ref[:, lanes]
        gate_sig = sigmoid(gate)
        gate_silu = gate * gate_sig
        pv = pv_ref[:, lanes]
        pv_sig = sigmoid(pv)
        values = pv * pv_sig
        og = og_ref[:, lanes]
        y_ssm = y_ref[:, lanes]
        y = y_ssm + skip * values
        gated = y * gate_silu
        strong = gated * strength
        mixed_out[:, lanes] = (strong * gain).astype(BF16)
        gated_grad = gain * strength * og - gated * pull
        low_out[:, lanes] = (
            gated_grad * y * (gate_sig * (1.0 + gate * (1.0 - gate_sig)))
        ).astype(BF16)
        grad = gated_grad * gate_silu
        wide_acc[40:48, lanes] += fold(og * strong)
        wide_acc[48:56, lanes] += fold(grad * values)

        state_grad = state_out[:, lanes]
        state_grad_low = state_grad.astype(BF16)
        old_low = saved_ref[0, :, lanes]
        pair_steps = pairwise(steps, pair, half)
        pair_out = pairwise(out, pair, half)
        u = values * pair_steps
        u_low = u.astype(BF16)
        g_low = grad.astype(BF16)
        g_split = split_pair(g_low, half)
        decays = [decay_of(local, local_t, bias, 2 * pair + k) for k in range(2)]
        weights = jnp.concatenate([(scores * d).astype(BF16) for d in decays], axis=0)
        weight_grad = matmul(g_split, u_low, (1, 1))
        score_grad = score_grad + weight_grad[:BLOCK] * decays[0] + weight_grad[BLOCK:] * decays[1]
        u_grad_out = matmul(b_low, state_grad_low) * pair_out
        u_grad = matmul(weights, g_split, (0, 0)) + u_grad_out
        u_near = u_low.astype(F32)
        spread_dl = spread_dl + group_sum(g_low.astype(F32) * y_ssm - u_near * u_grad, spread)
        spread_ds = spread_ds + group_sum(values * u_grad, spread)
        keep_row = pairwise(keep, pair, half_row)
        spread_end = spread_end + group_sum(
            fold(u_near * u_grad_out) + fold(state_grad * old_low.astype(F32)) * keep_row, spread
        )
        entering = (grad * pairwise(into, pair, half)).astype(BF16)
        leaving = (u * pair_out).astype(BF16)
        c_grad = c_grad + matmul(entering, old_low, (1, 1))
        b_grad = b_grad + matmul(leaving, state_grad_low, (1, 1))
        state_out[:, lanes] = state_grad * keep_row + matmul(c_turned, entering)
        pre_grad = (pair_steps * u_grad + skip * grad) * (pv_sig * (1.0 + pv * (1.0 - pv_sig)))
        raw_grad = conv_back(
            pre_grad, vraw_ref[:, lanes].astype(F32), lanes, tail_out, KERNEL_ROW, wide_acc
        )
        low_out[:, channels + pair * LANES : channels + (pair + 1) * LANES] = raw_grad.astype(BF16)
    score_low = score_grad.astype(BF16)
    c_grad = c_grad + matmul(score_low, b_low)
    b_grad = b_grad + matmul(score_low, c_low, (0, 0))
    rate_grad = exact(triangle(False), spread_dl) + jnp.sum(spread_end, axis=0, keepdims=True)
    step_grad = (spread_ds - rate * rate_grad) * sigmoid(step_raw + step_bias)
    heads_acc[0:8] += fold(step_grad)
    heads_acc[8:16] += fold(rates * rate_grad)
    for part, grad in enumerate((b_grad, c_grad)):
        lanes = slice(part * LANES, (part + 1) * LANES)
        pre_grad = grad * (spv_sig[part] * (1.0 + spv[part] * (1.0 - spv_sig[part])))
        raw_grad = conv_back(
            pre_grad, sraw_ref[:, lanes].astype(F32), lanes, state_tail_out, STATE_KERNEL_ROW, narrow_acc
        )
        at = 2 * channels + part * LANES
        low_out[:, at : at + LANES] = raw_grad.astype(BF16)
    heads_here = channels // (LANES // 2)
    low_out[:, 2 * channels + 2 * LANES :] = pltpu.roll(step_grad, place * heads_here, 1).astype(BF16)


def out_grad_kernel(unused, cot, out_w, *refs):
    og, token = refs[unused : unused + 2]
    og[...] = matmul(cot[...], out_w[...], (1, 1))
    token[...] = jnp.zeros((8, LANES), F32)


def run_out_grad(chain, cot, out_w, passes):
    length, channels = cot.shape[0], out_w.shape[0]
    deps = chain.deps()
    results = pl.pallas_call(
        functools.partial(out_grad_kernel, len(deps) + len(passes)),
        grid=(length // CHUNK,),
        in_specs=[pl.BlockSpec((CHUNK, D), lambda i: (i, 0)), whole(out_w.shape)]
        + [ANYWHERE for _ in deps + passes],
        out_specs=[pl.BlockSpec((CHUNK, channels), lambda i: (i, 0)), whole((8, LANES))]
        + [ANYWHERE for _ in passes],
        out_shape=[
            jax.ShapeDtypeStruct((length, channels), F32),
            jax.ShapeDtypeStruct((8, LANES), F32),
        ]
        + [jax.ShapeDtypeStruct(p.shape, p.dtype) for p in passes],
        input_output_aliases={2 + len(deps) + k: 2 + k for k in range(len(passes))},
        compiler_params=pltpu.CompilerParams(vmem_limit_bytes=VMEM_LIMIT),
        cost_estimate=SMALL_COST,
        name="out_grad",
    )(cot, out_w, *deps, *passes)
    chain.last = results[1]
    return results[0], results[2:]


def run_matmul(chain, body, ins, outs, count, scratch=(), name=None):
    deps = chain.deps()
    arrays = [a for a, _, _ in ins]

    def kernel(*refs):
        body(*refs[: len(arrays)], *refs[len(arrays) + len(deps) :])
        refs[len(arrays) + len(deps) + len(outs)][...] = jnp.zeros((8, LANES), F32)

    results = pl.pallas_call(
        kernel,
        grid=(count,),
        in_specs=[whole(a.shape) if m is None else pl.BlockSpec(b, m) for a, b, m in ins]
        + [ANYWHERE for _ in deps],
        out_specs=[pl.BlockSpec(b, m) for _, b, m in outs] + [whole((8, LANES))],
        out_shape=[jax.ShapeDtypeStruct(s, F32) for s, _, _ in outs]
        + [jax.ShapeDtypeStruct((8, LANES), F32)],
        scratch_shapes=list(scratch),
        compiler_params=pltpu.CompilerParams(vmem_limit_bytes=VMEM_LIMIT),
        cost_estimate=SMALL_COST,
        name=name,
    )(*arrays, *deps)
    chain.last = results[-1]
    return results[:-1]


def gain_row(value, count):
    out = []
    for k in range(count // BLOCK):
        column = jnp.sum(value[k * BLOCK : (k + 1) * BLOCK], axis=-1, keepdims=True)
        out.append(jnp.broadcast_to(column, (BLOCK, BLOCK)).T[:8])
    return jnp.concatenate(out, axis=1)


def run_rest_grad(chain, normed, low, small_rows, weights):
    width = small_rows.shape[1]
    count = D // CHUNK
    states = weights[0].shape[1]

    def body(left, right, extra, state_w, step_w, out, gain, token):
        @pl.when(pl.program_id(0) < count)
        def _():
            value = matmul(left[...], right[...], (0, 0))
            out[...] = value
            both = jnp.concatenate([state_w[...], step_w[...]], axis=1).astype(F32)
            gain[...] = gain_row(value * both, CHUNK)

        @pl.when(pl.program_id(0) == count)
        def _():
            out[...] = extra[...]

    length, total = low.shape
    held = lambda i: jnp.minimum(i, count - 1)
    tile = lambda a: (a, (CHUNK, a.shape[1]), lambda i: (held(i), 0))
    return run_matmul(
        chain,
        body,
        [
            (normed, (length, CHUNK), lambda i: (0, held(i))),
            (low, (length, width), lambda i: (0, total // width - 1)),
            (small_rows, None, None),
            *[tile(w) for w in weights],
        ],
        [
            ((D + CHUNK, width), (CHUNK, width), lambda i: (i, 0)),
            ((8, D), (8, CHUNK), lambda i: (0, held(i))),
        ],
        count + 1,
        name="rest_grad",
    )


def run_weight_grads(chain, core, normed, low, cot, mixed, weights, gains, unit):
    length = normed.shape[0]
    channels = mixed.shape[1]
    tile = D // 4
    deps = chain.deps()

    def which(i, p):
        return jnp.where(i < 2, 1 - p[0], p[0]) * 2 + i % 2

    def kernel(place, left, right, cots, mix, gate_w, value_w, gain_in, *refs):
        outs, gain, token = refs[len(deps) : len(deps) + 4], refs[-2], refs[-1]
        i = pl.program_id(0)

        @pl.when(i == 0)
        def _():
            gain[...] = gain_in[...]
            token[...] = jnp.zeros((8, LANES), F32)

        gate = matmul(left[...], right[:, :channels], (0, 0))
        value = matmul(left[...], right[:, channels:], (0, 0))
        out = matmul(cots[...], mix[...], (0, 0))
        at = pl.ds(pl.multiple_of(which(i, place) * tile, LANES), tile)
        products = gate * gate_w[...].astype(F32) + value * value_w[...].astype(F32)
        gain[:, at] = gain[:, at] + gain_row(products, tile)
        for k in range(4):

            @pl.when(i == k)
            def _(k=k):
                for n in range(tile // unit):
                    rows = slice(n * unit, (n + 1) * unit)
                    for m, part in enumerate((gate, value, out)):
                        first = (3 * n + m) * unit
                        outs[k][first : first + unit, :] = part[rows]

    lanes = lambda i, p: (0, which(i, p))
    weight_spec = pl.BlockSpec((tile, channels), lambda i, p: (which(i, p), 0))
    results = pl.pallas_call(
        kernel,
        grid_spec=pltpu.PrefetchScalarGridSpec(
            num_scalar_prefetch=1,
            grid=(4,),
            in_specs=[
                pl.BlockSpec((length, tile), lanes),
                pl.BlockSpec((length, 2 * channels), lambda i, p: (0, 0)),
                pl.BlockSpec((length, tile), lanes),
                whole(mixed.shape),
                weight_spec,
                weight_spec,
                whole(gains.shape),
            ]
            + [ANYWHERE for _ in deps],
            out_specs=[whole((3 * tile, channels))] * 4 + [whole(gains.shape), whole((8, LANES))],
        ),
        out_shape=[jax.ShapeDtypeStruct((3 * tile, channels), F32)] * 4
        + [jax.ShapeDtypeStruct(gains.shape, F32), jax.ShapeDtypeStruct((8, LANES), F32)],
        compiler_params=pltpu.CompilerParams(vmem_limit_bytes=VMEM_LIMIT),
        cost_estimate=SMALL_COST,
        name="weight_grads",
    )(core, normed, low, cot, mixed, *weights, gains, *deps)
    chain.last = results[-1]
    return results[:4], results[4]


def run_assemble(chain, core, own, got, unit):
    rows, channels = own[0].shape
    tile = rows // 3
    deps = chain.deps()

    def kernel(place, own_a, own_b, got_a, got_b, *refs):
        gate, value, out, token = refs[len(deps) :]
        i = pl.program_id(0)
        token[...] = jnp.zeros((8, LANES), F32)
        for n, (mine, other) in enumerate(((own_a, got_a), (own_b, got_b))):

            @pl.when(i % 2 == n)
            def _(mine=mine, other=other):
                use_own = i // 2 == place[0]
                pieces = []
                for k in range(rows // unit):
                    at = slice(k * unit, (k + 1) * unit)
                    pieces.append(jnp.where(use_own, mine[at, :], other[at, :]))
                gate[...] = jnp.concatenate(pieces[0::3], axis=0)
                value[...] = jnp.concatenate(pieces[1::3], axis=0)
                out[...] = jnp.concatenate(pieces[2::3], axis=0).T

    row = pl.BlockSpec((tile, channels), lambda i, p: (i, 0))
    gate, value, out, chain.last = pl.pallas_call(
        kernel,
        grid_spec=pltpu.PrefetchScalarGridSpec(
            num_scalar_prefetch=1,
            grid=(4,),
            in_specs=[whole(own[0].shape)] * 4 + [ANYWHERE for _ in deps],
            out_specs=[
                row,
                row,
                pl.BlockSpec((channels, tile), lambda i, p: (0, i)),
                whole((8, LANES)),
            ],
        ),
        out_shape=[
            jax.ShapeDtypeStruct((D, channels), F32),
            jax.ShapeDtypeStruct((D, channels), F32),
            jax.ShapeDtypeStruct((channels, D), F32),
            jax.ShapeDtypeStruct((8, LANES), F32),
        ],
        compiler_params=pltpu.CompilerParams(vmem_limit_bytes=VMEM_LIMIT),
        cost_estimate=SMALL_COST,
        name="assemble",
    )(core, *own, *got, *deps)
    return gate, value, out


def run_total(chain, low, weights):
    length, width = low.shape

    def body(left, gate_w, value_w, state_w, step_w, out, token, joined):
        @pl.when(pl.program_id(0) == 0)
        def _():
            at = 0
            for ref in (gate_w, value_w, state_w, step_w):
                joined[:, at : at + ref.shape[1]] = ref[...]
                at += ref.shape[1]

        out[...] = matmul(left[...], joined[...], (1, 1))

    (out,) = run_matmul(
        chain,
        body,
        [(low, (CHUNK, width), lambda i: (i, 0))] + [(w, None, None) for w in weights],
        [((length, D), (CHUNK, D), lambda i: (i, 0))],
        length // CHUNK,
        scratch=[pltpu.VMEM((D, width), BF16)],
        name="normed_grad",
    )
    return out


def whole(shape):
    return pl.BlockSpec(shape, lambda i, *_: (0,) * len(shape))


ANYWHERE = pl.BlockSpec(memory_space=pl.ANY)


def run_forward(start, count, chunks, tokens, cot, seg, small, carried, kept, deps):
    channels = small["gate_w"].shape[1]
    states = 2 * LANES
    size = CHUNK
    length = count * size
    first = start // size
    per = size // BLOCK
    full = tokens.shape[0]

    def row_in(width):
        return pl.BlockSpec((size, width), lambda i: (first + i, 0))

    def row_out(width):
        return pl.BlockSpec((size, width), lambda i: (i, 0))

    def chunk_out(index):
        each = count // chunks
        return pl.BlockSpec((size, D), lambda i: (jnp.clip(i - index * each, 0, each - 1), 0))

    constant = [small[n] for n in ("par", "gate_w", "value_w", "state_w", "step_w", "out_w")]
    carry_shapes = [(LANES, channels), (8, channels), (8, states)]
    widths = (
        (channels, F32),
        (channels, BF16),
        (channels, F32),
        (channels, F32),
        (states, BF16),
        (states, F32),
        (LANES, F32),
    )
    inputs = [tokens, cot, seg, *constant, *carried, *deps, *kept]
    outs = pl.pallas_call(
        functools.partial(
            forward_kernel, not carried, len(deps) + len(kept), start // BLOCK, chunks
        ),
        grid=(count,),
        in_specs=[row_in(D), row_in(D), whole(seg.shape)]
        + [whole(c.shape) for c in constant]
        + [whole(c.shape) for c in carried]
        + [ANYWHERE for _ in deps + kept],
        out_specs=[row_out(w) for w, _ in widths]
        + [pl.BlockSpec((per, LANES, channels), lambda i: (i, 0, 0))]
        + [pl.BlockSpec((8, size), lambda i: (0, first + i))]
        + [row_in(D)]
        + [whole(c) for c in carry_shapes]
        + [chunk_out(index) for index in range(chunks)],
        out_shape=[jax.ShapeDtypeStruct((length, w), k) for w, k in widths]
        + [jax.ShapeDtypeStruct((length // BLOCK, LANES, channels), BF16)]
        + [jax.ShapeDtypeStruct((8, full), F32)]
        + [jax.ShapeDtypeStruct((full, D), BF16)]
        + [jax.ShapeDtypeStruct(c, F32) for c in carry_shapes]
        + [jax.ShapeDtypeStruct((length // chunks, D), F32)] * chunks,
        scratch_shapes=[
            pltpu.VMEM((size + 8, channels), F32),
            pltpu.VMEM((size + 8, states), F32),
            pltpu.VMEM((size, channels), BF16),
            pltpu.VMEM((size, D), F32),
        ],
        input_output_aliases={len(inputs) - len(kept) + k: 8 + k for k in range(len(kept))},
        compiler_params=pltpu.CompilerParams(vmem_limit_bytes=VMEM_LIMIT),
        cost_estimate=SMALL_COST,
        name="forward_piece",
    )(*inputs)
    outs = list(outs)
    names = ("gate", "vraw", "pv", "y", "sraw", "spv", "step", "saved")
    return dict(zip(names, outs[:8])), outs[8:10], outs[10:13], outs[13:]


def run_backward(start, piece, og, stats, place, seg, small, carried, low, mixed, deps):
    channels = small["gate_w"].shape[1]
    length = piece["gate"].shape[0]
    full = og.shape[0]
    count = length // BLOCK
    first = start // BLOCK
    flip = lambda i: count - 1 - i

    def row(width):
        return pl.BlockSpec((BLOCK, width), lambda i, *_: (flip(i), 0))

    def shared(width):
        return pl.BlockSpec((BLOCK, width), lambda i, *_: (first + flip(i), 0))

    names = ("gate", "vraw", "pv", "y", "sraw", "spv", "step")
    ins = [piece[n] for n in names]
    low_width = 2 * channels + 3 * LANES
    kept = [] if low is None else [low, mixed]
    carry_shapes = [
        (LANES, channels),
        (8, channels),
        (8, 2 * LANES),
        (56, channels),
        (40, 2 * LANES),
        (16, LANES),
    ]
    inputs = [og, *ins, *stats, piece["saved"], seg, small["par"], *carried, *deps, *kept]
    outs = pl.pallas_call(
        functools.partial(
            backward_kernel, not carried, len(deps) + len(kept), first, full // BLOCK
        ),
        grid_spec=pltpu.PrefetchScalarGridSpec(
            num_scalar_prefetch=1,
            grid=(count,),
            in_specs=[shared(channels)]
            + [row(a.shape[1]) for a in ins]
            + [pl.BlockSpec((8, BLOCK), lambda i, *_: (0, first + flip(i))) for _ in stats]
            + [pl.BlockSpec((1, LANES, channels), lambda i, *_: (flip(i), 0, 0))]
            + [whole(seg.shape), whole(small["par"].shape)]
            + [whole(c.shape) for c in carried]
            + [ANYWHERE for _ in deps + kept],
            out_specs=[shared(low_width), shared(channels)] + [whole(c) for c in carry_shapes],
        ),
        out_shape=[
            jax.ShapeDtypeStruct((full, low_width), BF16),
            jax.ShapeDtypeStruct((full, channels), BF16),
        ]
        + [jax.ShapeDtypeStruct(c, F32) for c in carry_shapes],
        compiler_params=pltpu.CompilerParams(vmem_limit_bytes=VMEM_LIMIT),
        cost_estimate=SMALL_COST,
        input_output_aliases={1 + len(inputs) - 2 + k: k for k in range(len(kept))},
        name="backward_piece",
    )(place, *inputs)
    return outs[0], outs[1], list(outs[2:])


class Chain:
    def __init__(self):
        self.last = None
        self.more = []

    def deps(self):
        found = ([] if self.last is None else [self.last]) + self.more
        self.more = []
        return found


def rowwise(
    chain, place, body, ins, outs, rows, passes=(), step=0, whole_place=False, name=None
):
    step = step or STEP
    steps = rows // step

    def spec(width, first, most=steps, where=None):
        if where is not None:
            base = first if callable(first) else lambda p: first
            return pl.BlockSpec(
                (step, width),
                lambda i, p: (
                    jnp.where(where(p[0]), base(p[0]) + jnp.minimum(i, most - 1), 0),
                    0,
                ),
            )
        if callable(first):
            return pl.BlockSpec(
                (step, width),
                lambda i, p: (
                    jnp.maximum(first(p if whole_place else p[0]) + jnp.minimum(i, most - 1), 0),
                    0,
                ),
            )
        return pl.BlockSpec((step, width), lambda i, p: (first + jnp.minimum(i, most - 1), 0))

    def lying(height, first):
        if callable(first):
            return pl.BlockSpec((height, STEP), lambda i, p: (0, first(p[0]) + i))
        return pl.BlockSpec((height, STEP), lambda i, p: (0, first + i))

    def spec_of(array, first, across=False, most=steps, where=None):
        if first is None:
            return fixed(array.shape)
        return lying(array.shape[0], first) if across else spec(array.shape[1], first, most, where)

    def fixed(shape):
        return pl.BlockSpec(shape, lambda i, p: (0,) * len(shape))

    anywhere = pl.BlockSpec(memory_space=pl.ANY)
    arrays = [entry[0] for entry in ins]
    in_specs = [spec_of(*entry) for entry in ins]
    kept = [(k, o[4]) for k, o in enumerate(outs) if o[4] is not None]
    deps = chain.deps()
    inputs = [*arrays, *[a for _, a in kept], *passes, *deps]
    aliases = {1 + len(arrays) + n: k for n, (k, _) in enumerate(kept)}
    for n in range(len(passes)):
        aliases[1 + len(arrays) + len(kept) + n] = len(outs) + n

    def kernel(place_ref, *refs):
        results = refs[len(inputs) :]
        values = body(place_ref if whole_place else place_ref[0], *refs[: len(arrays)])
        for ref, value in zip(results[: len(outs)], values):
            ref[...] = value
        results[-1][...] = jnp.zeros((8, LANES), F32)

    results = pl.pallas_call(
        kernel,
        grid_spec=pltpu.PrefetchScalarGridSpec(
            num_scalar_prefetch=1,
            grid=(steps,),
            in_specs=in_specs + [anywhere] * (len(inputs) - len(arrays)),
            out_specs=[spec(o[1], o[3], *o[5:]) for o in outs]
            + [anywhere] * len(passes)
            + [fixed((8, LANES))],
        ),
        out_shape=[jax.ShapeDtypeStruct((o[0], o[1]), o[2]) for o in outs]
        + [jax.ShapeDtypeStruct(p.shape, p.dtype) for p in passes]
        + [jax.ShapeDtypeStruct((8, LANES), F32)],
        input_output_aliases=aliases,
        compiler_params=pltpu.CompilerParams(vmem_limit_bytes=VMEM_LIMIT),
        cost_estimate=SMALL_COST,
        name=name,
    )(place, *inputs)
    chain.last = results[-1]
    return list(results[:-1])


def after(chain, *arrays):
    def kernel(*refs):
        refs[-1][...] = jnp.zeros((8, LANES), F32)

    anywhere = pl.BlockSpec(memory_space=pl.ANY)
    deps = chain.deps()
    results = pl.pallas_call(
        kernel,
        in_specs=[anywhere] * (len(arrays) + len(deps)),
        out_specs=[anywhere] * len(arrays) + [pl.BlockSpec(memory_space=pltpu.VMEM)],
        out_shape=[jax.ShapeDtypeStruct(a.shape, a.dtype) for a in arrays]
        + [jax.ShapeDtypeStruct((8, LANES), F32)],
        input_output_aliases={k: k for k in range(len(arrays))},
        cost_estimate=SMALL_COST,
        name="in_order",
    )(*arrays, *deps)
    chain.last = results[-1]
    return list(results[:-1])


INWARD = ((0, 1), (3, 2))
ACROSS = ((1, 2), (2, 1))
OUTWARD = ((1, 0), (2, 3))


def on_device(
    tokens,
    norm_gain,
    gate_weight,
    value_weight,
    state_weight,
    step_weight,
    value_kernel,
    value_bias,
    state_kernel,
    state_bias,
    step_bias,
    decay_log,
    skip_scale,
    gated_gain,
    out_weight,
    segment_ids,
    out_cotangent,
):
    parts = lax.axis_size("tensor")
    place = lax.axis_index("tensor")
    middle = jnp.logical_and(place > 0, place < parts - 1)
    length = tokens.shape[0]
    channels = gate_weight.shape[1]
    head_count = step_bias.shape[0]
    rows = length // parts
    states = 2 * LANES
    where = place.astype(jnp.int32)[None]
    par, step_wide, step_place = run_pack(
        where,
        norm_gain,
        value_kernel,
        value_bias,
        gated_gain,
        skip_scale,
        state_kernel,
        state_bias,
        step_bias,
        decay_log,
        step_weight.T,
    )
    small = {
        "gate_w": gate_weight,
        "value_w": value_weight,
        "state_w": state_weight,
        "step_w": step_wide,
        "out_w": out_weight,
        "par": par,
    }
    chain = Chain()
    send = lambda x, pairs: lax.ppermute(x, "tensor", pairs)
    run = functools.partial(rowwise, chain, where)
    steps = lambda n: n // STEP

    piece_spans = [p * length // sum(PIECES) for p in PIECES]
    piece_firsts = [sum(piece_spans[:k]) for k in range(len(piece_spans))]
    pieces = []
    partials = []
    spans = [length // sum(PIECES)] * sum(PIECES)
    firsts = [sum(spans[:k]) for k in range(len(spans))]
    carried = []
    kept = []
    late = {}
    count = len(spans)
    outer, inner, outer_sent, pair_sum = {}, {}, {}, {}

    def forward():
        nonlocal carried, kept
        k = len(pieces)
        outs, kept, carried, made = run_forward(
            piece_firsts[k],
            piece_spans[k] // CHUNK,
            PIECES[k],
            tokens,
            out_cotangent,
            segment_ids,
            small,
            carried,
            kept,
            chain.deps(),
        )
        partials.extend(made)
        pieces.append(outs)
        chain.last = carried[2]


    def send_outer(n, message, both=True):
        outer_sent[n] = message
        outer[n] = send(message, INWARD + OUTWARD if both else INWARD)

    is_middle = lambda p: jnp.logical_and(p > 0, p < parts - 1)
    per = steps(rows)
    at_ends = lambda low_end, high_end: lambda p: jnp.where(p < 2, low_end, high_end) * per

    def event(n, following=None, middle_segment=None):
        chunk = n < count
        step = STEP
        blocks = spans[0] // step
        size = spans[0]
        is_end = lambda p: jnp.logical_not(is_middle(p))
        if chunk:
            mine = (partials[n], 0, False, blocks, is_middle)
        else:
            mine = (late["total"], middle_segment, False, blocks, is_middle)
        ins = [mine, (outer[n], 0, False, blocks, is_middle)]
        outs = [(size, D, F32, 0, None, blocks, is_middle)]
        if n > 0:
            array, first = following
            from_middle = (inner[n], 0, False, blocks, is_middle)
            if n <= count:
                ins += [(pair_sum[n - 1], 0, False, blocks, is_middle), from_middle]
                ins += [(array, first, False, blocks, is_end)]
            else:
                ins += [(array, first, False, blocks), from_middle]
            outs.append((spans[0], D, F32, 0, None, blocks))

        def body(p, a, b, *others):
            value = a[...] + b[...]
            results = [value]
            if n > 0:
                message = others[0][...] + others[1][...]
                if n <= count:
                    message = jnp.where(is_middle(p), message, others[2][...])
                results.append(message)
            return results

        results = run(body, ins, outs, size, step=step, name="event")
        pair_sum[n] = results[0]
        inner[n + 1] = send(results[0], ACROSS)
        if n > 0:
            send_outer(n + 1, results[1])
        else:
            send_outer(1, following[0], False)

    def finish_chunk(k):
        def body(p, own, got, token, *stats):
            inside = jnp.logical_and(p > 0, p < parts - 1)
            total = jnp.where(inside, own[...], got[...])
            table = upright(sum_over_places(p, stats[0][...], [x[...] for x in stats[1:]]))
            strength = lax.rsqrt(table[:, 0:1] / INNER + EPS)
            return [(token[...].astype(F32) + total * strength).astype(BF16)]

        first = steps(firsts[k])
        (late["block_out"],) = run(
            body,
            [(outer_sent[k + 2], 0), (outer[k + 2], 0), (tokens, first)]
            + [(x, first, True) for x in late["stats"]],
            [(length, D, BF16, first, late.get("block_out"))],
            spans[k],
            name="finish_chunk",
        )

    def finish_grad(n):
        def body(p, mine, side_got, middle_got, token, scale, cot, gain):
            token = token[...].astype(F32)
            scale = upright(scale[...])[:, 2:3]
            weighted = (mine[...] + side_got[...] + middle_got[...]) * gain[...]
            pull = jnp.sum(weighted * token, axis=-1, keepdims=True) / D
            return [cot[...].astype(F32) + scale * weighted - token * scale * scale * scale * pull]

        mine = lambda p: p * per
        (late["tokens_grad"],) = run(
            body,
            [
                (late["total"], mine),
                (outer[n], 0),
                (inner[n], 0),
                (tokens, mine),
                (late["own_stats"], mine, True),
                (out_cotangent, mine),
                (norm_gain[None], None),
            ],
            [(rows, D, F32, 0, None)],
            rows,
            name="finish_grad",
        )

    low = mixed = None
    back = []

    def backward(k):
        nonlocal low, mixed, back
        low, mixed, back = run_backward(
            piece_firsts[k],
            pieces[k],
            late["og"],
            late["stats"],
            where,
            segment_ids,
            small,
            back,
            low,
            mixed,
            chain.deps(),
        )
        chain.last = back[2]

    def exchange_stats():
        own = late["own_stats"] = kept[0]
        late["stats"] = [own] + [
            send(own, [(k, (k + turn) % parts) for k in range(parts)]) for turn in range(1, parts)
        ]
        chain.more = late["stats"][1:]

    forward()
    send_outer(0, partials[0], False)
    late["og"], _ = run_out_grad(chain, out_cotangent, out_weight, [])
    forward()
    exchange_stats()
    event(0, (partials[1], 0))
    backward(1)
    backward(0)
    event(1, (partials[2], 0))

    normed = kept[1]
    wide_acc, narrow_acc, heads_acc = back[3:]
    back_weights = [gate_weight, value_weight, state_weight, step_place]
    width = 3 * LANES
    fit = lambda x: jnp.pad(x.reshape(-1), (0, -x.size % width)).reshape(-1, width)
    narrow = narrow_acc.reshape(5, 8, states).sum(axis=1)
    wide_sums = wide_acc.reshape(7, 8, channels).sum(axis=1)
    head_sums = heads_acc.reshape(2, 8, LANES).sum(axis=1)[:, :head_count]
    skip_grad = wide_sums[6].reshape(head_count, channels // head_count).sum(axis=1)
    mine = jnp.concatenate([fit(wide_sums[:6]), fit(jnp.concatenate([head_sums, skip_grad[None]]))])
    mine_rows = mine.shape[0]
    slots = jnp.where(
        lax.broadcasted_iota(jnp.int32, (parts, 1, 1), 0) == place, mine[None], 0.0
    ).reshape(-1, width)
    narrow_rows = fit(narrow)
    filler = jnp.zeros((CHUNK - narrow_rows.shape[0] - slots.shape[0], width), F32)
    shared, gains = run_rest_grad(
        chain, normed, low, jnp.concatenate([narrow_rows, slots, filler]), back_weights[2:]
    )

    ways = lax.axis_size("dp")
    own_dp = lax.axis_index("dp")
    bits = []
    while 2 ** len(bits) < ways:
        bits.append(2 ** len(bits))
    shared_rows = shared.shape[0]
    swap = lambda x, bit: lax.ppermute(x, "dp", [(k, k ^ bit) for k in range(ways)])
    side = lambda n: (own_dp // bits[n]) % 2
    halving = {"keep": shared, "rows": shared_rows, "got": None}

    def halve(n):
        keep, size = halving["keep"], halving["rows"]
        if n > 0:
            add = lambda p, a, b: [a[...] + b[...]]
            size = size // 2
            (keep,) = rowwise(
                chain,
                side(n - 1).astype(jnp.int32)[None],
                add,
                [(keep, lambda p: p), (halving["got"], 0)],
                [(size, width, F32, 0, None)],
                size,
                step=size,
                name="halve",
            )
            halving["rows"] = size
        if n < len(bits):
            away = lax.dynamic_slice_in_dim(keep, (1 - side(n)) * (size // 2), size // 2, 0)
            halving["got"] = swap(away, bits[n])
        halving["keep"] = keep

    core = side(0).astype(jnp.int32)[None]
    core_bit, axes = bits[0], list(range(1, len(bits)))
    turned = axes[len(axes) // 2 :] + axes[: len(axes) // 2]
    orders = (axes, turned)
    sums = {}

    def reduce_step(step):
        sides = jnp.stack([side(orders[k][step]).astype(jnp.int32) for k in range(2)])
        ins, outs = [], []
        size = sums["keep"][0].shape[0] // 2
        unit = size if size < 512 else size // 2
        for k in range(2):
            for stay in (1, 0):
                at = functools.partial(
                    lambda p, k, stay: (p[k] if stay else 1 - p[k]) * (size // unit), k=k, stay=stay
                )
                ins += [(sums["keep"][k], at), (sums["got"][k], at)]
                outs.append((size, channels, F32, 0, None))
        results = rowwise(
            chain,
            sides,
            lambda p, *refs: [refs[2 * n][...] + refs[2 * n + 1][...] for n in range(4)],
            ins,
            outs,
            size,
            step=unit,
            whole_place=True,
            name="reduce_step",
        )
        sums["keep"] = [results[0], results[2]]
        sums["size"] = size
        sums["got"] = [swap(results[2 * k + 1], bits[orders[k][step]]) for k in range(2)]

    unit = D // 4 // 2 ** len(axes)

    def reduce_start():
        tiles, sums["gains"] = run_weight_grads(
            chain, core, normed, low, out_cotangent, mixed, back_weights[:2], gains, unit
        )
        sums["keep"] = tiles[2:]
        sums["got"] = [swap(x, core_bit) for x in tiles[:2]]

    def gather_first():
        sums["full"] = rowwise(
            chain,
            where,
            lambda p, a, b, c, d: [a[...] + b[...], c[...] + d[...]],
            [(x, 0) for k in range(2) for x in (sums["keep"][k], sums["got"][k])],
            [(sums["size"], channels, F32, 0, None)] * 2,
            sums["size"],
            step=sums["size"],
            name="gather_first",
        )
        step = len(axes) - 1
        sums["got"] = [swap(sums["full"][k], bits[orders[k][step]]) for k in range(2)]

    def gather_step(step):
        size = sums["size"]
        sides = jnp.stack([side(orders[k][step]).astype(jnp.int32) for k in range(2)])

        def body(p, *refs):
            upper = pl.program_id(0)
            picked = []
            for k in range(2):
                own, got = refs[2 * k][...], refs[2 * k + 1][...]
                picked.append(jnp.where(upper == p[k], own, got))
            return picked

        sums["full"] = rowwise(
            chain,
            sides,
            body,
            [(x, 0, False, 1) for k in range(2) for x in (sums["full"][k], sums["got"][k])],
            [(2 * size, channels, F32, 0, None)] * 2,
            2 * size,
            step=size,
            whole_place=True,
            name="gather_step",
        )
        sums["size"] = 2 * size
        if step > 0:
            sums["got"] = [swap(sums["full"][k], bits[orders[k][step - 1]]) for k in range(2)]

    def gather_core():
        sums["got"] = [swap(x, core_bit) for x in sums["full"]]

    halve(0)
    reduce_start()
    gain_rows = fit(sums["gains"][0] / norm_gain)
    gain_rows = jnp.pad(gain_rows, ((0, 8 - gain_rows.shape[0]), (0, 0)))
    halve(1)
    event(2, (partials[3], 0))

    halve(2)
    reduce_step(0)
    late["total"] = run_total(chain, low, back_weights)
    finish_chunk(0)
    event(3, (late["total"], at_ends(3, 0)))

    for step in range(1, len(axes)):
        reduce_step(step)
    gather_first()
    finish_chunk(1)
    for step in range(len(axes) - 1, 0, -1):
        gather_step(step)
    for n in range(3, len(bits) + 1):
        halve(n)
    share = jnp.concatenate([halving["keep"], gain_rows])
    share = lax.psum(share, "tensor")
    event(4, (late["total"], at_ends(2, 1)), at_ends(3, 0))

    gather_step(0)
    gather_core()
    finish_chunk(2)
    event(5, (late["total"], lambda p: jnp.where(p < 2, 1 - p, 5 - p) * per), at_ends(2, 1))

    (share,) = after(chain, share)
    share = lax.all_gather(share, "dp")
    finish_chunk(3)
    gate_weight_grad, value_weight_grad, out_weight_grad = run_assemble(
        chain, core, sums["full"], sums["got"], unit
    )

    places = np.array(
        [sum((k >> n & 1) << (len(bits) - 1 - n) for n in range(len(bits))) for k in range(ways)]
    )
    order = np.argsort(places)
    gain_sums = share[:, -8:].sum(axis=0)
    share = jnp.concatenate([share[k, :-8] for k in order] + [gain_sums])
    shared = share
    norm_gain_grad = shared[-8:].reshape(-1)[:D]
    rest, shared = shared[:D], shared[D:]
    state_weight_grad = rest[:, :states]
    step_weight_grad = lax.dynamic_slice(rest, (0, states + place * head_count), (D, head_count))
    at = narrow_rows.shape[0]
    narrow = shared[:at].reshape(-1)[: 5 * states].reshape(5, states)
    mine = lax.dynamic_slice_in_dim(shared, at + place * mine_rows, mine_rows, 0).reshape(-1)
    wide_sums = mine[: 6 * channels].reshape(6, channels)
    head_sums = mine[6 * channels :][: 3 * head_count].reshape(3, head_count)
    chain.more = [state_weight_grad, step_weight_grad, norm_gain_grad, narrow, wide_sums, head_sums]
    finish_grad(6)
    return (
        late["block_out"],
        late["tokens_grad"],
        norm_gain_grad,
        gate_weight_grad,
        value_weight_grad,
        state_weight_grad,
        step_weight_grad,
        wide_sums[:4],
        wide_sums[4],
        narrow[:4],
        narrow[4],
        head_sums[0],
        head_sums[1],
        head_sums[2],
        wide_sums[5],
        out_weight_grad,
    )


def solution(mesh):
    placed = (
        P("dp", None),
        P(),
        P(None, "tensor"),
        P(None, "tensor"),
        P(),
        P(None, "tensor"),
        P(None, "tensor"),
        P("tensor"),
        P(),
        P(),
        P("tensor"),
        P("tensor"),
        P("tensor"),
        P("tensor"),
        P("tensor", None),
        P("dp", None),
        P("dp", None),
    )
    return jax.shard_map(
        on_device,
        mesh=mesh,
        in_specs=placed,
        out_specs=(
            P("dp", None),
            P(("dp", "tensor"), None),
            P(),
            P(None, "tensor"),
            P(None, "tensor"),
            P(),
            P(None, "tensor"),
            P(None, "tensor"),
            P("tensor"),
            P(),
            P(),
            P("tensor"),
            P("tensor"),
            P("tensor"),
            P("tensor"),
            P("tensor", None),
        ),
        check_vma=False,
    )
```

```python
import functools

import jax
import jax.numpy as jnp
import numpy as np
from jax import lax
from jax.experimental import pallas as pl
from jax.experimental.pallas import tpu as pltpu
from jax.sharding import PartitionSpec as P

D = 1536
INNER = 3072
EPS = 1e-05
BLOCK = 128
LANES = 128
FAR = -1e30
F32 = jnp.float32
BF16 = jnp.bfloat16
CHUNK = 256
STEP = 128
ROWS = 32
VMEM_LIMIT = 63 * 2**20
SMALL_COST = pl.CostEstimate(flops=1, bytes_accessed=1, transcendentals=0)
PIECES = (1, 3)


def matmul(left, right, dims=(1, 0)):
    return lax.dot_general(
        left, right, (((dims[0],), (dims[1],)), ((), ())), preferred_element_type=F32
    )


def exact(left, right):
    return lax.dot_general(
        left,
        right,
        (((1,), (0,)), ((), ())),
        precision=lax.Precision.HIGHEST,
        preferred_element_type=F32,
    )


def sigmoid(v):
    return 0.5 * jnp.tanh(0.5 * v) + 0.5


def softplus(v):
    return jnp.maximum(v, 0.0) + jnp.log1p(jnp.exp(-jnp.abs(v)))


def fold(x):
    return x.reshape(x.shape[0] // 8, 8, x.shape[1]).sum(axis=0)


def triangle(lower):
    row = lax.broadcasted_iota(jnp.int32, (BLOCK, BLOCK), 0)
    col = lax.broadcasted_iota(jnp.int32, (BLOCK, BLOCK), 1)
    return jnp.where(row >= col if lower else row <= col, 1.0, 0.0).astype(F32)


def group_sum(x, spread):
    high = x.astype(BF16)
    low = (x - high.astype(F32)).astype(BF16)
    return matmul(high, spread) + matmul(low, spread)


def upright(rows):
    fill = jnp.zeros((BLOCK - rows.shape[0], BLOCK), F32)
    return jnp.concatenate([rows, fill], axis=0).T


def segment_columns(seg_ref, block, blocks, ahead):
    part = lambda k: seg_ref[:, pl.ds(pl.multiple_of(k * BLOCK, BLOCK), BLOCK)].astype(F32)
    ids = part(block)
    before = jnp.where(block > 0, part(jnp.maximum(block - 1, 0)), -1.0)
    lane = lax.broadcasted_iota(jnp.int32, (1, BLOCK), 1)
    rows = [ids]
    if ahead:
        behind = jnp.where(block < blocks - 1, part(jnp.minimum(block + 1, blocks - 1)), -1.0)
    for far in range(1, 4):
        if ahead:
            moved = jnp.where(
                lane >= BLOCK - far,
                pltpu.roll(behind, BLOCK - far, 1),
                pltpu.roll(ids, BLOCK - far, 1),
            )
        else:
            moved = jnp.where(lane < far, pltpu.roll(before, far, 1), pltpu.roll(ids, far, 1))
        rows.append(jnp.where(moved == ids, 1.0, 0.0))
    rows.append(jnp.where(ids == before[:, BLOCK - 1 :], 1.0, 0.0))
    rows.append(jnp.where(ids == ids[:, BLOCK - 1 :], 1.0, 0.0))
    rows.append(jnp.zeros((2, BLOCK), F32))
    return upright(jnp.concatenate(rows, axis=0)), ids


def decay_terms(step_raw, step_bias, rate, cols, seg_row):
    steps = softplus(step_raw + step_bias)
    rates = -steps * rate
    local = exact(triangle(True), rates)
    last = local[BLOCK - 1 :]
    into = jnp.exp(jnp.where(cols[:, 4:5] > 0.5, local, FAR))
    out = jnp.exp(jnp.where(cols[:, 5:6] > 0.5, last - local, FAR))
    row = lax.broadcasted_iota(jnp.int32, (BLOCK, BLOCK), 0)
    col = lax.broadcasted_iota(jnp.int32, (BLOCK, BLOCK), 1)
    allowed = jnp.logical_and(row >= col, cols[:, 0:1] == seg_row)
    bias = jnp.where(allowed, 0.0, FAR)
    return steps, rates, local, local.T, into, out, bias


def pairwise(x, pair, half):
    return jnp.where(half, x[:, 2 * pair : 2 * pair + 1], x[:, 2 * pair + 1 : 2 * pair + 2])


def split_pair(x, half):
    zero = jnp.zeros_like(x)
    return jnp.concatenate([jnp.where(half, x, zero), jnp.where(half, zero, x)], axis=0)


def decay_of(local, local_t, bias, head):
    return jnp.exp(local[:, head : head + 1] - local_t[head : head + 1, :] + bias)


def sum_over_places(place, own, others):
    parts = len(others) + 1
    total = None
    for k in range(parts):
        value = own
        for turn in range(1, parts):
            value = jnp.where((place - k + parts) % parts == turn, others[turn - 1], value)
        total = value if total is None else total + value
    return total


GAIN_ROW, KERNEL_ROW, BIAS_ROW, GATED_ROW, SKIP_ROW = 0, 2, 6, 7, 8
STATE_KERNEL_ROW, STATE_BIAS_ROW, STEP_ROW, DECAY_ROW = 9, 13, 14, 15


def run_pack(place, *arrays):
    channels = arrays[1].shape[1]

    def kernel(place_ref, *refs):
        (norm_gain, kernel, bias, gated, skip, state_kernel, state_bias, step_bias, decay, step_w) = refs[
            :10
        ]
        table, wide, placed = refs[10:]
        table[...] = jnp.zeros_like(table)
        table[GAIN_ROW : GAIN_ROW + 1, :] = norm_gain[:channels].reshape(1, channels)
        table[GAIN_ROW + 1 : GAIN_ROW + 2, :] = norm_gain[channels:].reshape(1, channels)
        table[KERNEL_ROW : KERNEL_ROW + 4, :] = kernel[...]
        table[STATE_KERNEL_ROW : STATE_KERNEL_ROW + 4, : state_kernel.shape[1]] = state_kernel[...]
        rows = ((BIAS_ROW, bias), (GATED_ROW, gated), (SKIP_ROW, skip), (STATE_BIAS_ROW, state_bias))
        for row, ref in rows + ((STEP_ROW, step_bias), (DECAY_ROW, decay)):
            size = ref.shape[0]
            table[row : row + 1, :size] = ref[...].reshape(1, size)
        rows = step_w[...].astype(F32)
        fill = jnp.zeros((LANES - rows.shape[0], rows.shape[1]), F32)
        columns = jnp.concatenate([rows, fill], axis=0).T
        wide[...] = columns.astype(BF16)
        placed[...] = pltpu.roll(columns, place_ref[0] * rows.shape[0], 1).astype(BF16)

    return pl.pallas_call(
        kernel,
        out_shape=[
            jax.ShapeDtypeStruct((16, channels), F32),
            jax.ShapeDtypeStruct((arrays[-1].shape[1], LANES), BF16),
            jax.ShapeDtypeStruct((arrays[-1].shape[1], LANES), BF16),
        ],
        in_specs=[pl.BlockSpec(memory_space=pltpu.SMEM)]
        + [pl.BlockSpec(memory_space=pltpu.VMEM) for _ in arrays],
        cost_estimate=SMALL_COST,
        name="pack",
    )(place, *arrays)


def forward_kernel(first_piece, unused, block_base, chunks, *refs):
    tokens, cot, seg, par, gate_w, value_w, state_w, step_w, out_w = refs[:9]
    refs = refs[9:]
    if not first_piece:
        state_in, tail_in, state_tail_in = refs[:3]
        refs = refs[3:]
    refs = refs[unused:]
    (
        gate_out,
        vraw_out,
        pv_out,
        y_out,
        sraw_out,
        spv_out,
        step_out,
        saved_out,
        stats_out,
        normed_out,
        state,
        tail_out,
        state_tail_out,
    ) = refs[:13]
    partial_outs = refs[13 : 13 + chunks]
    vbuf, sbuf, scaled, partial = refs[13 + chunks :]
    size = tokens.shape[0]
    channels = gate_w.shape[1]
    states = 2 * LANES

    @pl.when(pl.program_id(0) == 0)
    def _():
        if first_piece:
            state[...] = jnp.zeros_like(state)
            vbuf[:8] = jnp.zeros((8, channels), F32)
            sbuf[:8] = jnp.zeros((8, states), F32)
        else:
            state[...] = state_in[...]
            vbuf[:8] = tail_in[...]
            sbuf[:8] = state_tail_in[...]

    norm_gain = jnp.concatenate([par[GAIN_ROW : GAIN_ROW + 1], par[GAIN_ROW + 1 : GAIN_ROW + 2]], axis=1)
    scales = []
    for row in range(0, size, ROWS):
        wide = tokens[row : row + ROWS].astype(F32)
        scale = lax.rsqrt(jnp.mean(wide * wide, axis=-1, keepdims=True) + EPS)
        normed_out[row : row + ROWS] = (wide * scale * norm_gain).astype(BF16)
        scales.append(scale)
    normed = normed_out[...]
    vbuf[8:] = matmul(normed, value_w[...])
    sbuf[8:] = matmul(normed, state_w[...])
    step_out[...] = matmul(normed, step_w[...])
    gate_out[...] = matmul(normed, gate_w[...])

    def conv(buf, row, lanes, cols, kernel_row, bias_row):
        raw = buf[row + 8 : row + 8 + BLOCK, lanes]
        total = par[bias_row : bias_row + 1, lanes] + raw * par[kernel_row + 3 : kernel_row + 4, lanes]
        for back in range(1, 4):
            tap = par[kernel_row + 3 - back : kernel_row + 4 - back, lanes]
            moved = buf[row + 8 - back : row + 8 - back + BLOCK, lanes]
            total = total + moved * tap * cols[:, back : back + 1]
        return raw, total

    half = lax.broadcasted_iota(jnp.int32, (BLOCK, LANES), 1) < LANES // 2
    half_row = half[0:1]
    lane = lax.broadcasted_iota(jnp.int32, (BLOCK, LANES), 1)
    step_bias = par[STEP_ROW : STEP_ROW + 1, :LANES]
    rate = jnp.exp(par[DECAY_ROW : DECAY_ROW + 1, :LANES])
    skips = par[SKIP_ROW : SKIP_ROW + 1, :LANES]
    squares = []
    for sub in range(size // BLOCK):
        rows = slice(sub * BLOCK, (sub + 1) * BLOCK)
        row = sub * BLOCK
        block = block_base + pl.program_id(0) * (size // BLOCK) + sub
        cols, seg_row = segment_columns(seg, block, None, False)
        mixed_state = []
        for part in range(2):
            lanes = slice(part * LANES, (part + 1) * LANES)
            raw, spv = conv(sbuf, row, lanes, cols, STATE_KERNEL_ROW, STATE_BIAS_ROW)
            sraw_out[rows, lanes] = raw.astype(BF16)
            spv_out[rows, lanes] = spv
            mixed_state.append(spv * sigmoid(spv))
        b_low = mixed_state[0].astype(BF16)
        b_turned = mixed_state[0].T.astype(BF16)
        c_low = mixed_state[1].astype(BF16)
        steps, _, local, local_t, into, out, bias = decay_terms(
            step_out[rows], step_bias, rate, cols, seg_row
        )
        keep = into[BLOCK - 1 :]
        scores = matmul(c_low, b_low, (1, 1))
        square = jnp.zeros((BLOCK, LANES), F32)
        for pair in range(channels // LANES):
            lanes = slice(pair * LANES, (pair + 1) * LANES)
            raw, pv = conv(vbuf, row, lanes, cols, KERNEL_ROW, BIAS_ROW)
            vraw_out[rows, lanes] = raw.astype(BF16)
            pv_out[rows, lanes] = pv
            values = pv * sigmoid(pv)
            old = state[:, lanes]
            old_low = old.astype(BF16)
            saved_out[sub, :, lanes] = old_low
            u = values * pairwise(steps, pair, half)
            weights = [
                (scores * decay_of(local, local_t, bias, 2 * pair + k)).astype(BF16)
                for k in range(2)
            ]
            inner = matmul(jnp.concatenate(weights, axis=1), split_pair(u.astype(BF16), half))
            y_ssm = inner + matmul(c_low, old_low) * pairwise(into, pair, half)
            y_out[rows, lanes] = y_ssm
            leaving = (u * pairwise(out, pair, half)).astype(BF16)
            state[:, lanes] = old * pairwise(keep, pair, half_row) + matmul(b_turned, leaving)
            gate = gate_out[rows, lanes]
            gated = (y_ssm + pairwise(skips, pair, half_row) * values) * (gate * sigmoid(gate))
            square = square + gated * gated
            scaled[rows, lanes] = (gated * par[GATED_ROW : GATED_ROW + 1, lanes]).astype(BF16)
        squares.append(jnp.sum(square, axis=-1, keepdims=True))
    vbuf[:8] = vbuf[size:]
    sbuf[:8] = sbuf[size:]
    tail_out[...] = vbuf[:8]
    state_tail_out[...] = sbuf[:8]
    partial[...] = matmul(scaled[...], out_w[...])
    steps_each = pl.num_programs(0) // chunks
    for index, partial_out in enumerate(partial_outs):

        @pl.when(pl.program_id(0) // steps_each == index)
        def _(partial_out=partial_out):
            partial_out[...] = partial[...]

    products = [
        jnp.sum(cot[row : row + ROWS].astype(F32) * partial[row : row + ROWS], axis=-1, keepdims=True)
        for row in range(0, size, ROWS)
    ]
    per = BLOCK // ROWS
    for sub in range(size // BLOCK):
        product = jnp.concatenate(products[sub * per : (sub + 1) * per], axis=0)
        scale = jnp.concatenate(scales[sub * per : (sub + 1) * per], axis=0)
        table = jnp.where(
            lane == 0, squares[sub], jnp.where(lane == 1, product, jnp.where(lane == 2, scale, 0.0))
        )
        stats_out[:, sub * BLOCK : (sub + 1) * BLOCK] = table.T[:8]


def backward_kernel(first_piece, unused, block_base, blocks, *refs):
    (
        place_ref,
        og_ref,
        gate_ref,
        vraw_ref,
        pv_ref,
        y_ref,
        sraw_ref,
        spv_ref,
        step_ref,
        own_stats,
        stats_1,
        stats_2,
        stats_3,
        saved_ref,
        seg,
        par,
    ) = refs[:16]
    refs = refs[16:]
    if not first_piece:
        carried_in = refs[:6]
        refs = refs[6:]
    refs = refs[unused:]
    (
        low_out,
        mixed_out,
        state_out,
        tail_out,
        state_tail_out,
        wide_acc,
        narrow_acc,
        heads_acc,
    ) = refs
    channels = gate_ref.shape[1]
    place = place_ref[0]

    @pl.when(pl.program_id(0) == 0)
    def _():
        outs = (state_out, tail_out, state_tail_out, wide_acc, narrow_acc, heads_acc)
        for k, ref in enumerate(outs):
            ref[...] = jnp.zeros_like(ref) if first_piece else carried_in[k][...]

    block = block_base + pl.num_programs(0) - 1 - pl.program_id(0)
    cols, seg_row = segment_columns(seg, block, blocks, True)
    stats = sum_over_places(place, own_stats[...], [stats_1[...], stats_2[...], stats_3[...]])
    stats = upright(stats)
    strength = lax.rsqrt(stats[:, 0:1] / INNER + EPS)
    pull = strength * strength * strength * stats[:, 1:2] / INNER

    half = lax.broadcasted_iota(jnp.int32, (BLOCK, LANES), 1) < LANES // 2
    half_row = half[0:1]
    spv = [spv_ref[:, :LANES], spv_ref[:, LANES:]]
    spv_sig = [sigmoid(v) for v in spv]
    b_part = spv[0] * spv_sig[0]
    c_part = spv[1] * spv_sig[1]
    b_low = b_part.astype(BF16)
    c_low = c_part.astype(BF16)
    c_turned = c_part.T.astype(BF16)
    step_raw = step_ref[...]
    step_bias = par[STEP_ROW : STEP_ROW + 1, :LANES]
    rate = jnp.exp(par[DECAY_ROW : DECAY_ROW + 1, :LANES])
    skips = par[SKIP_ROW : SKIP_ROW + 1, :LANES]
    steps, rates, local, local_t, into, out, bias = decay_terms(
        step_raw, step_bias, rate, cols, seg_row
    )
    keep = into[BLOCK - 1 :]
    scores = matmul(c_low, b_low, (1, 1))

    def conv_back(pre_grad, raw, lanes, after, kernel_row, acc):
        ext = jnp.concatenate([pre_grad, after[:, lanes]], axis=0)
        after[:, lanes] = pre_grad[:8]
        total = pre_grad * par[kernel_row + 3 : kernel_row + 4, lanes]
        acc[24:32, lanes] += fold(raw * pre_grad)
        acc[32:40, lanes] += fold(pre_grad)
        for ahead in range(1, 4):
            moved = pltpu.roll(ext, BLOCK + 8 - ahead, 0)[:BLOCK]
            term = moved * cols[:, ahead : ahead + 1]
            total = total + term * par[kernel_row + 3 - ahead : kernel_row + 4 - ahead, lanes]
            acc[8 * (3 - ahead) : 8 * (4 - ahead), lanes] += fold(raw * term)
        return total

    score_grad = jnp.zeros((BLOCK, BLOCK), F32)
    b_grad = jnp.zeros((BLOCK, LANES), F32)
    c_grad = jnp.zeros((BLOCK, LANES), F32)
    spread_dl = jnp.zeros((BLOCK, LANES), F32)
    spread_ds = jnp.zeros((BLOCK, LANES), F32)
    spread_end = jnp.zeros((8, LANES), F32)
    for pair in range(channels // LANES):
        lanes = slice(pair * LANES, (pair + 1) * LANES)
        spread = (
            lax.broadcasted_iota(jnp.int32, (LANES, LANES), 0) // (LANES // 2) + 2 * pair
            == lax.broadcasted_iota(jnp.int32, (LANES, LANES), 1)
        ).astype(BF16)
        gain = par[GATED_ROW : GATED_ROW + 1, lanes]
        skip = pairwise(skips, pair, half_row)
        gate = gate_ref[:, lanes]
        gate_sig = sigmoid(gate)
        gate_silu = gate * gate_sig
        pv = pv_ref[:, lanes]
        pv_sig = sigmoid(pv)
        values = pv * pv_sig
        og = og_ref[:, lanes]
        y_ssm = y_ref[:, lanes]
        y = y_ssm + skip * values
        gated = y * gate_silu
        strong = gated * strength
        mixed_out[:, lanes] = (strong * gain).astype(BF16)
        gated_grad = gain * strength * og - gated * pull
        low_out[:, lanes] = (
            gated_grad * y * (gate_sig * (1.0 + gate * (1.0 - gate_sig)))
        ).astype(BF16)
        grad = gated_grad * gate_silu
        wide_acc[40:48, lanes] += fold(og * strong)
        wide_acc[48:56, lanes] += fold(grad * values)

        state_grad = state_out[:, lanes]
        state_grad_low = state_grad.astype(BF16)
        old_low = saved_ref[0, :, lanes]
        pair_steps = pairwise(steps, pair, half)
        pair_out = pairwise(out, pair, half)
        u = values * pair_steps
        u_low = u.astype(BF16)
        g_low = grad.astype(BF16)
        g_split = split_pair(g_low, half)
        decays = [decay_of(local, local_t, bias, 2 * pair + k) for k in range(2)]
        weights = jnp.concatenate([(scores * d).astype(BF16) for d in decays], axis=0)
        weight_grad = matmul(g_split, u_low, (1, 1))
        score_grad = score_grad + weight_grad[:BLOCK] * decays[0] + weight_grad[BLOCK:] * decays[1]
        u_grad_out = matmul(b_low, state_grad_low) * pair_out
        u_grad = matmul(weights, g_split, (0, 0)) + u_grad_out
        u_near = u_low.astype(F32)
        spread_dl = spread_dl + group_sum(g_low.astype(F32) * y_ssm - u_near * u_grad, spread)
        spread_ds = spread_ds + group_sum(values * u_grad, spread)
        keep_row = pairwise(keep, pair, half_row)
        spread_end = spread_end + group_sum(
            fold(u_near * u_grad_out) + fold(state_grad * old_low.astype(F32)) * keep_row, spread
        )
        entering = (grad * pairwise(into, pair, half)).astype(BF16)
        leaving = (u * pair_out).astype(BF16)
        c_grad = c_grad + matmul(entering, old_low, (1, 1))
        b_grad = b_grad + matmul(leaving, state_grad_low, (1, 1))
        state_out[:, lanes] = state_grad * keep_row + matmul(c_turned, entering)
        pre_grad = (pair_steps * u_grad + skip * grad) * (pv_sig * (1.0 + pv * (1.0 - pv_sig)))
        raw_grad = conv_back(
            pre_grad, vraw_ref[:, lanes].astype(F32), lanes, tail_out, KERNEL_ROW, wide_acc
        )
        low_out[:, channels + pair * LANES : channels + (pair + 1) * LANES] = raw_grad.astype(BF16)
    score_low = score_grad.astype(BF16)
    c_grad = c_grad + matmul(score_low, b_low)
    b_grad = b_grad + matmul(score_low, c_low, (0, 0))
    rate_grad = exact(triangle(False), spread_dl) + jnp.sum(spread_end, axis=0, keepdims=True)
    step_grad = (spread_ds - rate * rate_grad) * sigmoid(step_raw + step_bias)
    heads_acc[0:8] += fold(step_grad)
    heads_acc[8:16] += fold(rates * rate_grad)
    for part, grad in enumerate((b_grad, c_grad)):
        lanes = slice(part * LANES, (part + 1) * LANES)
        pre_grad = grad * (spv_sig[part] * (1.0 + spv[part] * (1.0 - spv_sig[part])))
        raw_grad = conv_back(
            pre_grad, sraw_ref[:, lanes].astype(F32), lanes, state_tail_out, STATE_KERNEL_ROW, narrow_acc
        )
        at = 2 * channels + part * LANES
        low_out[:, at : at + LANES] = raw_grad.astype(BF16)
    heads_here = channels // (LANES // 2)
    low_out[:, 2 * channels + 2 * LANES :] = pltpu.roll(step_grad, place * heads_here, 1).astype(BF16)


def out_grad_kernel(unused, cot, out_w, *refs):
    og, token = refs[unused : unused + 2]
    og[...] = matmul(cot[...], out_w[...], (1, 1))
    token[...] = jnp.zeros((8, LANES), F32)


def run_out_grad(chain, cot, out_w, passes):
    length, channels = cot.shape[0], out_w.shape[0]
    deps = chain.deps()
    results = pl.pallas_call(
        functools.partial(out_grad_kernel, len(deps) + len(passes)),
        grid=(length // CHUNK,),
        in_specs=[pl.BlockSpec((CHUNK, D), lambda i: (i, 0)), whole(out_w.shape)]
        + [ANYWHERE for _ in deps + passes],
        out_specs=[pl.BlockSpec((CHUNK, channels), lambda i: (i, 0)), whole((8, LANES))]
        + [ANYWHERE for _ in passes],
        out_shape=[
            jax.ShapeDtypeStruct((length, channels), F32),
            jax.ShapeDtypeStruct((8, LANES), F32),
        ]
        + [jax.ShapeDtypeStruct(p.shape, p.dtype) for p in passes],
        input_output_aliases={2 + len(deps) + k: 2 + k for k in range(len(passes))},
        compiler_params=pltpu.CompilerParams(vmem_limit_bytes=VMEM_LIMIT),
        cost_estimate=SMALL_COST,
        name="out_grad",
    )(cot, out_w, *deps, *passes)
    chain.last = results[1]
    return results[0], results[2:]


def run_matmul(chain, body, ins, outs, count, scratch=(), name=None):
    deps = chain.deps()
    arrays = [a for a, _, _ in ins]

    def kernel(*refs):
        body(*refs[: len(arrays)], *refs[len(arrays) + len(deps) :])
        refs[len(arrays) + len(deps) + len(outs)][...] = jnp.zeros((8, LANES), F32)

    results = pl.pallas_call(
        kernel,
        grid=(count,),
        in_specs=[whole(a.shape) if m is None else pl.BlockSpec(b, m) for a, b, m in ins]
        + [ANYWHERE for _ in deps],
        out_specs=[pl.BlockSpec(b, m) for _, b, m in outs] + [whole((8, LANES))],
        out_shape=[jax.ShapeDtypeStruct(s, F32) for s, _, _ in outs]
        + [jax.ShapeDtypeStruct((8, LANES), F32)],
        scratch_shapes=list(scratch),
        compiler_params=pltpu.CompilerParams(vmem_limit_bytes=VMEM_LIMIT),
        cost_estimate=SMALL_COST,
        name=name,
    )(*arrays, *deps)
    chain.last = results[-1]
    return results[:-1]


def gain_row(value, count):
    out = []
    for k in range(count // BLOCK):
        column = jnp.sum(value[k * BLOCK : (k + 1) * BLOCK], axis=-1, keepdims=True)
        out.append(jnp.broadcast_to(column, (BLOCK, BLOCK)).T[:8])
    return jnp.concatenate(out, axis=1)


def run_rest_grad(chain, normed, low, small_rows, weights):
    width = small_rows.shape[1]
    count = D // CHUNK
    states = weights[0].shape[1]

    def body(left, right, extra, state_w, step_w, out, gain, token):
        @pl.when(pl.program_id(0) < count)
        def _():
            value = matmul(left[...], right[...], (0, 0))
            out[...] = value
            both = jnp.concatenate([state_w[...], step_w[...]], axis=1).astype(F32)
            gain[...] = gain_row(value * both, CHUNK)

        @pl.when(pl.program_id(0) == count)
        def _():
            out[...] = extra[...]

    length, total = low.shape
    held = lambda i: jnp.minimum(i, count - 1)
    tile = lambda a: (a, (CHUNK, a.shape[1]), lambda i: (held(i), 0))
    return run_matmul(
        chain,
        body,
        [
            (normed, (length, CHUNK), lambda i: (0, held(i))),
            (low, (length, width), lambda i: (0, total // width - 1)),
            (small_rows, None, None),
            *[tile(w) for w in weights],
        ],
        [
            ((D + CHUNK, width), (CHUNK, width), lambda i: (i, 0)),
            ((8, D), (8, CHUNK), lambda i: (0, held(i))),
        ],
        count + 1,
        name="rest_grad",
    )


def run_weight_grads(chain, core, normed, low, cot, mixed, weights, gains, unit):
    length = normed.shape[0]
    channels = mixed.shape[1]
    tile = D // 4
    deps = chain.deps()

    def which(i, p):
        return jnp.where(i < 2, 1 - p[0], p[0]) * 2 + i % 2

    def kernel(place, left, right, cots, mix, gate_w, value_w, gain_in, *refs):
        outs, gain, token = refs[len(deps) : len(deps) + 4], refs[-2], refs[-1]
        i = pl.program_id(0)

        @pl.when(i == 0)
        def _():
            gain[...] = gain_in[...]
            token[...] = jnp.zeros((8, LANES), F32)

        gate = matmul(left[...], right[:, :channels], (0, 0))
        value = matmul(left[...], right[:, channels:], (0, 0))
        out = matmul(cots[...], mix[...], (0, 0))
        at = pl.ds(pl.multiple_of(which(i, place) * tile, LANES), tile)
        products = gate * gate_w[...].astype(F32) + value * value_w[...].astype(F32)
        gain[:, at] = gain[:, at] + gain_row(products, tile)
        for k in range(4):

            @pl.when(i == k)
            def _(k=k):
                for n in range(tile // unit):
                    rows = slice(n * unit, (n + 1) * unit)
                    for m, part in enumerate((gate, value, out)):
                        first = (3 * n + m) * unit
                        outs[k][first : first + unit, :] = part[rows]

    lanes = lambda i, p: (0, which(i, p))
    weight_spec = pl.BlockSpec((tile, channels), lambda i, p: (which(i, p), 0))
    results = pl.pallas_call(
        kernel,
        grid_spec=pltpu.PrefetchScalarGridSpec(
            num_scalar_prefetch=1,
            grid=(4,),
            in_specs=[
                pl.BlockSpec((length, tile), lanes),
                pl.BlockSpec((length, 2 * channels), lambda i, p: (0, 0)),
                pl.BlockSpec((length, tile), lanes),
                whole(mixed.shape),
                weight_spec,
                weight_spec,
                whole(gains.shape),
            ]
            + [ANYWHERE for _ in deps],
            out_specs=[whole((3 * tile, channels))] * 4 + [whole(gains.shape), whole((8, LANES))],
        ),
        out_shape=[jax.ShapeDtypeStruct((3 * tile, channels), F32)] * 4
        + [jax.ShapeDtypeStruct(gains.shape, F32), jax.ShapeDtypeStruct((8, LANES), F32)],
        compiler_params=pltpu.CompilerParams(vmem_limit_bytes=VMEM_LIMIT),
        cost_estimate=SMALL_COST,
        name="weight_grads",
    )(core, normed, low, cot, mixed, *weights, gains, *deps)
    chain.last = results[-1]
    return results[:4], results[4]


def run_assemble(chain, core, own, got, unit):
    rows, channels = own[0].shape
    tile = rows // 3
    deps = chain.deps()

    def kernel(place, own_a, own_b, got_a, got_b, *refs):
        gate, value, out, token = refs[len(deps) :]
        i = pl.program_id(0)
        token[...] = jnp.zeros((8, LANES), F32)
        for n, (mine, other) in enumerate(((own_a, got_a), (own_b, got_b))):

            @pl.when(i % 2 == n)
            def _(mine=mine, other=other):
                use_own = i // 2 == place[0]
                pieces = []
                for k in range(rows // unit):
                    at = slice(k * unit, (k + 1) * unit)
                    pieces.append(jnp.where(use_own, mine[at, :], other[at, :]))
                gate[...] = jnp.concatenate(pieces[0::3], axis=0)
                value[...] = jnp.concatenate(pieces[1::3], axis=0)
                out[...] = jnp.concatenate(pieces[2::3], axis=0).T

    row = pl.BlockSpec((tile, channels), lambda i, p: (i, 0))
    gate, value, out, chain.last = pl.pallas_call(
        kernel,
        grid_spec=pltpu.PrefetchScalarGridSpec(
            num_scalar_prefetch=1,
            grid=(4,),
            in_specs=[whole(own[0].shape)] * 4 + [ANYWHERE for _ in deps],
            out_specs=[
                row,
                row,
                pl.BlockSpec((channels, tile), lambda i, p: (0, i)),
                whole((8, LANES)),
            ],
        ),
        out_shape=[
            jax.ShapeDtypeStruct((D, channels), F32),
            jax.ShapeDtypeStruct((D, channels), F32),
            jax.ShapeDtypeStruct((channels, D), F32),
            jax.ShapeDtypeStruct((8, LANES), F32),
        ],
        compiler_params=pltpu.CompilerParams(vmem_limit_bytes=VMEM_LIMIT),
        cost_estimate=SMALL_COST,
        name="assemble",
    )(core, *own, *got, *deps)
    return gate, value, out


def run_total(chain, low, weights):
    length, width = low.shape

    def body(left, gate_w, value_w, state_w, step_w, out, token, joined):
        @pl.when(pl.program_id(0) == 0)
        def _():
            at = 0
            for ref in (gate_w, value_w, state_w, step_w):
                joined[:, at : at + ref.shape[1]] = ref[...]
                at += ref.shape[1]

        out[...] = matmul(left[...], joined[...], (1, 1))

    (out,) = run_matmul(
        chain,
        body,
        [(low, (CHUNK, width), lambda i: (i, 0))] + [(w, None, None) for w in weights],
        [((length, D), (CHUNK, D), lambda i: (i, 0))],
        length // CHUNK,
        scratch=[pltpu.VMEM((D, width), BF16)],
        name="normed_grad",
    )
    return out


def whole(shape):
    return pl.BlockSpec(shape, lambda i, *_: (0,) * len(shape))


ANYWHERE = pl.BlockSpec(memory_space=pl.ANY)


def run_forward(start, count, chunks, tokens, cot, seg, small, carried, kept, deps):
    channels = small["gate_w"].shape[1]
    states = 2 * LANES
    size = CHUNK
    length = count * size
    first = start // size
    per = size // BLOCK
    full = tokens.shape[0]

    def row_in(width):
        return pl.BlockSpec((size, width), lambda i: (first + i, 0))

    def row_out(width):
        return pl.BlockSpec((size, width), lambda i: (i, 0))

    def chunk_out(index):
        each = count // chunks
        return pl.BlockSpec((size, D), lambda i: (jnp.clip(i - index * each, 0, each - 1), 0))

    constant = [small[n] for n in ("par", "gate_w", "value_w", "state_w", "step_w", "out_w")]
    carry_shapes = [(LANES, channels), (8, channels), (8, states)]
    widths = (
        (channels, F32),
        (channels, BF16),
        (channels, F32),
        (channels, F32),
        (states, BF16),
        (states, F32),
        (LANES, F32),
    )
    inputs = [tokens, cot, seg, *constant, *carried, *deps, *kept]
    outs = pl.pallas_call(
        functools.partial(
            forward_kernel, not carried, len(deps) + len(kept), start // BLOCK, chunks
        ),
        grid=(count,),
        in_specs=[row_in(D), row_in(D), whole(seg.shape)]
        + [whole(c.shape) for c in constant]
        + [whole(c.shape) for c in carried]
        + [ANYWHERE for _ in deps + kept],
        out_specs=[row_out(w) for w, _ in widths]
        + [pl.BlockSpec((per, LANES, channels), lambda i: (i, 0, 0))]
        + [pl.BlockSpec((8, size), lambda i: (0, first + i))]
        + [row_in(D)]
        + [whole(c) for c in carry_shapes]
        + [chunk_out(index) for index in range(chunks)],
        out_shape=[jax.ShapeDtypeStruct((length, w), k) for w, k in widths]
        + [jax.ShapeDtypeStruct((length // BLOCK, LANES, channels), BF16)]
        + [jax.ShapeDtypeStruct((8, full), F32)]
        + [jax.ShapeDtypeStruct((full, D), BF16)]
        + [jax.ShapeDtypeStruct(c, F32) for c in carry_shapes]
        + [jax.ShapeDtypeStruct((length // chunks, D), F32)] * chunks,
        scratch_shapes=[
            pltpu.VMEM((size + 8, channels), F32),
            pltpu.VMEM((size + 8, states), F32),
            pltpu.VMEM((size, channels), BF16),
            pltpu.VMEM((size, D), F32),
        ],
        input_output_aliases={len(inputs) - len(kept) + k: 8 + k for k in range(len(kept))},
        compiler_params=pltpu.CompilerParams(vmem_limit_bytes=VMEM_LIMIT),
        cost_estimate=SMALL_COST,
        name="forward_piece",
    )(*inputs)
    outs = list(outs)
    names = ("gate", "vraw", "pv", "y", "sraw", "spv", "step", "saved")
    return dict(zip(names, outs[:8])), outs[8:10], outs[10:13], outs[13:]


def run_backward(start, piece, og, stats, place, seg, small, carried, low, mixed, deps):
    channels = small["gate_w"].shape[1]
    length = piece["gate"].shape[0]
    full = og.shape[0]
    count = length // BLOCK
    first = start // BLOCK
    flip = lambda i: count - 1 - i

    def row(width):
        return pl.BlockSpec((BLOCK, width), lambda i, *_: (flip(i), 0))

    def shared(width):
        return pl.BlockSpec((BLOCK, width), lambda i, *_: (first + flip(i), 0))

    names = ("gate", "vraw", "pv", "y", "sraw", "spv", "step")
    ins = [piece[n] for n in names]
    low_width = 2 * channels + 3 * LANES
    kept = [] if low is None else [low, mixed]
    carry_shapes = [
        (LANES, channels),
        (8, channels),
        (8, 2 * LANES),
        (56, channels),
        (40, 2 * LANES),
        (16, LANES),
    ]
    inputs = [og, *ins, *stats, piece["saved"], seg, small["par"], *carried, *deps, *kept]
    outs = pl.pallas_call(
        functools.partial(
            backward_kernel, not carried, len(deps) + len(kept), first, full // BLOCK
        ),
        grid_spec=pltpu.PrefetchScalarGridSpec(
            num_scalar_prefetch=1,
            grid=(count,),
            in_specs=[shared(channels)]
            + [row(a.shape[1]) for a in ins]
            + [pl.BlockSpec((8, BLOCK), lambda i, *_: (0, first + flip(i))) for _ in stats]
            + [pl.BlockSpec((1, LANES, channels), lambda i, *_: (flip(i), 0, 0))]
            + [whole(seg.shape), whole(small["par"].shape)]
            + [whole(c.shape) for c in carried]
            + [ANYWHERE for _ in deps + kept],
            out_specs=[shared(low_width), shared(channels)] + [whole(c) for c in carry_shapes],
        ),
        out_shape=[
            jax.ShapeDtypeStruct((full, low_width), BF16),
            jax.ShapeDtypeStruct((full, channels), BF16),
        ]
        + [jax.ShapeDtypeStruct(c, F32) for c in carry_shapes],
        compiler_params=pltpu.CompilerParams(vmem_limit_bytes=VMEM_LIMIT),
        cost_estimate=SMALL_COST,
        input_output_aliases={1 + len(inputs) - 2 + k: k for k in range(len(kept))},
        name="backward_piece",
    )(place, *inputs)
    return outs[0], outs[1], list(outs[2:])


class Chain:
    def __init__(self):
        self.last = None
        self.more = []

    def deps(self):
        found = ([] if self.last is None else [self.last]) + self.more
        self.more = []
        return found


def rowwise(
    chain, place, body, ins, outs, rows, passes=(), step=0, whole_place=False, name=None
):
    step = step or STEP
    steps = rows // step

    def spec(width, first, most=steps, where=None):
        if where is not None:
            base = first if callable(first) else lambda p: first
            return pl.BlockSpec(
                (step, width),
                lambda i, p: (
                    jnp.where(where(p[0]), base(p[0]) + jnp.minimum(i, most - 1), 0),
                    0,
                ),
            )
        if callable(first):
            return pl.BlockSpec(
                (step, width),
                lambda i, p: (
                    jnp.maximum(first(p if whole_place else p[0]) + jnp.minimum(i, most - 1), 0),
                    0,
                ),
            )
        return pl.BlockSpec((step, width), lambda i, p: (first + jnp.minimum(i, most - 1), 0))

    def lying(height, first):
        if callable(first):
            return pl.BlockSpec((height, STEP), lambda i, p: (0, first(p[0]) + i))
        return pl.BlockSpec((height, STEP), lambda i, p: (0, first + i))

    def spec_of(array, first, across=False, most=steps, where=None):
        if first is None:
            return fixed(array.shape)
        return lying(array.shape[0], first) if across else spec(array.shape[1], first, most, where)

    def fixed(shape):
        return pl.BlockSpec(shape, lambda i, p: (0,) * len(shape))

    anywhere = pl.BlockSpec(memory_space=pl.ANY)
    arrays = [entry[0] for entry in ins]
    in_specs = [spec_of(*entry) for entry in ins]
    kept = [(k, o[4]) for k, o in enumerate(outs) if o[4] is not None]
    deps = chain.deps()
    inputs = [*arrays, *[a for _, a in kept], *passes, *deps]
    aliases = {1 + len(arrays) + n: k for n, (k, _) in enumerate(kept)}
    for n in range(len(passes)):
        aliases[1 + len(arrays) + len(kept) + n] = len(outs) + n

    def kernel(place_ref, *refs):
        results = refs[len(inputs) :]
        values = body(place_ref if whole_place else place_ref[0], *refs[: len(arrays)])
        for ref, value in zip(results[: len(outs)], values):
            ref[...] = value
        results[-1][...] = jnp.zeros((8, LANES), F32)

    results = pl.pallas_call(
        kernel,
        grid_spec=pltpu.PrefetchScalarGridSpec(
            num_scalar_prefetch=1,
            grid=(steps,),
            in_specs=in_specs + [anywhere] * (len(inputs) - len(arrays)),
            out_specs=[spec(o[1], o[3], *o[5:]) for o in outs]
            + [anywhere] * len(passes)
            + [fixed((8, LANES))],
        ),
        out_shape=[jax.ShapeDtypeStruct((o[0], o[1]), o[2]) for o in outs]
        + [jax.ShapeDtypeStruct(p.shape, p.dtype) for p in passes]
        + [jax.ShapeDtypeStruct((8, LANES), F32)],
        input_output_aliases=aliases,
        compiler_params=pltpu.CompilerParams(vmem_limit_bytes=VMEM_LIMIT),
        cost_estimate=SMALL_COST,
        name=name,
    )(place, *inputs)
    chain.last = results[-1]
    return list(results[:-1])


def after(chain, *arrays):
    def kernel(*refs):
        refs[-1][...] = jnp.zeros((8, LANES), F32)

    anywhere = pl.BlockSpec(memory_space=pl.ANY)
    deps = chain.deps()
    results = pl.pallas_call(
        kernel,
        in_specs=[anywhere] * (len(arrays) + len(deps)),
        out_specs=[anywhere] * len(arrays) + [pl.BlockSpec(memory_space=pltpu.VMEM)],
        out_shape=[jax.ShapeDtypeStruct(a.shape, a.dtype) for a in arrays]
        + [jax.ShapeDtypeStruct((8, LANES), F32)],
        input_output_aliases={k: k for k in range(len(arrays))},
        cost_estimate=SMALL_COST,
        name="in_order",
    )(*arrays, *deps)
    chain.last = results[-1]
    return list(results[:-1])


INWARD = ((0, 1), (3, 2))
ACROSS = ((1, 2), (2, 1))
OUTWARD = ((1, 0), (2, 3))


def on_device(
    tokens,
    norm_gain,
    gate_weight,
    value_weight,
    state_weight,
    step_weight,
    value_kernel,
    value_bias,
    state_kernel,
    state_bias,
    step_bias,
    decay_log,
    skip_scale,
    gated_gain,
    out_weight,
    segment_ids,
    out_cotangent,
):
    parts = lax.axis_size("tensor")
    place = lax.axis_index("tensor")
    middle = jnp.logical_and(place > 0, place < parts - 1)
    length = tokens.shape[0]
    channels = gate_weight.shape[1]
    head_count = step_bias.shape[0]
    rows = length // parts
    states = 2 * LANES
    where = place.astype(jnp.int32)[None]
    par, step_wide, step_place = run_pack(
        where,
        norm_gain,
        value_kernel,
        value_bias,
        gated_gain,
        skip_scale,
        state_kernel,
        state_bias,
        step_bias,
        decay_log,
        step_weight.T,
    )
    small = {
        "gate_w": gate_weight,
        "value_w": value_weight,
        "state_w": state_weight,
        "step_w": step_wide,
        "out_w": out_weight,
        "par": par,
    }
    chain = Chain()
    send = lambda x, pairs: lax.ppermute(x, "tensor", pairs)
    run = functools.partial(rowwise, chain, where)
    steps = lambda n: n // STEP

    piece_spans = [p * length // sum(PIECES) for p in PIECES]
    piece_firsts = [sum(piece_spans[:k]) for k in range(len(piece_spans))]
    pieces = []
    partials = []
    spans = [length // sum(PIECES)] * sum(PIECES)
    firsts = [sum(spans[:k]) for k in range(len(spans))]
    carried = []
    kept = []
    late = {}
    count = len(spans)
    outer, inner, outer_sent, pair_sum = {}, {}, {}, {}

    def forward():
        nonlocal carried, kept
        k = len(pieces)
        outs, kept, carried, made = run_forward(
            piece_firsts[k],
            piece_spans[k] // CHUNK,
            PIECES[k],
            tokens,
            out_cotangent,
            segment_ids,
            small,
            carried,
            kept,
            chain.deps(),
        )
        partials.extend(made)
        pieces.append(outs)
        chain.last = carried[2]


    def send_outer(n, message, both=True):
        outer_sent[n] = message
        outer[n] = send(message, INWARD + OUTWARD if both else INWARD)

    is_middle = lambda p: jnp.logical_and(p > 0, p < parts - 1)
    per = steps(rows)
    at_ends = lambda low_end, high_end: lambda p: jnp.where(p < 2, low_end, high_end) * per

    def event(n, following=None, middle_segment=None):
        chunk = n < count
        step = STEP
        blocks = spans[0] // step
        size = spans[0]
        is_end = lambda p: jnp.logical_not(is_middle(p))
        if chunk:
            mine = (partials[n], 0, False, blocks, is_middle)
        else:
            mine = (late["total"], middle_segment, False, blocks, is_middle)
        ins = [mine, (outer[n], 0, False, blocks, is_middle)]
        outs = [(size, D, F32, 0, None, blocks, is_middle)]
        if n > 0:
            array, first = following
            from_middle = (inner[n], 0, False, blocks, is_middle)
            if n <= count:
                ins += [(pair_sum[n - 1], 0, False, blocks, is_middle), from_middle]
                ins += [(array, first, False, blocks, is_end)]
            else:
                ins += [(array, first, False, blocks), from_middle]
            outs.append((spans[0], D, F32, 0, None, blocks))

        def body(p, a, b, *others):
            value = a[...] + b[...]
            results = [value]
            if n > 0:
                message = others[0][...] + others[1][...]
                if n <= count:
                    message = jnp.where(is_middle(p), message, others[2][...])
                results.append(message)
            return results

        results = run(body, ins, outs, size, step=step, name="event")
        if n == 0:
            chain.more = late["stats"][1:]
            results = after(chain, *results)
        pair_sum[n] = results[0]
        inner[n + 1] = send(results[0], ACROSS)
        if n > 0:
            send_outer(n + 1, results[1])
        else:
            send_outer(1, following[0], False)

    def finish_chunk(k):
        def body(p, own, got, token, *stats):
            inside = jnp.logical_and(p > 0, p < parts - 1)
            total = jnp.where(inside, own[...], got[...])
            table = upright(sum_over_places(p, stats[0][...], [x[...] for x in stats[1:]]))
            strength = lax.rsqrt(table[:, 0:1] / INNER + EPS)
            return [(token[...].astype(F32) + total * strength).astype(BF16)]

        first = steps(firsts[k])
        (late["block_out"],) = run(
            body,
            [(outer_sent[k + 2], 0), (outer[k + 2], 0), (tokens, first)]
            + [(x, first, True) for x in late["stats"]],
            [(length, D, BF16, first, late.get("block_out"))],
            spans[k],
            name="finish_chunk",
        )

    def finish_grad(n):
        def body(p, mine, side_got, middle_got, token, scale, cot, gain):
            token = token[...].astype(F32)
            scale = upright(scale[...])[:, 2:3]
            weighted = (mine[...] + side_got[...] + middle_got[...]) * gain[...]
            pull = jnp.sum(weighted * token, axis=-1, keepdims=True) / D
            return [cot[...].astype(F32) + scale * weighted - token * scale * scale * scale * pull]

        mine = lambda p: p * per
        (late["tokens_grad"],) = run(
            body,
            [
                (late["total"], mine),
                (outer[n], 0),
                (inner[n], 0),
                (tokens, mine),
                (late["own_stats"], mine, True),
                (out_cotangent, mine),
                (norm_gain[None], None),
            ],
            [(rows, D, F32, 0, None)],
            rows,
            name="finish_grad",
        )

    low = mixed = None
    back = []

    def backward(k):
        nonlocal low, mixed, back
        low, mixed, back = run_backward(
            piece_firsts[k],
            pieces[k],
            late["og"],
            late["stats"],
            where,
            segment_ids,
            small,
            back,
            low,
            mixed,
            chain.deps(),
        )
        chain.last = back[2]

    def exchange_stats():
        own = late["own_stats"] = kept[0]
        late["stats"] = [own] + [
            send(own, [(k, (k + turn) % parts) for k in range(parts)]) for turn in range(1, parts)
        ]

    forward()
    send_outer(0, partials[0], False)
    late["og"], _ = run_out_grad(chain, out_cotangent, out_weight, [])
    forward()
    exchange_stats()
    event(0, (partials[1], 0))
    backward(1)
    backward(0)
    event(1, (partials[2], 0))

    normed = kept[1]
    wide_acc, narrow_acc, heads_acc = back[3:]
    back_weights = [gate_weight, value_weight, state_weight, step_place]
    width = 3 * LANES
    fit = lambda x: jnp.pad(x.reshape(-1), (0, -x.size % width)).reshape(-1, width)
    narrow = narrow_acc.reshape(5, 8, states).sum(axis=1)
    wide_sums = wide_acc.reshape(7, 8, channels).sum(axis=1)
    head_sums = heads_acc.reshape(2, 8, LANES).sum(axis=1)[:, :head_count]
    skip_grad = wide_sums[6].reshape(head_count, channels // head_count).sum(axis=1)
    mine = jnp.concatenate([fit(wide_sums[:6]), fit(jnp.concatenate([head_sums, skip_grad[None]]))])
    mine_rows = mine.shape[0]
    slots = jnp.where(
        lax.broadcasted_iota(jnp.int32, (parts, 1, 1), 0) == place, mine[None], 0.0
    ).reshape(-1, width)
    narrow_rows = fit(narrow)
    filler = jnp.zeros((CHUNK - narrow_rows.shape[0] - slots.shape[0], width), F32)
    shared, gains = run_rest_grad(
        chain, normed, low, jnp.concatenate([narrow_rows, slots, filler]), back_weights[2:]
    )

    ways = lax.axis_size("dp")
    own_dp = lax.axis_index("dp")
    bits = []
    while 2 ** len(bits) < ways:
        bits.append(2 ** len(bits))
    shared_rows = shared.shape[0]
    swap = lambda x, bit: lax.ppermute(x, "dp", [(k, k ^ bit) for k in range(ways)])
    side = lambda n: (own_dp // bits[n]) % 2
    halving = {"keep": shared, "rows": shared_rows, "got": None}

    def halve(n):
        keep, size = halving["keep"], halving["rows"]
        if n > 0:
            add = lambda p, a, b: [a[...] + b[...]]
            size = size // 2
            (keep,) = rowwise(
                chain,
                side(n - 1).astype(jnp.int32)[None],
                add,
                [(keep, lambda p: p), (halving["got"], 0)],
                [(size, width, F32, 0, None)],
                size,
                step=size,
                name="halve",
            )
            halving["rows"] = size
        if n < len(bits):
            away = lax.dynamic_slice_in_dim(keep, (1 - side(n)) * (size // 2), size // 2, 0)
            halving["got"] = swap(away, bits[n])
        halving["keep"] = keep

    core = side(0).astype(jnp.int32)[None]
    core_bit, axes = bits[0], list(range(1, len(bits)))
    turned = axes[len(axes) // 2 :] + axes[: len(axes) // 2]
    orders = (axes, turned)
    sums = {}

    def reduce_step(step):
        sides = jnp.stack([side(orders[k][step]).astype(jnp.int32) for k in range(2)])
        ins, outs = [], []
        size = sums["keep"][0].shape[0] // 2
        unit = size if size < 512 else size // 2
        for k in range(2):
            for stay in (1, 0):
                at = functools.partial(
                    lambda p, k, stay: (p[k] if stay else 1 - p[k]) * (size // unit), k=k, stay=stay
                )
                ins += [(sums["keep"][k], at), (sums["got"][k], at)]
                outs.append((size, channels, F32, 0, None))
        results = rowwise(
            chain,
            sides,
            lambda p, *refs: [refs[2 * n][...] + refs[2 * n + 1][...] for n in range(4)],
            ins,
            outs,
            size,
            step=unit,
            whole_place=True,
            name="reduce_step",
        )
        sums["keep"] = [results[0], results[2]]
        sums["size"] = size
        sums["got"] = [swap(results[2 * k + 1], bits[orders[k][step]]) for k in range(2)]

    unit = D // 4 // 2 ** len(axes)

    def reduce_start():
        tiles, sums["gains"] = run_weight_grads(
            chain, core, normed, low, out_cotangent, mixed, back_weights[:2], gains, unit
        )
        sums["keep"] = tiles[2:]
        sums["got"] = [swap(x, core_bit) for x in tiles[:2]]

    def gather_first():
        sums["full"] = rowwise(
            chain,
            where,
            lambda p, a, b, c, d: [a[...] + b[...], c[...] + d[...]],
            [(x, 0) for k in range(2) for x in (sums["keep"][k], sums["got"][k])],
            [(sums["size"], channels, F32, 0, None)] * 2,
            sums["size"],
            step=sums["size"],
            name="gather_first",
        )
        step = len(axes) - 1
        sums["got"] = [swap(sums["full"][k], bits[orders[k][step]]) for k in range(2)]

    def gather_step(step):
        size = sums["size"]
        sides = jnp.stack([side(orders[k][step]).astype(jnp.int32) for k in range(2)])

        def body(p, *refs):
            upper = pl.program_id(0)
            picked = []
            for k in range(2):
                own, got = refs[2 * k][...], refs[2 * k + 1][...]
                picked.append(jnp.where(upper == p[k], own, got))
            return picked

        sums["full"] = rowwise(
            chain,
            sides,
            body,
            [(x, 0, False, 1) for k in range(2) for x in (sums["full"][k], sums["got"][k])],
            [(2 * size, channels, F32, 0, None)] * 2,
            2 * size,
            step=size,
            whole_place=True,
            name="gather_step",
        )
        sums["size"] = 2 * size
        if step > 0:
            sums["got"] = [swap(sums["full"][k], bits[orders[k][step - 1]]) for k in range(2)]

    def gather_core():
        sums["got"] = [swap(x, core_bit) for x in sums["full"]]

    halve(0)
    reduce_start()
    gain_rows = fit(sums["gains"][0] / norm_gain)
    gain_rows = jnp.pad(gain_rows, ((0, 8 - gain_rows.shape[0]), (0, 0)))
    halve(1)
    event(2, (partials[3], 0))

    halve(2)
    reduce_step(0)
    late["total"] = run_total(chain, low, back_weights)
    finish_chunk(0)
    event(3, (late["total"], at_ends(3, 0)))

    for step in range(1, len(axes)):
        reduce_step(step)
    gather_first()
    finish_chunk(1)
    for step in range(len(axes) - 1, 0, -1):
        gather_step(step)
    for n in range(3, len(bits) + 1):
        halve(n)
    share = jnp.concatenate([halving["keep"], gain_rows])
    share = lax.psum(share, "tensor")
    event(4, (late["total"], at_ends(2, 1)), at_ends(3, 0))

    gather_step(0)
    gather_core()
    finish_chunk(2)
    event(5, (late["total"], lambda p: jnp.where(p < 2, 1 - p, 5 - p) * per), at_ends(2, 1))

    (share,) = after(chain, share)
    share = lax.all_gather(share, "dp")
    finish_chunk(3)
    gate_weight_grad, value_weight_grad, out_weight_grad = run_assemble(
        chain, core, sums["full"], sums["got"], unit
    )

    places = np.array(
        [sum((k >> n & 1) << (len(bits) - 1 - n) for n in range(len(bits))) for k in range(ways)]
    )
    order = np.argsort(places)
    gain_sums = share[:, -8:].sum(axis=0)
    share = jnp.concatenate([share[k, :-8] for k in order] + [gain_sums])
    shared = share
    norm_gain_grad = shared[-8:].reshape(-1)[:D]
    rest, shared = shared[:D], shared[D:]
    state_weight_grad = rest[:, :states]
    step_weight_grad = lax.dynamic_slice(rest, (0, states + place * head_count), (D, head_count))
    at = narrow_rows.shape[0]
    narrow = shared[:at].reshape(-1)[: 5 * states].reshape(5, states)
    mine = lax.dynamic_slice_in_dim(shared, at + place * mine_rows, mine_rows, 0).reshape(-1)
    wide_sums = mine[: 6 * channels].reshape(6, channels)
    head_sums = mine[6 * channels :][: 3 * head_count].reshape(3, head_count)
    chain.more = [state_weight_grad, step_weight_grad, norm_gain_grad, narrow, wide_sums, head_sums]
    finish_grad(6)
    return (
        late["block_out"],
        late["tokens_grad"],
        norm_gain_grad,
        gate_weight_grad,
        value_weight_grad,
        state_weight_grad,
        step_weight_grad,
        wide_sums[:4],
        wide_sums[4],
        narrow[:4],
        narrow[4],
        head_sums[0],
        head_sums[1],
        head_sums[2],
        wide_sums[5],
        out_weight_grad,
    )


def solution(mesh):
    placed = (
        P("dp", None),
        P(),
        P(None, "tensor"),
        P(None, "tensor"),
        P(),
        P(None, "tensor"),
        P(None, "tensor"),
        P("tensor"),
        P(),
        P(),
        P("tensor"),
        P("tensor"),
        P("tensor"),
        P("tensor"),
        P("tensor", None),
        P("dp", None),
        P("dp", None),
    )
    return jax.shard_map(
        on_device,
        mesh=mesh,
        in_specs=placed,
        out_specs=(
            P("dp", None),
            P(("dp", "tensor"), None),
            P(),
            P(None, "tensor"),
            P(None, "tensor"),
            P(),
            P(None, "tensor"),
            P(None, "tensor"),
            P("tensor"),
            P(),
            P(),
            P("tensor"),
            P("tensor"),
            P("tensor"),
            P("tensor"),
            P("tensor", None),
        ),
        check_vma=False,
    )
```

```python
import functools

import jax
import jax.numpy as jnp
import numpy as np
from jax import lax
from jax.experimental import pallas as pl
from jax.experimental.pallas import tpu as pltpu
from jax.sharding import PartitionSpec as P

D = 1536
INNER = 3072
EPS = 1e-05
BLOCK = 128
LANES = 128
FAR = -1e30
F32 = jnp.float32
BF16 = jnp.bfloat16
CHUNK = 256
STEP = 128
ROWS = 32
VMEM_LIMIT = 63 * 2**20
SMALL_COST = pl.CostEstimate(flops=1, bytes_accessed=1, transcendentals=0)
PIECES = (1, 3)


def matmul(left, right, dims=(1, 0)):
    return lax.dot_general(
        left, right, (((dims[0],), (dims[1],)), ((), ())), preferred_element_type=F32
    )


def exact(left, right):
    return lax.dot_general(
        left,
        right,
        (((1,), (0,)), ((), ())),
        precision=lax.Precision.HIGHEST,
        preferred_element_type=F32,
    )


def sigmoid(v):
    return 0.5 * jnp.tanh(0.5 * v) + 0.5


def softplus(v):
    return jnp.maximum(v, 0.0) + jnp.log1p(jnp.exp(-jnp.abs(v)))


def fold(x):
    return x.reshape(x.shape[0] // 8, 8, x.shape[1]).sum(axis=0)


def triangle(lower):
    row = lax.broadcasted_iota(jnp.int32, (BLOCK, BLOCK), 0)
    col = lax.broadcasted_iota(jnp.int32, (BLOCK, BLOCK), 1)
    return jnp.where(row >= col if lower else row <= col, 1.0, 0.0).astype(F32)


def group_sum(x, spread):
    high = x.astype(BF16)
    low = (x - high.astype(F32)).astype(BF16)
    return matmul(high, spread) + matmul(low, spread)


def upright(rows):
    fill = jnp.zeros((BLOCK - rows.shape[0], BLOCK), F32)
    return jnp.concatenate([rows, fill], axis=0).T


def segment_columns(seg_ref, block, blocks, ahead):
    part = lambda k: seg_ref[:, pl.ds(pl.multiple_of(k * BLOCK, BLOCK), BLOCK)].astype(F32)
    ids = part(block)
    before = jnp.where(block > 0, part(jnp.maximum(block - 1, 0)), -1.0)
    lane = lax.broadcasted_iota(jnp.int32, (1, BLOCK), 1)
    rows = [ids]
    if ahead:
        behind = jnp.where(block < blocks - 1, part(jnp.minimum(block + 1, blocks - 1)), -1.0)
    for far in range(1, 4):
        if ahead:
            moved = jnp.where(
                lane >= BLOCK - far,
                pltpu.roll(behind, BLOCK - far, 1),
                pltpu.roll(ids, BLOCK - far, 1),
            )
        else:
            moved = jnp.where(lane < far, pltpu.roll(before, far, 1), pltpu.roll(ids, far, 1))
        rows.append(jnp.where(moved == ids, 1.0, 0.0))
    rows.append(jnp.where(ids == before[:, BLOCK - 1 :], 1.0, 0.0))
    rows.append(jnp.where(ids == ids[:, BLOCK - 1 :], 1.0, 0.0))
    rows.append(jnp.zeros((2, BLOCK), F32))
    return upright(jnp.concatenate(rows, axis=0)), ids


def decay_terms(step_raw, step_bias, rate, cols, seg_row):
    steps = softplus(step_raw + step_bias)
    rates = -steps * rate
    local = exact(triangle(True), rates)
    last = local[BLOCK - 1 :]
    into = jnp.exp(jnp.where(cols[:, 4:5] > 0.5, local, FAR))
    out = jnp.exp(jnp.where(cols[:, 5:6] > 0.5, last - local, FAR))
    row = lax.broadcasted_iota(jnp.int32, (BLOCK, BLOCK), 0)
    col = lax.broadcasted_iota(jnp.int32, (BLOCK, BLOCK), 1)
    allowed = jnp.logical_and(row >= col, cols[:, 0:1] == seg_row)
    bias = jnp.where(allowed, 0.0, FAR)
    return steps, rates, local, local.T, into, out, bias


def pairwise(x, pair, half):
    return jnp.where(half, x[:, 2 * pair : 2 * pair + 1], x[:, 2 * pair + 1 : 2 * pair + 2])


def split_pair(x, half):
    zero = jnp.zeros_like(x)
    return jnp.concatenate([jnp.where(half, x, zero), jnp.where(half, zero, x)], axis=0)


def decay_of(local, local_t, bias, head):
    return jnp.exp(local[:, head : head + 1] - local_t[head : head + 1, :] + bias)


def sum_over_places(place, own, others):
    parts = len(others) + 1
    total = None
    for k in range(parts):
        value = own
        for turn in range(1, parts):
            value = jnp.where((place - k + parts) % parts == turn, others[turn - 1], value)
        total = value if total is None else total + value
    return total


GAIN_ROW, KERNEL_ROW, BIAS_ROW, GATED_ROW, SKIP_ROW = 0, 2, 6, 7, 8
STATE_KERNEL_ROW, STATE_BIAS_ROW, STEP_ROW, DECAY_ROW = 9, 13, 14, 15


def run_pack(place, *arrays):
    channels = arrays[1].shape[1]

    def kernel(place_ref, *refs):
        (norm_gain, kernel, bias, gated, skip, state_kernel, state_bias, step_bias, decay, step_w) = refs[
            :10
        ]
        table, wide, placed = refs[10:]
        table[...] = jnp.zeros_like(table)
        table[GAIN_ROW : GAIN_ROW + 1, :] = norm_gain[:channels].reshape(1, channels)
        table[GAIN_ROW + 1 : GAIN_ROW + 2, :] = norm_gain[channels:].reshape(1, channels)
        table[KERNEL_ROW : KERNEL_ROW + 4, :] = kernel[...]
        table[STATE_KERNEL_ROW : STATE_KERNEL_ROW + 4, : state_kernel.shape[1]] = state_kernel[...]
        rows = ((BIAS_ROW, bias), (GATED_ROW, gated), (SKIP_ROW, skip), (STATE_BIAS_ROW, state_bias))
        for row, ref in rows + ((STEP_ROW, step_bias), (DECAY_ROW, decay)):
            size = ref.shape[0]
            table[row : row + 1, :size] = ref[...].reshape(1, size)
        rows = step_w[...].astype(F32)
        fill = jnp.zeros((LANES - rows.shape[0], rows.shape[1]), F32)
        columns = jnp.concatenate([rows, fill], axis=0).T
        wide[...] = columns.astype(BF16)
        placed[...] = pltpu.roll(columns, place_ref[0] * rows.shape[0], 1).astype(BF16)

    return pl.pallas_call(
        kernel,
        out_shape=[
            jax.ShapeDtypeStruct((16, channels), F32),
            jax.ShapeDtypeStruct((arrays[-1].shape[1], LANES), BF16),
            jax.ShapeDtypeStruct((arrays[-1].shape[1], LANES), BF16),
        ],
        in_specs=[pl.BlockSpec(memory_space=pltpu.SMEM)]
        + [pl.BlockSpec(memory_space=pltpu.VMEM) for _ in arrays],
        cost_estimate=SMALL_COST,
        name="pack",
    )(place, *arrays)


def forward_kernel(first_piece, unused, block_base, chunks, *refs):
    tokens, cot, seg, par, gate_w, value_w, state_w, step_w, out_w = refs[:9]
    refs = refs[9:]
    if not first_piece:
        state_in, tail_in, state_tail_in = refs[:3]
        refs = refs[3:]
    refs = refs[unused:]
    (
        gate_out,
        vraw_out,
        pv_out,
        y_out,
        sraw_out,
        spv_out,
        step_out,
        saved_out,
        stats_out,
        normed_out,
        state,
        tail_out,
        state_tail_out,
    ) = refs[:13]
    partial_outs = refs[13 : 13 + chunks]
    vbuf, sbuf, scaled, partial = refs[13 + chunks :]
    size = tokens.shape[0]
    channels = gate_w.shape[1]
    states = 2 * LANES

    @pl.when(pl.program_id(0) == 0)
    def _():
        if first_piece:
            state[...] = jnp.zeros_like(state)
            vbuf[:8] = jnp.zeros((8, channels), F32)
            sbuf[:8] = jnp.zeros((8, states), F32)
        else:
            state[...] = state_in[...]
            vbuf[:8] = tail_in[...]
            sbuf[:8] = state_tail_in[...]

    norm_gain = jnp.concatenate([par[GAIN_ROW : GAIN_ROW + 1], par[GAIN_ROW + 1 : GAIN_ROW + 2]], axis=1)
    scales = []
    for row in range(0, size, ROWS):
        wide = tokens[row : row + ROWS].astype(F32)
        scale = lax.rsqrt(jnp.mean(wide * wide, axis=-1, keepdims=True) + EPS)
        normed_out[row : row + ROWS] = (wide * scale * norm_gain).astype(BF16)
        scales.append(scale)
    normed = normed_out[...]
    vbuf[8:] = matmul(normed, value_w[...])
    sbuf[8:] = matmul(normed, state_w[...])
    step_out[...] = matmul(normed, step_w[...])
    gate_out[...] = matmul(normed, gate_w[...])

    def conv(buf, row, lanes, cols, kernel_row, bias_row):
        raw = buf[row + 8 : row + 8 + BLOCK, lanes]
        total = par[bias_row : bias_row + 1, lanes] + raw * par[kernel_row + 3 : kernel_row + 4, lanes]
        for back in range(1, 4):
            tap = par[kernel_row + 3 - back : kernel_row + 4 - back, lanes]
            moved = buf[row + 8 - back : row + 8 - back + BLOCK, lanes]
            total = total + moved * tap * cols[:, back : back + 1]
        return raw, total

    half = lax.broadcasted_iota(jnp.int32, (BLOCK, LANES), 1) < LANES // 2
    half_row = half[0:1]
    lane = lax.broadcasted_iota(jnp.int32, (BLOCK, LANES), 1)
    step_bias = par[STEP_ROW : STEP_ROW + 1, :LANES]
    rate = jnp.exp(par[DECAY_ROW : DECAY_ROW + 1, :LANES])
    skips = par[SKIP_ROW : SKIP_ROW + 1, :LANES]
    squares = []
    for sub in range(size // BLOCK):
        rows = slice(sub * BLOCK, (sub + 1) * BLOCK)
        row = sub * BLOCK
        block = block_base + pl.program_id(0) * (size // BLOCK) + sub
        cols, seg_row = segment_columns(seg, block, None, False)
        mixed_state = []
        for part in range(2):
            lanes = slice(part * LANES, (part + 1) * LANES)
            raw, spv = conv(sbuf, row, lanes, cols, STATE_KERNEL_ROW, STATE_BIAS_ROW)
            sraw_out[rows, lanes] = raw.astype(BF16)
            spv_out[rows, lanes] = spv
            mixed_state.append(spv * sigmoid(spv))
        b_low = mixed_state[0].astype(BF16)
        b_turned = mixed_state[0].T.astype(BF16)
        c_low = mixed_state[1].astype(BF16)
        steps, _, local, local_t, into, out, bias = decay_terms(
            step_out[rows], step_bias, rate, cols, seg_row
        )
        keep = into[BLOCK - 1 :]
        scores = matmul(c_low, b_low, (1, 1))
        square = jnp.zeros((BLOCK, LANES), F32)
        for pair in range(channels // LANES):
            lanes = slice(pair * LANES, (pair + 1) * LANES)
            raw, pv = conv(vbuf, row, lanes, cols, KERNEL_ROW, BIAS_ROW)
            vraw_out[rows, lanes] = raw.astype(BF16)
            pv_out[rows, lanes] = pv
            values = pv * sigmoid(pv)
            old = state[:, lanes]
            old_low = old.astype(BF16)
            saved_out[sub, :, lanes] = old_low
            u = values * pairwise(steps, pair, half)
            weights = [
                (scores * decay_of(local, local_t, bias, 2 * pair + k)).astype(BF16)
                for k in range(2)
            ]
            inner = matmul(jnp.concatenate(weights, axis=1), split_pair(u.astype(BF16), half))
            y_ssm = inner + matmul(c_low, old_low) * pairwise(into, pair, half)
            y_out[rows, lanes] = y_ssm
            leaving = (u * pairwise(out, pair, half)).astype(BF16)
            state[:, lanes] = old * pairwise(keep, pair, half_row) + matmul(b_turned, leaving)
            gate = gate_out[rows, lanes]
            gated = (y_ssm + pairwise(skips, pair, half_row) * values) * (gate * sigmoid(gate))
            square = square + gated * gated
            scaled[rows, lanes] = (gated * par[GATED_ROW : GATED_ROW + 1, lanes]).astype(BF16)
        squares.append(jnp.sum(square, axis=-1, keepdims=True))
    vbuf[:8] = vbuf[size:]
    sbuf[:8] = sbuf[size:]
    tail_out[...] = vbuf[:8]
    state_tail_out[...] = sbuf[:8]
    partial[...] = matmul(scaled[...], out_w[...])
    steps_each = pl.num_programs(0) // chunks
    for index, partial_out in enumerate(partial_outs):

        @pl.when(pl.program_id(0) // steps_each == index)
        def _(partial_out=partial_out):
            partial_out[...] = partial[...]

    products = [
        jnp.sum(cot[row : row + ROWS].astype(F32) * partial[row : row + ROWS], axis=-1, keepdims=True)
        for row in range(0, size, ROWS)
    ]
    per = BLOCK // ROWS
    for sub in range(size // BLOCK):
        product = jnp.concatenate(products[sub * per : (sub + 1) * per], axis=0)
        scale = jnp.concatenate(scales[sub * per : (sub + 1) * per], axis=0)
        table = jnp.where(
            lane == 0, squares[sub], jnp.where(lane == 1, product, jnp.where(lane == 2, scale, 0.0))
        )
        stats_out[:, sub * BLOCK : (sub + 1) * BLOCK] = table.T[:8]


def backward_kernel(first_piece, unused, block_base, blocks, *refs):
    (
        place_ref,
        og_ref,
        gate_ref,
        vraw_ref,
        pv_ref,
        y_ref,
        sraw_ref,
        spv_ref,
        step_ref,
        own_stats,
        stats_1,
        stats_2,
        stats_3,
        saved_ref,
        seg,
        par,
    ) = refs[:16]
    refs = refs[16:]
    if not first_piece:
        carried_in = refs[:6]
        refs = refs[6:]
    refs = refs[unused:]
    (
        low_out,
        mixed_out,
        state_out,
        tail_out,
        state_tail_out,
        wide_acc,
        narrow_acc,
        heads_acc,
    ) = refs
    channels = gate_ref.shape[1]
    place = place_ref[0]

    @pl.when(pl.program_id(0) == 0)
    def _():
        outs = (state_out, tail_out, state_tail_out, wide_acc, narrow_acc, heads_acc)
        for k, ref in enumerate(outs):
            ref[...] = jnp.zeros_like(ref) if first_piece else carried_in[k][...]

    block = block_base + pl.num_programs(0) - 1 - pl.program_id(0)
    cols, seg_row = segment_columns(seg, block, blocks, True)
    stats = sum_over_places(place, own_stats[...], [stats_1[...], stats_2[...], stats_3[...]])
    stats = upright(stats)
    strength = lax.rsqrt(stats[:, 0:1] / INNER + EPS)
    pull = strength * strength * strength * stats[:, 1:2] / INNER

    half = lax.broadcasted_iota(jnp.int32, (BLOCK, LANES), 1) < LANES // 2
    half_row = half[0:1]
    spv = [spv_ref[:, :LANES], spv_ref[:, LANES:]]
    spv_sig = [sigmoid(v) for v in spv]
    b_part = spv[0] * spv_sig[0]
    c_part = spv[1] * spv_sig[1]
    b_low = b_part.astype(BF16)
    c_low = c_part.astype(BF16)
    c_turned = c_part.T.astype(BF16)
    step_raw = step_ref[...]
    step_bias = par[STEP_ROW : STEP_ROW + 1, :LANES]
    rate = jnp.exp(par[DECAY_ROW : DECAY_ROW + 1, :LANES])
    skips = par[SKIP_ROW : SKIP_ROW + 1, :LANES]
    steps, rates, local, local_t, into, out, bias = decay_terms(
        step_raw, step_bias, rate, cols, seg_row
    )
    keep = into[BLOCK - 1 :]
    scores = matmul(c_low, b_low, (1, 1))

    def conv_back(pre_grad, raw, lanes, after, kernel_row, acc):
        ext = jnp.concatenate([pre_grad, after[:, lanes]], axis=0)
        after[:, lanes] = pre_grad[:8]
        total = pre_grad * par[kernel_row + 3 : kernel_row + 4, lanes]
        acc[24:32, lanes] += fold(raw * pre_grad)
        acc[32:40, lanes] += fold(pre_grad)
        for ahead in range(1, 4):
            moved = pltpu.roll(ext, BLOCK + 8 - ahead, 0)[:BLOCK]
            term = moved * cols[:, ahead : ahead + 1]
            total = total + term * par[kernel_row + 3 - ahead : kernel_row + 4 - ahead, lanes]
            acc[8 * (3 - ahead) : 8 * (4 - ahead), lanes] += fold(raw * term)
        return total

    score_grad = jnp.zeros((BLOCK, BLOCK), F32)
    b_grad = jnp.zeros((BLOCK, LANES), F32)
    c_grad = jnp.zeros((BLOCK, LANES), F32)
    spread_dl = jnp.zeros((BLOCK, LANES), F32)
    spread_ds = jnp.zeros((BLOCK, LANES), F32)
    spread_end = jnp.zeros((8, LANES), F32)
    for pair in range(channels // LANES):
        lanes = slice(pair * LANES, (pair + 1) * LANES)
        spread = (
            lax.broadcasted_iota(jnp.int32, (LANES, LANES), 0) // (LANES // 2) + 2 * pair
            == lax.broadcasted_iota(jnp.int32, (LANES, LANES), 1)
        ).astype(BF16)
        gain = par[GATED_ROW : GATED_ROW + 1, lanes]
        skip = pairwise(skips, pair, half_row)
        gate = gate_ref[:, lanes]
        gate_sig = sigmoid(gate)
        gate_silu = gate * gate_sig
        pv = pv_ref[:, lanes]
        pv_sig = sigmoid(pv)
        values = pv * pv_sig
        og = og_ref[:, lanes]
        y_ssm = y_ref[:, lanes]
        y = y_ssm + skip * values
        gated = y * gate_silu
        strong = gated * strength
        mixed_out[:, lanes] = (strong * gain).astype(BF16)
        gated_grad = gain * strength * og - gated * pull
        low_out[:, lanes] = (
            gated_grad * y * (gate_sig * (1.0 + gate * (1.0 - gate_sig)))
        ).astype(BF16)
        grad = gated_grad * gate_silu
        wide_acc[40:48, lanes] += fold(og * strong)
        wide_acc[48:56, lanes] += fold(grad * values)

        state_grad = state_out[:, lanes]
        state_grad_low = state_grad.astype(BF16)
        old_low = saved_ref[0, :, lanes]
        pair_steps = pairwise(steps, pair, half)
        pair_out = pairwise(out, pair, half)
        u = values * pair_steps
        u_low = u.astype(BF16)
        g_low = grad.astype(BF16)
        g_split = split_pair(g_low, half)
        decays = [decay_of(local, local_t, bias, 2 * pair + k) for k in range(2)]
        weights = jnp.concatenate([(scores * d).astype(BF16) for d in decays], axis=0)
        weight_grad = matmul(g_split, u_low, (1, 1))
        score_grad = score_grad + weight_grad[:BLOCK] * decays[0] + weight_grad[BLOCK:] * decays[1]
        u_grad_out = matmul(b_low, state_grad_low) * pair_out
        u_grad = matmul(weights, g_split, (0, 0)) + u_grad_out
        u_near = u_low.astype(F32)
        spread_dl = spread_dl + group_sum(g_low.astype(F32) * y_ssm - u_near * u_grad, spread)
        spread_ds = spread_ds + group_sum(values * u_grad, spread)
        keep_row = pairwise(keep, pair, half_row)
        spread_end = spread_end + group_sum(
            fold(u_near * u_grad_out) + fold(state_grad * old_low.astype(F32)) * keep_row, spread
        )
        entering = (grad * pairwise(into, pair, half)).astype(BF16)
        leaving = (u * pair_out).astype(BF16)
        c_grad = c_grad + matmul(entering, old_low, (1, 1))
        b_grad = b_grad + matmul(leaving, state_grad_low, (1, 1))
        state_out[:, lanes] = state_grad * keep_row + matmul(c_turned, entering)
        pre_grad = (pair_steps * u_grad + skip * grad) * (pv_sig * (1.0 + pv * (1.0 - pv_sig)))
        raw_grad = conv_back(
            pre_grad, vraw_ref[:, lanes].astype(F32), lanes, tail_out, KERNEL_ROW, wide_acc
        )
        low_out[:, channels + pair * LANES : channels + (pair + 1) * LANES] = raw_grad.astype(BF16)
    score_low = score_grad.astype(BF16)
    c_grad = c_grad + matmul(score_low, b_low)
    b_grad = b_grad + matmul(score_low, c_low, (0, 0))
    rate_grad = exact(triangle(False), spread_dl) + jnp.sum(spread_end, axis=0, keepdims=True)
    step_grad = (spread_ds - rate * rate_grad) * sigmoid(step_raw + step_bias)
    heads_acc[0:8] += fold(step_grad)
    heads_acc[8:16] += fold(rates * rate_grad)
    for part, grad in enumerate((b_grad, c_grad)):
        lanes = slice(part * LANES, (part + 1) * LANES)
        pre_grad = grad * (spv_sig[part] * (1.0 + spv[part] * (1.0 - spv_sig[part])))
        raw_grad = conv_back(
            pre_grad, sraw_ref[:, lanes].astype(F32), lanes, state_tail_out, STATE_KERNEL_ROW, narrow_acc
        )
        at = 2 * channels + part * LANES
        low_out[:, at : at + LANES] = raw_grad.astype(BF16)
    heads_here = channels // (LANES // 2)
    low_out[:, 2 * channels + 2 * LANES :] = pltpu.roll(step_grad, place * heads_here, 1).astype(BF16)


def out_grad_kernel(unused, cot, out_w, *refs):
    og, token = refs[unused : unused + 2]
    og[...] = matmul(cot[...], out_w[...], (1, 1))
    token[...] = jnp.zeros((8, LANES), F32)


def run_out_grad(chain, cot, out_w, passes):
    length, channels = cot.shape[0], out_w.shape[0]
    deps = chain.deps()
    results = pl.pallas_call(
        functools.partial(out_grad_kernel, len(deps) + len(passes)),
        grid=(length // CHUNK,),
        in_specs=[pl.BlockSpec((CHUNK, D), lambda i: (i, 0)), whole(out_w.shape)]
        + [ANYWHERE for _ in deps + passes],
        out_specs=[pl.BlockSpec((CHUNK, channels), lambda i: (i, 0)), whole((8, LANES))]
        + [ANYWHERE for _ in passes],
        out_shape=[
            jax.ShapeDtypeStruct((length, channels), F32),
            jax.ShapeDtypeStruct((8, LANES), F32),
        ]
        + [jax.ShapeDtypeStruct(p.shape, p.dtype) for p in passes],
        input_output_aliases={2 + len(deps) + k: 2 + k for k in range(len(passes))},
        compiler_params=pltpu.CompilerParams(vmem_limit_bytes=VMEM_LIMIT),
        cost_estimate=SMALL_COST,
        name="out_grad",
    )(cot, out_w, *deps, *passes)
    chain.last = results[1]
    return results[0], results[2:]


def run_matmul(chain, body, ins, outs, count, scratch=(), name=None):
    deps = chain.deps()
    arrays = [a for a, _, _ in ins]

    def kernel(*refs):
        body(*refs[: len(arrays)], *refs[len(arrays) + len(deps) :])
        refs[len(arrays) + len(deps) + len(outs)][...] = jnp.zeros((8, LANES), F32)

    results = pl.pallas_call(
        kernel,
        grid=(count,),
        in_specs=[whole(a.shape) if m is None else pl.BlockSpec(b, m) for a, b, m in ins]
        + [ANYWHERE for _ in deps],
        out_specs=[pl.BlockSpec(b, m) for _, b, m in outs] + [whole((8, LANES))],
        out_shape=[jax.ShapeDtypeStruct(s, F32) for s, _, _ in outs]
        + [jax.ShapeDtypeStruct((8, LANES), F32)],
        scratch_shapes=list(scratch),
        compiler_params=pltpu.CompilerParams(vmem_limit_bytes=VMEM_LIMIT),
        cost_estimate=SMALL_COST,
        name=name,
    )(*arrays, *deps)
    chain.last = results[-1]
    return results[:-1]


def gain_row(value, count):
    out = []
    for k in range(count // BLOCK):
        column = jnp.sum(value[k * BLOCK : (k + 1) * BLOCK], axis=-1, keepdims=True)
        out.append(jnp.broadcast_to(column, (BLOCK, BLOCK)).T[:8])
    return jnp.concatenate(out, axis=1)


def run_rest_grad(chain, normed, low, small_rows, weights):
    width = small_rows.shape[1]
    count = D // CHUNK
    states = weights[0].shape[1]

    def body(left, right, extra, state_w, step_w, out, gain, token):
        @pl.when(pl.program_id(0) < count)
        def _():
            value = matmul(left[...], right[...], (0, 0))
            out[...] = value
            both = jnp.concatenate([state_w[...], step_w[...]], axis=1).astype(F32)
            gain[...] = gain_row(value * both, CHUNK)

        @pl.when(pl.program_id(0) == count)
        def _():
            out[...] = extra[...]

    length, total = low.shape
    held = lambda i: jnp.minimum(i, count - 1)
    tile = lambda a: (a, (CHUNK, a.shape[1]), lambda i: (held(i), 0))
    return run_matmul(
        chain,
        body,
        [
            (normed, (length, CHUNK), lambda i: (0, held(i))),
            (low, (length, width), lambda i: (0, total // width - 1)),
            (small_rows, None, None),
            *[tile(w) for w in weights],
        ],
        [
            ((D + CHUNK, width), (CHUNK, width), lambda i: (i, 0)),
            ((8, D), (8, CHUNK), lambda i: (0, held(i))),
        ],
        count + 1,
        name="rest_grad",
    )


def run_weight_grads(chain, core, normed, low, cot, mixed, weights, gains, unit):
    length = normed.shape[0]
    channels = mixed.shape[1]
    tile = D // 4
    deps = chain.deps()

    def which(i, p):
        return jnp.where(i < 2, 1 - p[0], p[0]) * 2 + i % 2

    def kernel(place, left, right, cots, mix, gate_w, value_w, gain_in, *refs):
        outs, gain, token = refs[len(deps) : len(deps) + 4], refs[-2], refs[-1]
        i = pl.program_id(0)

        @pl.when(i == 0)
        def _():
            gain[...] = gain_in[...]
            token[...] = jnp.zeros((8, LANES), F32)

        gate = matmul(left[...], right[:, :channels], (0, 0))
        value = matmul(left[...], right[:, channels:], (0, 0))
        out = matmul(cots[...], mix[...], (0, 0))
        at = pl.ds(pl.multiple_of(which(i, place) * tile, LANES), tile)
        products = gate * gate_w[...].astype(F32) + value * value_w[...].astype(F32)
        gain[:, at] = gain[:, at] + gain_row(products, tile)
        for k in range(4):

            @pl.when(i == k)
            def _(k=k):
                for n in range(tile // unit):
                    rows = slice(n * unit, (n + 1) * unit)
                    for m, part in enumerate((gate, value, out)):
                        first = (3 * n + m) * unit
                        outs[k][first : first + unit, :] = part[rows]

    lanes = lambda i, p: (0, which(i, p))
    weight_spec = pl.BlockSpec((tile, channels), lambda i, p: (which(i, p), 0))
    results = pl.pallas_call(
        kernel,
        grid_spec=pltpu.PrefetchScalarGridSpec(
            num_scalar_prefetch=1,
            grid=(4,),
            in_specs=[
                pl.BlockSpec((length, tile), lanes),
                pl.BlockSpec((length, 2 * channels), lambda i, p: (0, 0)),
                pl.BlockSpec((length, tile), lanes),
                whole(mixed.shape),
                weight_spec,
                weight_spec,
                whole(gains.shape),
            ]
            + [ANYWHERE for _ in deps],
            out_specs=[whole((3 * tile, channels))] * 4 + [whole(gains.shape), whole((8, LANES))],
        ),
        out_shape=[jax.ShapeDtypeStruct((3 * tile, channels), F32)] * 4
        + [jax.ShapeDtypeStruct(gains.shape, F32), jax.ShapeDtypeStruct((8, LANES), F32)],
        compiler_params=pltpu.CompilerParams(vmem_limit_bytes=VMEM_LIMIT),
        cost_estimate=SMALL_COST,
        name="weight_grads",
    )(core, normed, low, cot, mixed, *weights, gains, *deps)
    chain.last = results[-1]
    return results[:4], results[4]


def run_assemble(chain, core, own, got, unit):
    rows, channels = own[0].shape
    tile = rows // 3
    deps = chain.deps()

    def kernel(place, own_a, own_b, got_a, got_b, *refs):
        gate, value, out, token = refs[len(deps) :]
        i = pl.program_id(0)
        token[...] = jnp.zeros((8, LANES), F32)
        for n, (mine, other) in enumerate(((own_a, got_a), (own_b, got_b))):

            @pl.when(i % 2 == n)
            def _(mine=mine, other=other):
                use_own = i // 2 == place[0]
                pieces = []
                for k in range(rows // unit):
                    at = slice(k * unit, (k + 1) * unit)
                    pieces.append(jnp.where(use_own, mine[at, :], other[at, :]))
                gate[...] = jnp.concatenate(pieces[0::3], axis=0)
                value[...] = jnp.concatenate(pieces[1::3], axis=0)
                out[...] = jnp.concatenate(pieces[2::3], axis=0).T

    row = pl.BlockSpec((tile, channels), lambda i, p: (i, 0))
    gate, value, out, chain.last = pl.pallas_call(
        kernel,
        grid_spec=pltpu.PrefetchScalarGridSpec(
            num_scalar_prefetch=1,
            grid=(4,),
            in_specs=[whole(own[0].shape)] * 4 + [ANYWHERE for _ in deps],
            out_specs=[
                row,
                row,
                pl.BlockSpec((channels, tile), lambda i, p: (0, i)),
                whole((8, LANES)),
            ],
        ),
        out_shape=[
            jax.ShapeDtypeStruct((D, channels), F32),
            jax.ShapeDtypeStruct((D, channels), F32),
            jax.ShapeDtypeStruct((channels, D), F32),
            jax.ShapeDtypeStruct((8, LANES), F32),
        ],
        compiler_params=pltpu.CompilerParams(vmem_limit_bytes=VMEM_LIMIT),
        cost_estimate=SMALL_COST,
        name="assemble",
    )(core, *own, *got, *deps)
    return gate, value, out


def run_total(chain, low, weights):
    length, width = low.shape

    def body(left, gate_w, value_w, state_w, step_w, out, token, joined):
        @pl.when(pl.program_id(0) == 0)
        def _():
            at = 0
            for ref in (gate_w, value_w, state_w, step_w):
                joined[:, at : at + ref.shape[1]] = ref[...]
                at += ref.shape[1]

        out[...] = matmul(left[...], joined[...], (1, 1))

    (out,) = run_matmul(
        chain,
        body,
        [(low, (CHUNK, width), lambda i: (i, 0))] + [(w, None, None) for w in weights],
        [((length, D), (CHUNK, D), lambda i: (i, 0))],
        length // CHUNK,
        scratch=[pltpu.VMEM((D, width), BF16)],
        name="normed_grad",
    )
    return out


def whole(shape):
    return pl.BlockSpec(shape, lambda i, *_: (0,) * len(shape))


ANYWHERE = pl.BlockSpec(memory_space=pl.ANY)


def run_forward(start, count, chunks, tokens, cot, seg, small, carried, kept, deps):
    channels = small["gate_w"].shape[1]
    states = 2 * LANES
    size = CHUNK
    length = count * size
    first = start // size
    per = size // BLOCK
    full = tokens.shape[0]

    def row_in(width):
        return pl.BlockSpec((size, width), lambda i: (first + i, 0))

    def row_out(width):
        return pl.BlockSpec((size, width), lambda i: (i, 0))

    def chunk_out(index):
        each = count // chunks
        return pl.BlockSpec((size, D), lambda i: (jnp.clip(i - index * each, 0, each - 1), 0))

    constant = [small[n] for n in ("par", "gate_w", "value_w", "state_w", "step_w", "out_w")]
    carry_shapes = [(LANES, channels), (8, channels), (8, states)]
    widths = (
        (channels, F32),
        (channels, BF16),
        (channels, F32),
        (channels, F32),
        (states, BF16),
        (states, F32),
        (LANES, F32),
    )
    inputs = [tokens, cot, seg, *constant, *carried, *deps, *kept]
    outs = pl.pallas_call(
        functools.partial(
            forward_kernel, not carried, len(deps) + len(kept), start // BLOCK, chunks
        ),
        grid=(count,),
        in_specs=[row_in(D), row_in(D), whole(seg.shape)]
        + [whole(c.shape) for c in constant]
        + [whole(c.shape) for c in carried]
        + [ANYWHERE for _ in deps + kept],
        out_specs=[row_out(w) for w, _ in widths]
        + [pl.BlockSpec((per, LANES, channels), lambda i: (i, 0, 0))]
        + [pl.BlockSpec((8, size), lambda i: (0, first + i))]
        + [row_in(D)]
        + [whole(c) for c in carry_shapes]
        + [chunk_out(index) for index in range(chunks)],
        out_shape=[jax.ShapeDtypeStruct((length, w), k) for w, k in widths]
        + [jax.ShapeDtypeStruct((length // BLOCK, LANES, channels), BF16)]
        + [jax.ShapeDtypeStruct((8, full), F32)]
        + [jax.ShapeDtypeStruct((full, D), BF16)]
        + [jax.ShapeDtypeStruct(c, F32) for c in carry_shapes]
        + [jax.ShapeDtypeStruct((length // chunks, D), F32)] * chunks,
        scratch_shapes=[
            pltpu.VMEM((size + 8, channels), F32),
            pltpu.VMEM((size + 8, states), F32),
            pltpu.VMEM((size, channels), BF16),
            pltpu.VMEM((size, D), F32),
        ],
        input_output_aliases={len(inputs) - len(kept) + k: 8 + k for k in range(len(kept))},
        compiler_params=pltpu.CompilerParams(vmem_limit_bytes=VMEM_LIMIT),
        cost_estimate=SMALL_COST,
        name="forward_piece",
    )(*inputs)
    outs = list(outs)
    names = ("gate", "vraw", "pv", "y", "sraw", "spv", "step", "saved")
    return dict(zip(names, outs[:8])), outs[8:10], outs[10:13], outs[13:]


def run_backward(start, piece, og, stats, place, seg, small, carried, low, mixed, deps):
    channels = small["gate_w"].shape[1]
    length = piece["gate"].shape[0]
    full = og.shape[0]
    count = length // BLOCK
    first = start // BLOCK
    flip = lambda i: count - 1 - i

    def row(width):
        return pl.BlockSpec((BLOCK, width), lambda i, *_: (flip(i), 0))

    def shared(width):
        return pl.BlockSpec((BLOCK, width), lambda i, *_: (first + flip(i), 0))

    names = ("gate", "vraw", "pv", "y", "sraw", "spv", "step")
    ins = [piece[n] for n in names]
    low_width = 2 * channels + 3 * LANES
    kept = [] if low is None else [low, mixed]
    carry_shapes = [
        (LANES, channels),
        (8, channels),
        (8, 2 * LANES),
        (56, channels),
        (40, 2 * LANES),
        (16, LANES),
    ]
    inputs = [og, *ins, *stats, piece["saved"], seg, small["par"], *carried, *deps, *kept]
    outs = pl.pallas_call(
        functools.partial(
            backward_kernel, not carried, len(deps) + len(kept), first, full // BLOCK
        ),
        grid_spec=pltpu.PrefetchScalarGridSpec(
            num_scalar_prefetch=1,
            grid=(count,),
            in_specs=[shared(channels)]
            + [row(a.shape[1]) for a in ins]
            + [pl.BlockSpec((8, BLOCK), lambda i, *_: (0, first + flip(i))) for _ in stats]
            + [pl.BlockSpec((1, LANES, channels), lambda i, *_: (flip(i), 0, 0))]
            + [whole(seg.shape), whole(small["par"].shape)]
            + [whole(c.shape) for c in carried]
            + [ANYWHERE for _ in deps + kept],
            out_specs=[shared(low_width), shared(channels)] + [whole(c) for c in carry_shapes],
        ),
        out_shape=[
            jax.ShapeDtypeStruct((full, low_width), BF16),
            jax.ShapeDtypeStruct((full, channels), BF16),
        ]
        + [jax.ShapeDtypeStruct(c, F32) for c in carry_shapes],
        compiler_params=pltpu.CompilerParams(vmem_limit_bytes=VMEM_LIMIT),
        cost_estimate=SMALL_COST,
        input_output_aliases={1 + len(inputs) - 2 + k: k for k in range(len(kept))},
        name="backward_piece",
    )(place, *inputs)
    return outs[0], outs[1], list(outs[2:])


class Chain:
    def __init__(self):
        self.last = None
        self.more = []

    def deps(self):
        found = ([] if self.last is None else [self.last]) + self.more
        self.more = []
        return found


def rowwise(
    chain, place, body, ins, outs, rows, passes=(), step=0, whole_place=False, name=None
):
    step = step or STEP
    steps = rows // step

    def spec(width, first, most=steps, where=None):
        if where is not None:
            base = first if callable(first) else lambda p: first
            return pl.BlockSpec(
                (step, width),
                lambda i, p: (
                    jnp.where(where(p[0]), base(p[0]) + jnp.minimum(i, most - 1), 0),
                    0,
                ),
            )
        if callable(first):
            return pl.BlockSpec(
                (step, width),
                lambda i, p: (
                    jnp.maximum(first(p if whole_place else p[0]) + jnp.minimum(i, most - 1), 0),
                    0,
                ),
            )
        return pl.BlockSpec((step, width), lambda i, p: (first + jnp.minimum(i, most - 1), 0))

    def lying(height, first):
        if callable(first):
            return pl.BlockSpec((height, STEP), lambda i, p: (0, first(p[0]) + i))
        return pl.BlockSpec((height, STEP), lambda i, p: (0, first + i))

    def spec_of(array, first, across=False, most=steps, where=None):
        if first is None:
            return fixed(array.shape)
        return lying(array.shape[0], first) if across else spec(array.shape[1], first, most, where)

    def fixed(shape):
        return pl.BlockSpec(shape, lambda i, p: (0,) * len(shape))

    anywhere = pl.BlockSpec(memory_space=pl.ANY)
    arrays = [entry[0] for entry in ins]
    in_specs = [spec_of(*entry) for entry in ins]
    kept = [(k, o[4]) for k, o in enumerate(outs) if o[4] is not None]
    deps = chain.deps()
    inputs = [*arrays, *[a for _, a in kept], *passes, *deps]
    aliases = {1 + len(arrays) + n: k for n, (k, _) in enumerate(kept)}
    for n in range(len(passes)):
        aliases[1 + len(arrays) + len(kept) + n] = len(outs) + n

    def kernel(place_ref, *refs):
        results = refs[len(inputs) :]
        values = body(place_ref if whole_place else place_ref[0], *refs[: len(arrays)])
        for ref, value in zip(results[: len(outs)], values):
            ref[...] = value
        results[-1][...] = jnp.zeros((8, LANES), F32)

    results = pl.pallas_call(
        kernel,
        grid_spec=pltpu.PrefetchScalarGridSpec(
            num_scalar_prefetch=1,
            grid=(steps,),
            in_specs=in_specs + [anywhere] * (len(inputs) - len(arrays)),
            out_specs=[spec(o[1], o[3], *o[5:]) for o in outs]
            + [anywhere] * len(passes)
            + [fixed((8, LANES))],
        ),
        out_shape=[jax.ShapeDtypeStruct((o[0], o[1]), o[2]) for o in outs]
        + [jax.ShapeDtypeStruct(p.shape, p.dtype) for p in passes]
        + [jax.ShapeDtypeStruct((8, LANES), F32)],
        input_output_aliases=aliases,
        compiler_params=pltpu.CompilerParams(vmem_limit_bytes=VMEM_LIMIT),
        cost_estimate=SMALL_COST,
        name=name,
    )(place, *inputs)
    chain.last = results[-1]
    return list(results[:-1])


def after(chain, *arrays):
    def kernel(*refs):
        refs[-1][...] = jnp.zeros((8, LANES), F32)

    anywhere = pl.BlockSpec(memory_space=pl.ANY)
    deps = chain.deps()
    results = pl.pallas_call(
        kernel,
        in_specs=[anywhere] * (len(arrays) + len(deps)),
        out_specs=[anywhere] * len(arrays) + [pl.BlockSpec(memory_space=pltpu.VMEM)],
        out_shape=[jax.ShapeDtypeStruct(a.shape, a.dtype) for a in arrays]
        + [jax.ShapeDtypeStruct((8, LANES), F32)],
        input_output_aliases={k: k for k in range(len(arrays))},
        cost_estimate=SMALL_COST,
        name="in_order",
    )(*arrays, *deps)
    chain.last = results[-1]
    return list(results[:-1])


INWARD = ((0, 1), (3, 2))
ACROSS = ((1, 2), (2, 1))
OUTWARD = ((1, 0), (2, 3))


def on_device(
    tokens,
    norm_gain,
    gate_weight,
    value_weight,
    state_weight,
    step_weight,
    value_kernel,
    value_bias,
    state_kernel,
    state_bias,
    step_bias,
    decay_log,
    skip_scale,
    gated_gain,
    out_weight,
    segment_ids,
    out_cotangent,
):
    parts = lax.axis_size("tensor")
    place = lax.axis_index("tensor")
    middle = jnp.logical_and(place > 0, place < parts - 1)
    length = tokens.shape[0]
    channels = gate_weight.shape[1]
    head_count = step_bias.shape[0]
    rows = length // parts
    states = 2 * LANES
    where = place.astype(jnp.int32)[None]
    par, step_wide, step_place = run_pack(
        where,
        norm_gain,
        value_kernel,
        value_bias,
        gated_gain,
        skip_scale,
        state_kernel,
        state_bias,
        step_bias,
        decay_log,
        step_weight.T,
    )
    small = {
        "gate_w": gate_weight,
        "value_w": value_weight,
        "state_w": state_weight,
        "step_w": step_wide,
        "out_w": out_weight,
        "par": par,
    }
    chain = Chain()
    send = lambda x, pairs: lax.ppermute(x, "tensor", pairs)
    run = functools.partial(rowwise, chain, where)
    steps = lambda n: n // STEP

    piece_spans = [p * length // sum(PIECES) for p in PIECES]
    piece_firsts = [sum(piece_spans[:k]) for k in range(len(piece_spans))]
    pieces = []
    partials = []
    spans = [length // sum(PIECES)] * sum(PIECES)
    firsts = [sum(spans[:k]) for k in range(len(spans))]
    carried = []
    kept = []
    late = {}
    count = len(spans)
    outer, inner, outer_sent, pair_sum = {}, {}, {}, {}

    def forward():
        nonlocal carried, kept
        k = len(pieces)
        outs, kept, carried, made = run_forward(
            piece_firsts[k],
            piece_spans[k] // CHUNK,
            PIECES[k],
            tokens,
            out_cotangent,
            segment_ids,
            small,
            carried,
            kept,
            chain.deps(),
        )
        partials.extend(made)
        pieces.append(outs)
        chain.last = carried[2]


    def send_outer(n, message, both=True):
        outer_sent[n] = message
        outer[n] = send(message, INWARD + OUTWARD if both else INWARD)

    is_middle = lambda p: jnp.logical_and(p > 0, p < parts - 1)
    per = steps(rows)
    at_ends = lambda low_end, high_end: lambda p: jnp.where(p < 2, low_end, high_end) * per

    def event(n, following=None, middle_segment=None):
        chunk = n < count
        step = STEP
        blocks = spans[0] // step
        size = spans[0]
        is_end = lambda p: jnp.logical_not(is_middle(p))
        if chunk:
            mine = (partials[n], 0, False, blocks, is_middle)
        else:
            mine = (late["total"], middle_segment, False, blocks, is_middle)
        ins = [mine, (outer[n], 0, False, blocks, is_middle)]
        outs = [(size, D, F32, 0, None, blocks, is_middle)]
        if n > 0:
            array, first = following
            from_middle = (inner[n], 0, False, blocks, is_middle)
            if n <= count:
                ins += [(pair_sum[n - 1], 0, False, blocks, is_middle), from_middle]
                ins += [(array, first, False, blocks, is_end)]
            else:
                ins += [(array, first, False, blocks), from_middle]
            outs.append((spans[0], D, F32, 0, None, blocks))

        def body(p, a, b, *others):
            value = a[...] + b[...]
            results = [value]
            if n > 0:
                message = others[0][...] + others[1][...]
                if n <= count:
                    message = jnp.where(is_middle(p), message, others[2][...])
                results.append(message)
            return results

        results = run(body, ins, outs, size, step=step, name="event")
        if n == 0:
            chain.more = late["stats"][1:]
            results = after(chain, *results)
        pair_sum[n] = results[0]
        inner[n + 1] = send(results[0], ACROSS)
        if n > 0:
            send_outer(n + 1, results[1])
        else:
            send_outer(1, following[0], False)

    def finish_chunk(k):
        def body(p, own, got, token, *stats):
            inside = jnp.logical_and(p > 0, p < parts - 1)
            total = jnp.where(inside, own[...], got[...])
            table = upright(sum_over_places(p, stats[0][...], [x[...] for x in stats[1:]]))
            strength = lax.rsqrt(table[:, 0:1] / INNER + EPS)
            return [(token[...].astype(F32) + total * strength).astype(BF16)]

        first = steps(firsts[k])
        (late["block_out"],) = run(
            body,
            [(outer_sent[k + 2], 0), (outer[k + 2], 0), (tokens, first)]
            + [(x, first, True) for x in late["stats"]],
            [(length, D, BF16, first, late.get("block_out"))],
            spans[k],
            name="finish_chunk",
        )

    def finish_grad(n):
        def body(p, mine, side_got, middle_got, token, scale, cot, gain):
            token = token[...].astype(F32)
            scale = upright(scale[...])[:, 2:3]
            weighted = (mine[...] + side_got[...] + middle_got[...]) * gain[...]
            pull = jnp.sum(weighted * token, axis=-1, keepdims=True) / D
            return [cot[...].astype(F32) + scale * weighted - token * scale * scale * scale * pull]

        mine = lambda p: p * per
        (late["tokens_grad"],) = run(
            body,
            [
                (late["total"], mine),
                (outer[n], 0),
                (inner[n], 0),
                (tokens, mine),
                (late["own_stats"], mine, True),
                (out_cotangent, mine),
                (norm_gain[None], None),
            ],
            [(rows, D, F32, 0, None)],
            rows,
            name="finish_grad",
        )

    low = mixed = None
    back = []

    def backward(k):
        nonlocal low, mixed, back
        low, mixed, back = run_backward(
            piece_firsts[k],
            pieces[k],
            late["og"],
            late["stats"],
            where,
            segment_ids,
            small,
            back,
            low,
            mixed,
            chain.deps(),
        )
        chain.last = back[2]

    def exchange_stats():
        own = late["own_stats"] = kept[0]
        late["stats"] = [own] + [
            send(own, [(k, (k + turn) % parts) for k in range(parts)]) for turn in range(1, parts)
        ]

    forward()
    send_outer(0, partials[0], False)
    late["og"], _ = run_out_grad(chain, out_cotangent, out_weight, [])
    forward()
    exchange_stats()
    event(0, (partials[1], 0))
    backward(1)
    backward(0)
    event(1, (partials[2], 0))

    normed = kept[1]
    wide_acc, narrow_acc, heads_acc = back[3:]
    back_weights = [gate_weight, value_weight, state_weight, step_place]
    width = 3 * LANES
    fit = lambda x: jnp.pad(x.reshape(-1), (0, -x.size % width)).reshape(-1, width)
    narrow = narrow_acc.reshape(5, 8, states).sum(axis=1)
    wide_sums = wide_acc.reshape(7, 8, channels).sum(axis=1)
    head_sums = heads_acc.reshape(2, 8, LANES).sum(axis=1)[:, :head_count]
    skip_grad = wide_sums[6].reshape(head_count, channels // head_count).sum(axis=1)
    mine = jnp.concatenate([fit(wide_sums[:6]), fit(jnp.concatenate([head_sums, skip_grad[None]]))])
    mine_rows = mine.shape[0]
    slots = jnp.where(
        lax.broadcasted_iota(jnp.int32, (parts, 1, 1), 0) == place, mine[None], 0.0
    ).reshape(-1, width)
    narrow_rows = fit(narrow)
    filler = jnp.zeros((CHUNK - narrow_rows.shape[0] - slots.shape[0], width), F32)
    shared, gains = run_rest_grad(
        chain, normed, low, jnp.concatenate([narrow_rows, slots, filler]), back_weights[2:]
    )

    ways = lax.axis_size("dp")
    own_dp = lax.axis_index("dp")
    bits = []
    while 2 ** len(bits) < ways:
        bits.append(2 ** len(bits))
    tile_rows = 8 * ways
    shared_rows = D + -(-(narrow_rows.shape[0] + slots.shape[0]) // tile_rows) * tile_rows
    swap = lambda x, bit: lax.ppermute(x, "dp", [(k, k ^ bit) for k in range(ways)])
    side = lambda n: (own_dp // bits[n]) % 2
    halving = {"keep": shared, "rows": shared_rows, "got": None}

    def halve(n):
        keep, size = halving["keep"], halving["rows"]
        if n > 0:
            add = lambda p, a, b: [a[...] + b[...]]
            size = size // 2
            (keep,) = rowwise(
                chain,
                side(n - 1).astype(jnp.int32)[None],
                add,
                [(keep, lambda p: p), (halving["got"], 0)],
                [(size, width, F32, 0, None)],
                size,
                step=size,
                name="halve",
            )
            halving["rows"] = size
        if n < len(bits):
            away = lax.dynamic_slice_in_dim(keep, (1 - side(n)) * (size // 2), size // 2, 0)
            halving["got"] = swap(away, bits[n])
        halving["keep"] = keep

    core = side(0).astype(jnp.int32)[None]
    core_bit, axes = bits[0], list(range(1, len(bits)))
    turned = axes[len(axes) // 2 :] + axes[: len(axes) // 2]
    orders = (axes, turned)
    sums = {}

    def reduce_step(step):
        sides = jnp.stack([side(orders[k][step]).astype(jnp.int32) for k in range(2)])
        ins, outs = [], []
        size = sums["keep"][0].shape[0] // 2
        unit = size if size < 512 else size // 2
        for k in range(2):
            for stay in (1, 0):
                at = functools.partial(
                    lambda p, k, stay: (p[k] if stay else 1 - p[k]) * (size // unit), k=k, stay=stay
                )
                ins += [(sums["keep"][k], at), (sums["got"][k], at)]
                outs.append((size, channels, F32, 0, None))
        results = rowwise(
            chain,
            sides,
            lambda p, *refs: [refs[2 * n][...] + refs[2 * n + 1][...] for n in range(4)],
            ins,
            outs,
            size,
            step=unit,
            whole_place=True,
            name="reduce_step",
        )
        sums["keep"] = [results[0], results[2]]
        sums["size"] = size
        sums["got"] = [swap(results[2 * k + 1], bits[orders[k][step]]) for k in range(2)]

    unit = D // 4 // 2 ** len(axes)

    def reduce_start():
        tiles, sums["gains"] = run_weight_grads(
            chain, core, normed, low, out_cotangent, mixed, back_weights[:2], gains, unit
        )
        sums["keep"] = tiles[2:]
        sums["got"] = [swap(x, core_bit) for x in tiles[:2]]

    def gather_first():
        sums["full"] = rowwise(
            chain,
            where,
            lambda p, a, b, c, d: [a[...] + b[...], c[...] + d[...]],
            [(x, 0) for k in range(2) for x in (sums["keep"][k], sums["got"][k])],
            [(sums["size"], channels, F32, 0, None)] * 2,
            sums["size"],
            step=sums["size"],
            name="gather_first",
        )
        step = len(axes) - 1
        sums["got"] = [swap(sums["full"][k], bits[orders[k][step]]) for k in range(2)]

    def gather_step(step):
        size = sums["size"]
        sides = jnp.stack([side(orders[k][step]).astype(jnp.int32) for k in range(2)])

        def body(p, *refs):
            upper = pl.program_id(0)
            picked = []
            for k in range(2):
                own, got = refs[2 * k][...], refs[2 * k + 1][...]
                picked.append(jnp.where(upper == p[k], own, got))
            return picked

        sums["full"] = rowwise(
            chain,
            sides,
            body,
            [(x, 0, False, 1) for k in range(2) for x in (sums["full"][k], sums["got"][k])],
            [(2 * size, channels, F32, 0, None)] * 2,
            2 * size,
            step=size,
            whole_place=True,
            name="gather_step",
        )
        sums["size"] = 2 * size
        if step > 0:
            sums["got"] = [swap(sums["full"][k], bits[orders[k][step - 1]]) for k in range(2)]

    def gather_core():
        sums["got"] = [swap(x, core_bit) for x in sums["full"]]

    halve(0)
    reduce_start()
    gain_rows = fit(sums["gains"][0] / norm_gain)
    gain_rows = jnp.pad(gain_rows, ((0, 8 - gain_rows.shape[0]), (0, 0)))
    halve(1)
    event(2, (partials[3], 0))

    halve(2)
    reduce_step(0)
    late["total"] = run_total(chain, low, back_weights)
    finish_chunk(0)
    event(3, (late["total"], at_ends(3, 0)))

    for step in range(1, len(axes)):
        reduce_step(step)
    gather_first()
    finish_chunk(1)
    for step in range(len(axes) - 1, 0, -1):
        gather_step(step)
    for n in range(3, len(bits) + 1):
        halve(n)
    share = jnp.concatenate([halving["keep"], gain_rows])
    share = lax.psum(share, "tensor")
    event(4, (late["total"], at_ends(2, 1)), at_ends(3, 0))

    gather_step(0)
    gather_core()
    finish_chunk(2)
    event(5, (late["total"], lambda p: jnp.where(p < 2, 1 - p, 5 - p) * per), at_ends(2, 1))

    (share,) = after(chain, share)
    share = lax.all_gather(share, "dp")
    finish_chunk(3)
    gate_weight_grad, value_weight_grad, out_weight_grad = run_assemble(
        chain, core, sums["full"], sums["got"], unit
    )

    places = np.array(
        [sum((k >> n & 1) << (len(bits) - 1 - n) for n in range(len(bits))) for k in range(ways)]
    )
    order = np.argsort(places)
    gain_sums = share[:, -8:].sum(axis=0)
    share = jnp.concatenate([share[k, :-8] for k in order] + [gain_sums])
    shared = share
    norm_gain_grad = shared[-8:].reshape(-1)[:D]
    rest, shared = shared[:D], shared[D:]
    state_weight_grad = rest[:, :states]
    step_weight_grad = lax.dynamic_slice(rest, (0, states + place * head_count), (D, head_count))
    at = narrow_rows.shape[0]
    narrow = shared[:at].reshape(-1)[: 5 * states].reshape(5, states)
    mine = lax.dynamic_slice_in_dim(shared, at + place * mine_rows, mine_rows, 0).reshape(-1)
    wide_sums = mine[: 6 * channels].reshape(6, channels)
    head_sums = mine[6 * channels :][: 3 * head_count].reshape(3, head_count)
    chain.more = [state_weight_grad, step_weight_grad, norm_gain_grad, narrow, wide_sums, head_sums]
    finish_grad(6)
    return (
        late["block_out"],
        late["tokens_grad"],
        norm_gain_grad,
        gate_weight_grad,
        value_weight_grad,
        state_weight_grad,
        step_weight_grad,
        wide_sums[:4],
        wide_sums[4],
        narrow[:4],
        narrow[4],
        head_sums[0],
        head_sums[1],
        head_sums[2],
        wide_sums[5],
        out_weight_grad,
    )


def solution(mesh):
    placed = (
        P("dp", None),
        P(),
        P(None, "tensor"),
        P(None, "tensor"),
        P(),
        P(None, "tensor"),
        P(None, "tensor"),
        P("tensor"),
        P(),
        P(),
        P("tensor"),
        P("tensor"),
        P("tensor"),
        P("tensor"),
        P("tensor", None),
        P("dp", None),
        P("dp", None),
    )
    return jax.shard_map(
        on_device,
        mesh=mesh,
        in_specs=placed,
        out_specs=(
            P("dp", None),
            P(("dp", "tensor"), None),
            P(),
            P(None, "tensor"),
            P(None, "tensor"),
            P(),
            P(None, "tensor"),
            P(None, "tensor"),
            P("tensor"),
            P(),
            P(),
            P("tensor"),
            P("tensor"),
            P("tensor"),
            P("tensor"),
            P("tensor", None),
        ),
        check_vma=False,
    )
```
